32 devices in a mesh: chan: 2 (over y), seqo: 4 (over z), seqi: 4 (over x, core).
Axes of the slice: x: 2, y: 2, z: 4, core: 2. Of those that a mesh axis runs over, the one named last changes fastest.
Arguments:
- gate_in: bfloat16 [32768, 4096], P(('seqo', 'seqi'), 'chan'), may hold values from -6 to 6
- value_in: bfloat16 [32768, 4096], P(('seqo', 'seqi'), 'chan'), may hold values from -6 to 6
- out_gate: bfloat16 [32768, 4096], P(('seqo', 'seqi'), 'chan'), may hold values from -6 to 6
- residual: bfloat16 [32768, 4096], P(('seqo', 'seqi'), 'chan'), may hold values from -200 to 200
- filters: bfloat16 [2, 16, 6, 32768], P('chan', ('seqo', 'seqi')), may hold values from -5 to 5
- kept_index: int32 [2, 64], P('chan'), may hold values from -1 to 2047, as said below
- kept_owner: int32 [2, 64], P('chan'), may hold values from -1 to 15, as said below
- skip_bias: float32 [4096], P('chan'), may hold values from -1 to 1
- norm_gain: float32 [4096], P('chan'), may hold values from 0.5 to 1.5
Outputs:
- hidden_out: bfloat16 [32768, 4096], P(('seqo', 'seqi'), 'chan')
- normed: bfloat16 [32768, 4096], P(('seqo', 'seqi'), 'chan')
The draws below stay inside these ranges and needn't reach their ends.
Inputs may be any that keep to these rules, and one draw needn't show every extreme that they name: `kept_index`: row s lists the kept channels of slab s in rising order, distinct, between 32 and 64 of them, followed by -1 in the unused slots; some slab lists exactly 64. `kept_owner`: -1 exactly where kept_index is -1, else a device index along seqo+seqi. Within a slab no device owns more than 6 kept channels, and in every slab some device owns exactly 6.
All inputs are finite; a program needn't handle non-finite values.
Results may differ from the reference program's by a relative error of at most 0.005.
Values may be sent and summed in bfloat16 or wider, within the bound.
No kernel may reach another device: no remote copies, remote signals or barrier semaphores. Data moves between devices by JAX's collectives and lax.ppermute only.
A program may use at most 128 MiB of HBM per device.

```python
import jax
import jax.numpy as jnp
from jax import lax

W = 4096
OWN_MAX = 6
SEQUENCE_LEN = 32768
SLAB = 2048
KMAX = 64
N_CHAN = 2
N_SEQO = 4
N_SEQI = 4


def kept_lists(key):
    owner_count = N_SEQO * N_SEQI
    random_key_list = jax.random.split(jax.random.fold_in(key, 7001), 3)
    counts = jax.random.randint(random_key_list[0], (N_CHAN,), KMAX // 2, KMAX + 1)
    full_slab = jax.random.randint(random_key_list[1], (), 0, N_CHAN)
    counts = jnp.where(jnp.arange(N_CHAN) == full_slab, KMAX, counts)
    slab_keys = jax.random.split(random_key_list[2], N_CHAN)

    def one_slab(packed):
        slab_key, count = packed
        pieces = jax.random.split(slab_key, 5)
        slot_pos = jnp.arange(KMAX, dtype=jnp.int32)
        is_live = slot_pos < count
        chosen = jax.random.permutation(pieces[0], SLAB)[:KMAX]
        sorted_index = jnp.sort(jnp.where(is_live, chosen, SLAB))
        index_row = jnp.where(is_live, sorted_index, -1)
        owner_step = jax.random.randint(pieces[1], (owner_count,), 1, 4)
        heavy_owner = jax.random.randint(pieces[2], (), 0, owner_count)
        pair_owner = jnp.repeat(jnp.arange(owner_count, dtype=jnp.int32), OWN_MAX)
        pair_slot = jnp.tile(jnp.arange(OWN_MAX, dtype=jnp.int32), owner_count)
        pair_level = pair_slot // owner_step[pair_owner]
        pair_level = jnp.where(pair_owner == heavy_owner, -1, pair_level)
        pair_noise = jax.random.permutation(pieces[3], owner_count * OWN_MAX)
        priority = (pair_level + 1) * (owner_count * OWN_MAX) + pair_noise
        pair_order = jnp.argsort(priority, stable=True)
        picked = pair_owner[pair_order[:KMAX]]
        shuffle_key = jnp.where(is_live, jax.random.permutation(pieces[4], KMAX), KMAX + slot_pos)
        live_rank = jnp.argsort(jnp.argsort(shuffle_key, stable=True), stable=True)
        owners_row = jnp.where(is_live, picked[live_rank], -1)
        return (index_row.astype(jnp.int32), owners_row.astype(jnp.int32))
    return lax.map(one_slab, (slab_keys, counts))


def draw_kept_index(key, part):
    return kept_lists(key)[0].astype(jnp.int32)


def draw_kept_owner(key, part):
    return kept_lists(key)[1].astype(jnp.int32)


def draw_filters(key, part):
    owner_count = N_SEQO * N_SEQI
    random_key_list = jax.random.split(jax.random.fold_in(key, 7002), 6)
    array_shape = (N_CHAN, owner_count, OWN_MAX)
    slow_share = 0.5
    is_slow = jax.random.uniform(random_key_list[0], array_shape) < slow_share
    fast_rate = jnp.exp(jax.random.uniform(random_key_list[1], array_shape, minval=jnp.log(1.0 / 50.0), maxval=jnp.log(1.0 / 30.0)))
    slow_rate = jnp.exp(jax.random.uniform(random_key_list[2], array_shape, minval=jnp.log(0.05 / SEQUENCE_LEN), maxval=jnp.log(0.8 / SEQUENCE_LEN)))
    decay_rate = jnp.where(is_slow, slow_rate, fast_rate)
    floor_level = jnp.where(is_slow, 0.0, jnp.sqrt(1.0 / (2.0 * fast_rate * SEQUENCE_LEN)))
    spike_location = jax.random.randint(random_key_list[3], array_shape + (2,), 0, SEQUENCE_LEN)
    spike_retained = jax.random.uniform(random_key_list[4], array_shape + (2,), minval=0.5, maxval=0.8)
    token_position = jnp.arange(SEQUENCE_LEN, dtype=jnp.float32)
    decay_envelope = jnp.exp(-decay_rate[..., None] * token_position) + floor_level[..., None]
    for spike_number in range(2):
        passed_through = token_position >= spike_location[..., spike_number:spike_number + 1].astype(jnp.float32)
        decay_envelope = decay_envelope * jnp.where(passed_through, spike_retained[..., spike_number:spike_number + 1], 1.0)
    tap_values = jax.random.truncated_normal(random_key_list[5], -5.0, 5.0, array_shape + (SEQUENCE_LEN,)) * decay_envelope
    tap_scale = jnp.sqrt(jnp.sum(decay_envelope * decay_envelope, axis=-1, keepdims=True))
    return (tap_values / tap_scale).astype(jnp.bfloat16)


def draw_residual(key, part):
    random_key_list = jax.random.split(jax.random.fold_in(key, 7003), 1)
    column = jnp.arange(W, dtype=jnp.float32)
    column_rise = 1.0 + column / W
    standard = jax.random.truncated_normal(random_key_list[0], -6.0, 6.0, (SEQUENCE_LEN, W))
    values = standard * column_rise[None, :]
    return jnp.clip(values, -200.0, 200.0).astype(jnp.bfloat16)


def level_of(key, shape, cuts, smallest, largest):
    level = 1.0
    for axis_at, parts in cuts:
        draws = jax.random.uniform(jax.random.fold_in(jax.random.fold_in(key, 6), axis_at), (parts,), jnp.float32, smallest / len(cuts), largest / len(cuts))
        level = level * jnp.repeat(jnp.exp(draws), shape[axis_at] // parts).reshape((-1,) + (1,) * (len(shape) - 1 - axis_at))
    return level


def centred(key, extent, deviation, bound, shards=(), kind=jnp.bfloat16):
    loudness = level_of(key, extent, shards, -0.22, 0.18) if shards else 1.0
    drawn = jax.random.normal(key, extent, jnp.float32) * deviation * loudness
    return jnp.minimum(jnp.maximum(drawn, -bound), bound).astype(kind)


def setup_inputs(seed: int = 0) -> dict:
    arg_keys = jax.random.split(jax.random.key(seed), 10)
    gate_in = centred(arg_keys[0], (SEQUENCE_LEN, W), 1.0, 6.0, ((0, 16), (1, 2)))
    value_in = centred(arg_keys[1], (SEQUENCE_LEN, W), 1.0, 6.0, ((0, 16), (1, 2)))
    out_gate = centred(arg_keys[2], (SEQUENCE_LEN, W), 1.0, 6.0, ((0, 16), (1, 2)))
    residual = draw_residual(jax.random.fold_in(arg_keys[9], 71), 0)
    filters = draw_filters(jax.random.fold_in(arg_keys[9], 71), 0)
    kept_index = draw_kept_index(jax.random.fold_in(arg_keys[9], 71), 0)
    kept_owner = draw_kept_owner(jax.random.fold_in(arg_keys[9], 71), 0)
    skip_bias = jnp.clip(jax.random.uniform(arg_keys[7], (W,), jnp.float32, -1.0, 1.0) * level_of(arg_keys[7], (W,), ((0, 2),), -0.4, 0.0), -1.0, 1.0)
    norm_gain = jnp.clip(1.0 + 0.1 * jax.random.normal(arg_keys[8], (W,), jnp.float32), 0.5, 1.5)
    return {"gate_in": gate_in, "value_in": value_in, "out_gate": out_gate, "residual": residual, "filters": filters, "kept_index": kept_index, "kept_owner": kept_owner, "skip_bias": skip_bias, "norm_gain": norm_gain}


def owner_ranks(owners_row):
    is_live = owners_row >= 0
    slot_count = owners_row.shape[0]
    token_position = jnp.arange(slot_count, dtype=jnp.int32)
    earlier = (owners_row[:, None] == owners_row[None, :]) & is_live[None, :] & (token_position[None, :] < token_position[:, None])
    return lax.optimization_barrier(jnp.sum(earlier.astype(jnp.int32), axis=1)).astype(jnp.int32)

def slab_convolve(gated_slab, slab_filters, index_row, owners_row):
    is_live = owners_row >= 0
    slot_ranks = owner_ranks(owners_row)
    safe_owner = jnp.where(is_live, owners_row, 0).astype(jnp.int32)
    safe_rank = jnp.where(is_live, slot_ranks, 0).astype(jnp.int32)
    kernels = slab_filters[safe_owner, safe_rank].astype(jnp.float32)
    safe_index = jnp.where(is_live, index_row, 0).astype(jnp.int32)
    signals = jnp.take(gated_slab, safe_index, axis=1).T
    padded = 2 * SEQUENCE_LEN
    spectrum = jnp.fft.rfft(signals, n=padded, axis=1) * jnp.fft.rfft(kernels, n=padded, axis=1)
    causal = jnp.fft.irfft(spectrum, n=padded, axis=1)[:, :SEQUENCE_LEN]
    causal = jnp.where(is_live[:, None], causal, 0.0).astype(jnp.float32)
    target = jnp.where(is_live, index_row, SLAB).astype(jnp.int32)
    return jnp.zeros((SEQUENCE_LEN, SLAB), jnp.float32).at[:, target].set(causal.T, mode='drop')

def reference(gate_in, value_in, out_gate, residual, filters, kept_index, kept_owner, skip_bias, norm_gain):
    gated_prod = (gate_in.astype(jnp.float32) * value_in.astype(jnp.float32)).astype(jnp.bfloat16)
    gated_wide = gated_prod.astype(jnp.float32)
    slab_count = W // SLAB
    by_slab = gated_wide.reshape(SEQUENCE_LEN, slab_count, SLAB).transpose(1, 0, 2)
    convolved = lax.map(lambda packed: slab_convolve(*packed), (by_slab, filters, kept_index, kept_owner))
    convolved = convolved.transpose(1, 0, 2).reshape(SEQUENCE_LEN, W)
    mixed_out = out_gate.astype(jnp.float32) * (convolved + skip_bias[None, :] * gated_wide)
    hidden_out = (residual.astype(jnp.float32) + mixed_out).astype(jnp.bfloat16)
    hidden_wide = hidden_out.astype(jnp.float32)
    row_total = lax.optimization_barrier(jnp.sum(hidden_wide * hidden_wide, axis=1, keepdims=True))
    normed = (hidden_wide * lax.rsqrt(row_total / W + 1e-06) * norm_gain[None, :]).astype(jnp.bfloat16)
    return (hidden_out, normed)
```

```python
import functools

import jax
import jax.numpy as jnp
import numpy as np
from jax import lax
from jax.experimental import pallas as pl
from jax.experimental.pallas import tpu as pltpu
from jax.sharding import PartitionSpec as P

LANES = 128
TILE = 256
MIB = 1 << 20
norm_eps = 1e-06
f32 = jnp.float32
bf16 = jnp.bfloat16


def split_np(table):
    high = table.astype(jnp.bfloat16)
    low = (table - high.astype(np.float64)).astype(jnp.bfloat16)
    return high, low


def dft_tables(length):
    inner = LANES
    outer = length // inner
    a = np.arange(outer)
    b = np.arange(inner)
    quarter = np.arange(outer) + 0.25
    outer_angle = 2 * np.pi / outer * np.mod(quarter[:, None] * a[None, :], outer)
    turn_angle = 2 * np.pi / length * (quarter[:, None] * b[None, :])
    inner_angle = 2 * np.pi / inner * np.mod(b[:, None] * b[None, :], inner)
    outer_fwd = np.concatenate([np.cos(outer_angle), -np.sin(outer_angle)], axis=0)
    c, s = np.cos(inner_angle), np.sin(inner_angle)
    inner_fwd = np.concatenate(
        [np.concatenate([c, -s], axis=1), np.concatenate([s, c], axis=1)], axis=0
    )
    inner_back = np.concatenate(
        [np.concatenate([c, s], axis=1), np.concatenate([-s, c], axis=1)], axis=0
    )
    outer_back = np.concatenate([np.cos(outer_angle).T, -np.sin(outer_angle).T], axis=1) / length
    turn = np.concatenate([np.cos(turn_angle), np.sin(turn_angle)], axis=1).astype(np.float32)
    outer_fwd = np.concatenate(split_np(outer_fwd), axis=1)
    high, low = split_np(inner_fwd)
    inner_fwd = np.concatenate([high, high, low], axis=0)
    high, low = split_np(inner_back)
    inner_back = np.concatenate([high, high, low], axis=0)
    high, low = split_np(outer_back)
    outer_back = np.concatenate([high, high, low], axis=1)
    return outer_fwd, turn, inner_fwd, inner_back, outer_back


def split(value):
    high = value.astype(bf16)
    low = (value - high.astype(f32)).astype(bf16)
    return high, low


def dot(x, y):
    return jnp.dot(x, y, preferred_element_type=f32)


def dot_rows(x, y):
    return lax.dot_general(x, y, (((0,), (0,)), ((), ())), preferred_element_type=f32)


def to_spectrum(blocks, slots, outer_fwd, turn, inner_fwd):
    outer = blocks.shape[0]
    first = dot(outer_fwd[...], jnp.concatenate([blocks, blocks], axis=0))
    cos, sin = turn[:, :LANES], turn[:, LANES:]
    result = []
    for s in range(slots):
        re = first[:outer, s * LANES : (s + 1) * LANES]
        im = first[outer:, s * LANES : (s + 1) * LANES]
        turned = jnp.concatenate([re * cos + im * sin, im * cos - re * sin], axis=1)
        high, low = split(turned)
        result.append(dot(jnp.concatenate([high, low, high], axis=1), inner_fwd[...]))
    return result


def filter_kernel(filters, outer_fwd, turn, inner_fwd, spectra):
    slots, length = filters.shape
    outer = length // LANES
    wide = filters[...].astype(f32)
    blocks = [wide[s].reshape(outer, LANES) for s in range(slots)]
    blocks = jnp.concatenate(blocks, axis=1).astype(bf16)
    parts = to_spectrum(blocks, slots, outer_fwd, turn, inner_fwd)
    for s in range(slots):
        spectra[s] = parts[s]


def convolve_kernel(signals, spectra, outer_fwd, turn, inner_fwd, inner_back, outer_back, out):
    slots = spectra.shape[0]
    outer = spectra.shape[1]
    cos, sin = turn[:, :LANES], turn[:, LANES:]
    blocks = signals[...].reshape(outer, slots * LANES)
    parts = to_spectrum(blocks, slots, outer_fwd, turn, inner_fwd)
    for s in range(slots):
        sig_re, sig_im = parts[s][:, :LANES], parts[s][:, LANES:]
        ker_re, ker_im = spectra[s, :, :LANES], spectra[s, :, LANES:]
        joint = jnp.concatenate(
            [sig_re * ker_re - sig_im * ker_im, sig_re * ker_im + sig_im * ker_re], axis=1
        )
        high, low = split(joint)
        back = dot(jnp.concatenate([high, low, high], axis=1), inner_back[...])
        re, im = back[:, :LANES], back[:, LANES:]
        turned = jnp.concatenate([re * cos - im * sin, im * cos + re * sin], axis=0)
        high, low = split(turned)
        causal = dot(outer_back[...], jnp.concatenate([high, low, high], axis=0))
        out[:, :, s * LANES : (s + 1) * LANES] = causal.reshape(
            out.shape[0], out.shape[1], LANES
        ).astype(bf16)


def iota(shape, axis):
    return lax.broadcasted_iota(jnp.int32, shape, axis)


def to_column(row):
    size = row.shape[1]
    same = iota((size, size), 0) == iota((size, size), 1)
    return jnp.sum(jnp.where(same, row, 0), axis=1, keepdims=True)


def channel_of_row(index_row, owners_row, owner_count, rows):
    slots = owners_row.shape[1]
    owners_col = to_column(owners_row)
    index_col = to_column(index_row)
    earlier = (owners_col == owners_row) & (iota((slots, slots), 1) < iota((slots, slots), 0))
    rank_col = jnp.sum(earlier.astype(jnp.int32), axis=1, keepdims=True)
    target_col = jnp.where(owners_col >= 0, rank_col * owner_count + owners_col, -1)
    hit = target_col == iota((slots, rows), 1)
    return jnp.sum(jnp.where(hit, index_col + 1, 0), axis=0, keepdims=True) - 1


def pick_rows(tile, onehot_t, rows):
    picked = dot(tile, onehot_t).T
    return [picked[:rows, i : i + LANES] for i in range(0, tile.shape[0], LANES)]


def pick_kernel(
    owner_count, slots, index, owners, gate, value, payload, picked, channels, onehot_t, acc
):
    step = pl.program_id(0)
    rows = owner_count * slots

    @pl.when(step == 0)
    def _():
        row = channel_of_row(index[...], owners[...], owner_count, onehot_t.shape[1])
        channels[...] = jnp.broadcast_to(row, channels.shape)
        onehot_t[...] = (iota(onehot_t.shape, 0) == row).astype(f32).astype(bf16)

    gated = (gate[...].astype(f32) * value[...].astype(f32)).astype(bf16)
    blocks = gate.shape[0] // LANES
    for i, block in enumerate(pick_rows(gated, onehot_t[...], rows)):
        acc[step * blocks + i] = block
        picked[i] = block.astype(bf16)

    @pl.when(step == pl.num_programs(0) - 1)
    def _():
        for s in range(slots):
            part = acc[:, s * owner_count : (s + 1) * owner_count, :]
            payload[:, :, s * LANES : (s + 1) * LANES] = jnp.swapaxes(part, 0, 1).astype(bf16)


def base_kernel(
    channels,
    skip,
    gate,
    value,
    out_gate,
    residual,
    base,
    sums,
    picked_gate,
    picked_res,
    skip_wide,
    onehot,
    kept,
    onehot_t,
):
    rows = onehot.shape[0]

    @pl.when(pl.program_id(0) == 0)
    def _():
        row = channels[0:1, :]
        onehot_t[...] = (iota(onehot_t.shape, 0) == row).astype(f32).astype(bf16)
        hit = iota(onehot.shape, 1) == to_column(row)[:rows]
        onehot[...] = hit.astype(f32).astype(bf16)
        kept[...] = jnp.broadcast_to(jnp.max(hit.astype(f32), axis=0, keepdims=True), kept.shape)
        skip_col = jnp.sum(jnp.where(hit, skip[...], 0.0), axis=1, keepdims=True)
        skip_wide[...] = jnp.broadcast_to(skip_col, skip_wide.shape)

    gated = (gate[...].astype(f32) * value[...].astype(f32)).astype(bf16).astype(f32)
    mixed = out_gate[...].astype(f32) * (skip[...] * gated)
    hidden = (residual[...].astype(f32) + mixed).astype(bf16)
    base[...] = hidden
    wide = jnp.where(kept[0:1, :] > 0.0, 0.0, hidden.astype(f32))
    squares = wide * wide
    partial = squares[:, :LANES]
    for i in range(LANES, squares.shape[1], LANES):
        partial = partial + squares[:, i : i + LANES]
    total = jnp.sum(partial.T, axis=0, keepdims=True)
    for i in range(sums.shape[0]):
        sums[i] = total[:, i * LANES : (i + 1) * LANES]
    for i, block in enumerate(pick_rows(out_gate[...], onehot_t[...], rows)):
        picked_gate[i] = block.astype(bf16)
    for i, block in enumerate(pick_rows(residual[...], onehot_t[...], rows)):
        picked_res[i] = block.astype(bf16)


def kept_kernel(conv, picked, picked_gate, picked_res, skip_wide, sums, hidden, totals):
    owner_count, blocks = conv.shape[:2]
    total = jnp.zeros((blocks, LANES), f32)
    for s in range(conv.shape[2] // LANES):
        at = slice(s * owner_count, (s + 1) * owner_count)
        conv_rows = jnp.swapaxes(conv[:, :, s * LANES : (s + 1) * LANES].astype(f32), 0, 1)
        wide = conv_rows + skip_wide[at, :] * picked[:, at, :].astype(f32)
        value = picked_res[:, at, :].astype(f32) + picked_gate[:, at, :].astype(f32) * wide
        value = value.astype(bf16)
        hidden[:, at, :] = value
        value = value.astype(f32)
        total = total + jnp.sum(value * value, axis=1)
    for i in range(blocks):
        totals[i] = total[i : i + 1, :] + sums[i]


def final_kernel(width, count, *refs):
    parts = refs[:count]
    base, hidden_kept, onehot, kept, gain, hidden, normed = refs[count:]
    for i in range(base.shape[0] // LANES):
        at = slice(i * LANES, (i + 1) * LANES)
        total = parts[0][i]
        for part in parts[1:]:
            total = total + part[i]
        scale = lax.rsqrt(total / width + norm_eps)
        scale = jnp.broadcast_to(scale, (LANES, LANES)).T[:, 0:1]
        placed = dot_rows(hidden_kept[i], onehot[...])
        wide = jnp.where(kept[0:1, :] > 0.0, placed, base[at, :].astype(f32))
        hidden[at, :] = wide.astype(bf16)
        normed[at, :] = (wide * scale * gain[...]).astype(bf16)


def whole(shape):
    return pl.BlockSpec(shape, lambda *_: (0,) * len(shape))


def call(kernel, outs, ins, flops, moved, limit, scratch=(), grid=(), specs=None, out_specs=None):
    return pl.pallas_call(
        kernel,
        out_shape=outs,
        grid=grid,
        in_specs=specs if specs is not None else [whole(x.shape) for x in ins],
        out_specs=out_specs if out_specs is not None else [whole(x.shape) for x in outs],
        scratch_shapes=list(scratch),
        compiler_params=pltpu.CompilerParams(vmem_limit_bytes=limit),
        cost_estimate=pl.CostEstimate(flops=flops, bytes_accessed=moved, transcendentals=0),
    )(*ins)


def local(
    gate_in, value_in, out_gate, residual, filters, kept_index, kept_owner, skip_bias, norm_gain
):
    tok_rows, slab = gate_in.shape
    slots, length = filters.shape[2:]
    chan_devices = lax.axis_size("chan")
    owner_count = lax.axis_size("seqo") * lax.axis_size("seqi")
    rows = slots * owner_count
    lanes_rows = -(-rows // LANES) * LANES
    blocks = tok_rows // LANES
    outer = length // LANES
    tile = min(TILE, tok_rows)
    steps = tok_rows // tile
    dense = tok_rows * slab * 2
    sds = jax.ShapeDtypeStruct
    buffer = (owner_count, blocks, slots * LANES)
    tables = [jnp.asarray(x) for x in dft_tables(length)]
    outer_fwd, turn, inner_fwd, inner_back, outer_back = tables
    skip_row = skip_bias[None, :]
    gain_row = norm_gain[None, :]
    row_tile = pl.BlockSpec((tile, slab), lambda i: (i, 0))

    block_tile = tile // LANES
    picks_tile = pl.BlockSpec((block_tile, rows, LANES), lambda i: (i, 0, 0))
    sums_tile = pl.BlockSpec((block_tile, 1, LANES), lambda i: (i, 0, 0))
    picks = sds((blocks, rows, LANES), bf16)
    row_sums = sds((blocks, 1, LANES), f32)

    outs = [sds(buffer, bf16), picks, sds((8, lanes_rows), jnp.int32)]
    payload, picked, channels = call(
        functools.partial(pick_kernel, owner_count, slots),
        outs,
        [kept_index, kept_owner, gate_in, value_in],
        2 * tok_rows * slab * rows,
        2 * dense,
        32 * MIB,
        scratch=[
            pltpu.VMEM((slab, lanes_rows), bf16),
            pltpu.VMEM((blocks, rows, LANES), f32),
        ],
        grid=(steps,),
        specs=[whole(kept_index.shape), whole(kept_owner.shape), row_tile, row_tile],
        out_specs=[whole(buffer), picks_tile, whole(outs[2].shape)],
    )

    incoming = lax.all_to_all(payload, ("seqo", "seqi"), split_axis=0, concat_axis=0, tiled=True)

    spectrum = (slots, outer, 2 * LANES)
    (spectra,) = call(
        filter_kernel,
        [sds(spectrum, f32)],
        [filters[0, 0], outer_fwd, turn, inner_fwd],
        2 * slots * length * 2 * (2 * outer + 6 * LANES),
        8 * MIB,
        32 * MIB,
    )

    outs = [
        sds((tok_rows, slab), bf16),
        row_sums,
        picks,
        picks,
        sds((rows, LANES), f32),
        sds((rows, slab), bf16),
        sds((8, slab), f32),
    ]
    base, sums, picked_gate, picked_res, skip_wide, onehot, kept = call(
        base_kernel,
        outs,
        [channels, skip_row, gate_in, value_in, out_gate, residual],
        4 * tok_rows * slab * rows,
        5 * dense,
        32 * MIB,
        scratch=[pltpu.VMEM((slab, lanes_rows), bf16)],
        grid=(steps,),
        specs=[whole(channels.shape), whole(skip_row.shape)] + [row_tile] * 4,
        out_specs=[row_tile, sums_tile, picks_tile, picks_tile]
        + [whole(x.shape) for x in outs[4:]],
    )

    (convolved,) = call(
        convolve_kernel,
        [sds(buffer, bf16)],
        [incoming, spectra, outer_fwd, turn, inner_fwd, inner_back, outer_back],
        2 * slots * length * 2 * (5 * outer + 12 * LANES),
        8 * MIB,
        32 * MIB,
    )

    returned = lax.all_to_all(convolved, ("seqo", "seqi"), split_axis=0, concat_axis=0, tiled=True)

    hidden_kept, totals = call(
        kept_kernel,
        [picks, row_sums],
        [returned, picked, picked_gate, picked_res, skip_wide, sums],
        8 * rows * tok_rows,
        10 * rows * tok_rows,
        32 * MIB,
    )

    parts = [totals]
    for shift in range(1, chan_devices):
        ring = [(i, (i + shift) % chan_devices) for i in range(chan_devices)]
        parts.append(lax.ppermute(totals, "chan", ring))

    ins = parts + [base, hidden_kept, onehot, kept, gain_row]
    specs = [sums_tile] * len(parts) + [
        row_tile,
        picks_tile,
        whole(onehot.shape),
        whole(kept.shape),
        whole(gain_row.shape),
    ]
    hidden, normed = call(
        functools.partial(final_kernel, float(slab * chan_devices), len(parts)),
        [sds((tok_rows, slab), bf16)] * 2,
        ins,
        2 * tok_rows * slab * rows,
        3 * dense,
        32 * MIB,
        grid=(steps,),
        specs=specs,
        out_specs=[row_tile, row_tile],
    )
    return (hidden, normed)


def solution(mesh):
    positions = P(("seqo", "seqi"), "chan")
    in_specs = (
        positions,
        positions,
        positions,
        positions,
        P("chan", ("seqo", "seqi"), None, None),
        P("chan", None),
        P("chan", None),
        P("chan"),
        P("chan"),
    )
    return jax.shard_map(
        local, mesh=mesh, in_specs=in_specs, out_specs=(positions, positions), check_vma=False
    )
```

```python
import functools

import jax
import jax.numpy as jnp
import numpy as np
from jax import lax
from jax.experimental import pallas as pl
from jax.experimental.pallas import tpu as pltpu
from jax.sharding import PartitionSpec as P

LANES = 128
TILE = 256
HALVES = 2
MIB = 1 << 20
norm_eps = 1e-06
f32 = jnp.float32
bf16 = jnp.bfloat16


def split_np(table):
    high = table.astype(jnp.bfloat16)
    low = (table - high.astype(np.float64)).astype(jnp.bfloat16)
    return high, low


def dft_tables(length):
    inner = LANES
    outer = length // inner
    a = np.arange(outer)
    b = np.arange(inner)
    quarter = np.arange(outer) + 0.25
    outer_angle = 2 * np.pi / outer * np.mod(quarter[:, None] * a[None, :], outer)
    turn_angle = 2 * np.pi / length * (quarter[:, None] * b[None, :])
    inner_angle = 2 * np.pi / inner * np.mod(b[:, None] * b[None, :], inner)
    outer_fwd = np.concatenate([np.cos(outer_angle), -np.sin(outer_angle)], axis=0)
    c, s = np.cos(inner_angle), np.sin(inner_angle)
    inner_fwd = np.concatenate(
        [np.concatenate([c, -s], axis=1), np.concatenate([s, c], axis=1)], axis=0
    )
    inner_back = np.concatenate(
        [np.concatenate([c, s], axis=1), np.concatenate([-s, c], axis=1)], axis=0
    )
    outer_back = np.concatenate([np.cos(outer_angle).T, -np.sin(outer_angle).T], axis=1) / length
    turn = np.concatenate([np.cos(turn_angle), np.sin(turn_angle)], axis=1).astype(np.float32)
    outer_fwd = np.concatenate(split_np(outer_fwd), axis=1)
    high, low = split_np(inner_fwd)
    inner_fwd = np.concatenate([high, high, low], axis=0)
    high, low = split_np(inner_back)
    inner_back = np.concatenate([high, high, low], axis=0)
    high, low = split_np(outer_back)
    outer_back = np.concatenate([high, high, low], axis=1)
    return outer_fwd, turn, inner_fwd, inner_back, outer_back


def split(value):
    high = value.astype(bf16)
    low = (value - high.astype(f32)).astype(bf16)
    return high, low


def dot(x, y):
    return jnp.dot(x, y, preferred_element_type=f32)


def dot_rows(x, y):
    return lax.dot_general(x, y, (((0,), (0,)), ((), ())), preferred_element_type=f32)


def to_spectrum(blocks, slots, outer_fwd, turn, inner_fwd):
    outer = blocks.shape[0]
    first = dot(outer_fwd[...], jnp.concatenate([blocks, blocks], axis=0))
    cos, sin = turn[:, :LANES], turn[:, LANES:]
    result = []
    for s in range(slots):
        re = first[:outer, s * LANES : (s + 1) * LANES]
        im = first[outer:, s * LANES : (s + 1) * LANES]
        turned = jnp.concatenate([re * cos + im * sin, im * cos - re * sin], axis=1)
        high, low = split(turned)
        result.append(dot(jnp.concatenate([high, low, high], axis=1), inner_fwd[...]))
    return result


def filter_kernel(filters, outer_fwd, turn, inner_fwd, spectra):
    slots, length = filters.shape
    outer = length // LANES
    wide = filters[...].astype(f32)
    blocks = [wide[s].reshape(outer, LANES) for s in range(slots)]
    blocks = jnp.concatenate(blocks, axis=1).astype(bf16)
    parts = to_spectrum(blocks, slots, outer_fwd, turn, inner_fwd)
    for s in range(slots):
        spectra[s] = parts[s]


def convolve_kernel(signals, spectra, outer_fwd, turn, inner_fwd, inner_back, outer_back, out):
    slots = spectra.shape[0]
    outer = spectra.shape[1]
    cos, sin = turn[:, :LANES], turn[:, LANES:]
    blocks = signals[...].reshape(outer, slots * LANES)
    parts = to_spectrum(blocks, slots, outer_fwd, turn, inner_fwd)
    for s in range(slots):
        sig_re, sig_im = parts[s][:, :LANES], parts[s][:, LANES:]
        ker_re, ker_im = spectra[s, :, :LANES], spectra[s, :, LANES:]
        joint = jnp.concatenate(
            [sig_re * ker_re - sig_im * ker_im, sig_re * ker_im + sig_im * ker_re], axis=1
        )
        high, low = split(joint)
        back = dot(jnp.concatenate([high, low, high], axis=1), inner_back[...])
        re, im = back[:, :LANES], back[:, LANES:]
        turned = jnp.concatenate([re * cos - im * sin, im * cos + re * sin], axis=0)
        high, low = split(turned)
        causal = dot(outer_back[...], jnp.concatenate([high, low, high], axis=0))
        out[:, :, s * LANES : (s + 1) * LANES] = causal.reshape(
            out.shape[0], out.shape[1], LANES
        ).astype(bf16)


def iota(shape, axis):
    return lax.broadcasted_iota(jnp.int32, shape, axis)


def to_column(row):
    size = row.shape[1]
    same = iota((size, size), 0) == iota((size, size), 1)
    return jnp.sum(jnp.where(same, row, 0), axis=1, keepdims=True)


def channel_of_row(index_row, owners_row, owner_count, rows):
    slots = owners_row.shape[1]
    owners_col = to_column(owners_row)
    index_col = to_column(index_row)
    earlier = (owners_col == owners_row) & (iota((slots, slots), 1) < iota((slots, slots), 0))
    rank_col = jnp.sum(earlier.astype(jnp.int32), axis=1, keepdims=True)
    target_col = jnp.where(owners_col >= 0, rank_col * owner_count + owners_col, -1)
    hit = target_col == iota((slots, rows), 1)
    return jnp.sum(jnp.where(hit, index_col + 1, 0), axis=0, keepdims=True) - 1


def pick_rows(tile, onehot_t, rows):
    picked = dot(tile, onehot_t).T
    return [picked[:rows, i : i + LANES] for i in range(0, tile.shape[0], LANES)]


def pick_kernel(
    owner_count, slots, index, owners, gate, value, payload, picked, channels, onehot_t, acc
):
    step = pl.program_id(0)
    rows = owner_count * slots

    @pl.when(step == 0)
    def _():
        row = channel_of_row(index[...], owners[...], owner_count, onehot_t.shape[1])
        channels[...] = jnp.broadcast_to(row, channels.shape)
        onehot_t[...] = (iota(onehot_t.shape, 0) == row).astype(f32).astype(bf16)

    blocks = gate.shape[0] // LANES
    for i, block in enumerate(pick_rows(gate[...] * value[...], onehot_t[...], rows)):
        acc[step * blocks + i] = block
        picked[i] = block.astype(bf16)

    @pl.when(step == pl.num_programs(0) - 1)
    def _():
        for s in range(slots):
            part = acc[:, s * owner_count : (s + 1) * owner_count, :]
            payload[:, :, s * LANES : (s + 1) * LANES] = jnp.swapaxes(part, 0, 1).astype(bf16)


def place_kernel(channels, skip, onehot, others, skip_wide):
    hit = iota(onehot.shape, 1) == to_column(channels[0:1, :])[: onehot.shape[0]]
    onehot[...] = hit.astype(f32).astype(bf16)
    others[...] = jnp.broadcast_to(1.0 - jnp.max(hit.astype(f32), axis=0, keepdims=True), others.shape)
    skip_col = jnp.sum(jnp.where(hit, skip[...], 0.0), axis=1, keepdims=True)
    skip_wide[...] = jnp.broadcast_to(skip_col, skip_wide.shape)


def base_kernel(onehot_t, others, skip, gate, value, out_gate, residual, *refs):
    base, sums, picked_gate, picked_res = refs[-4:]
    rows = picked_gate.shape[1]
    gated = (gate[...] * value[...]).astype(f32)
    mixed = out_gate[...].astype(f32) * (skip[...] * gated)
    hidden = ((residual[...].astype(f32) + mixed) * others[0:1, :]).astype(bf16)
    base[...] = hidden
    wide = hidden.astype(f32)
    squares = wide * wide
    partial = squares[:, :LANES]
    for i in range(LANES, squares.shape[1], LANES):
        partial = partial + squares[:, i : i + LANES]
    total = jnp.sum(partial.T, axis=0, keepdims=True)
    for i in range(sums.shape[0]):
        sums[i] = total[:, i * LANES : (i + 1) * LANES]
    for i, block in enumerate(pick_rows(out_gate[...], onehot_t[...], rows)):
        picked_gate[i] = block.astype(bf16)
    for i, block in enumerate(pick_rows(residual[...], onehot_t[...], rows)):
        picked_res[i] = block.astype(bf16)


def kept_kernel(halves, conv, picked, skip_wide, *refs):
    hidden, totals = refs[-2:]
    owner_count, blocks = conv.shape[:2]
    size = blocks // halves
    for h in range(halves):
        sums, picked_gate, picked_res = refs[3 * h : 3 * h + 3]
        at_h = slice(h * size, (h + 1) * size)
        total = jnp.zeros((size, LANES), f32)
        for s in range(conv.shape[2] // LANES):
            at = slice(s * owner_count, (s + 1) * owner_count)
            conv_rows = conv[:, at_h, s * LANES : (s + 1) * LANES].astype(f32)
            conv_rows = jnp.swapaxes(conv_rows, 0, 1)
            wide = conv_rows + skip_wide[at, :] * picked[at_h, at, :].astype(f32)
            value = picked_res[:, at, :].astype(f32) + picked_gate[:, at, :].astype(f32) * wide
            value = value.astype(bf16)
            hidden[at_h, at, :] = value
            value = value.astype(f32)
            total = total + jnp.sum(value * value, axis=1)
        for i in range(size):
            totals[h * size + i] = total[i : i + 1, :] + sums[i]


def hidden_kernel(base, hidden_kept, onehot, hidden, held):
    for i in range(hidden.shape[0] // LANES):
        rows = slice(i * LANES, (i + 1) * LANES)
        value = base[rows, :] + dot_rows(hidden_kept[i], onehot[...]).astype(bf16)
        hidden[rows, :] = value
        held[rows, :] = value


def norm_kernel(width, count, *refs):
    parts = refs[:count]
    held, gain, normed = refs[count:]
    for i in range(normed.shape[0] // LANES):
        total = parts[0][i]
        for part in parts[1:]:
            total = total + part[i]
        scale = lax.rsqrt(total / width + norm_eps)
        scale = jnp.broadcast_to(scale, (LANES, LANES)).T[:, 0:1]
        rows = slice(i * LANES, (i + 1) * LANES)
        wide = held[rows, :].astype(f32)
        normed[rows, :] = (wide * scale * gain[...]).astype(bf16)


def whole(shape):
    return pl.BlockSpec(shape, lambda *_: (0,) * len(shape))


def in_hbm(x):
    return pltpu.with_memory_space_constraint(x, pltpu.HBM)


def call(
    kernel, outs, ins, flops, moved, limit, scratch=(), grid=(), specs=None, out_specs=None, alias=None
):
    return pl.pallas_call(
        kernel,
        out_shape=outs,
        grid=grid,
        in_specs=specs if specs is not None else [whole(x.shape) for x in ins],
        out_specs=out_specs if out_specs is not None else [whole(x.shape) for x in outs],
        scratch_shapes=list(scratch),
        input_output_aliases=alias or {},
        compiler_params=pltpu.CompilerParams(vmem_limit_bytes=limit),
        cost_estimate=pl.CostEstimate(flops=flops, bytes_accessed=moved, transcendentals=0),
    )(*ins)


def local(
    gate_in, value_in, out_gate, residual, filters, kept_index, kept_owner, skip_bias, norm_gain
):
    tok_rows, slab = gate_in.shape
    slots, length = filters.shape[2:]
    chan_devices = lax.axis_size("chan")
    owner_count = lax.axis_size("seqo") * lax.axis_size("seqi")
    rows = slots * owner_count
    lanes_rows = -(-rows // LANES) * LANES
    blocks = tok_rows // LANES
    outer = length // LANES
    tile = min(TILE, tok_rows // HALVES)
    steps = tok_rows // tile
    half = steps // HALVES
    dense = tok_rows * slab * 2
    sds = jax.ShapeDtypeStruct
    buffer = (owner_count, blocks, slots * LANES)
    tables = [jnp.asarray(x) for x in dft_tables(length)]
    outer_fwd, turn, inner_fwd, inner_back, outer_back = tables
    skip_row = skip_bias[None, :]
    gain_row = norm_gain[None, :]
    gate_in, value_in, out_gate, residual = map(in_hbm, (gate_in, value_in, out_gate, residual))
    row_tile = pl.BlockSpec((tile, slab), lambda i: (i, 0))
    block_tile = tile // LANES
    picks_tile = pl.BlockSpec((block_tile, rows, LANES), lambda i: (i, 0, 0))
    sums_tile = pl.BlockSpec((block_tile, 1, LANES), lambda i: (i, 0, 0))
    picks = sds((blocks, rows, LANES), bf16)
    row_sums = sds((blocks, 1, LANES), f32)

    outs = [
        sds(buffer, bf16),
        picks,
        sds((8, lanes_rows), jnp.int32),
        sds((slab, lanes_rows), bf16),
    ]
    payload, picked, channels, onehot_t = call(
        functools.partial(pick_kernel, owner_count, slots),
        outs,
        [in_hbm(kept_index), in_hbm(kept_owner), gate_in, value_in],
        2 * tok_rows * slab * rows,
        2 * dense,
        16 * MIB,
        scratch=[pltpu.VMEM((blocks, rows, LANES), f32)],
        grid=(steps,),
        specs=[whole(kept_index.shape), whole(kept_owner.shape), row_tile, row_tile],
        out_specs=[whole(buffer), picks_tile] + [whole(x.shape) for x in outs[2:]],
    )

    incoming = lax.all_to_all(payload, ("seqo", "seqi"), split_axis=0, concat_axis=0, tiled=True)

    (spectra,) = call(
        filter_kernel,
        [sds((slots, outer, 2 * LANES), f32)],
        [filters[0, 0], outer_fwd, turn, inner_fwd],
        2 * slots * length * 2 * (2 * outer + 6 * LANES),
        8 * MIB,
        16 * MIB,
    )
    onehot, others, skip_wide = call(
        place_kernel,
        [sds((rows, slab), bf16), sds((8, slab), f32), sds((rows, LANES), f32)],
        [channels, skip_row],
        rows * slab * 8,
        rows * slab * 2,
        8 * MIB,
    )

    def base_half(h, onehot_t, base):
        first = h * half
        place = pl.BlockSpec((tile, slab), lambda i: (first + i, 0))
        outs = [
            pltpu.VMEM((tok_rows, slab), bf16),
            sds((blocks // HALVES, 1, LANES), f32),
            sds((blocks // HALVES, rows, LANES), bf16),
            sds((blocks // HALVES, rows, LANES), bf16),
        ]
        ins = [onehot_t, others, skip_row, gate_in, value_in, out_gate, residual]
        specs = [whole(x.shape) for x in ins[:3]] + [place] * 4
        alias = None
        if base is not None:
            alias = {len(ins): 0}
            ins = ins + [base]
            specs = specs + [pl.BlockSpec(memory_space=pl.ANY)]
        return call(
            base_kernel,
            outs,
            ins,
            4 * tok_rows * slab * rows // HALVES,
            5 * dense // HALVES,
            20 * MIB,
            grid=(half,),
            specs=specs,
            out_specs=[place, sums_tile, picks_tile, picks_tile],
            alias=alias,
        )

    base, *half_picks = base_half(0, onehot_t, None)
    spectra, base = lax.optimization_barrier((spectra, base))

    (convolved,) = call(
        convolve_kernel,
        [sds(buffer, bf16)],
        [incoming, spectra, outer_fwd, turn, inner_fwd, inner_back, outer_back],
        2 * slots * length * 2 * (5 * outer + 12 * LANES),
        8 * MIB,
        20 * MIB,
    )
    convolved, onehot_t = lax.optimization_barrier((convolved, onehot_t))

    returned = lax.all_to_all(convolved, ("seqo", "seqi"), split_axis=0, concat_axis=0, tiled=True)

    base, *more_picks = base_half(1, onehot_t, base)

    hidden_kept, totals = call(
        functools.partial(kept_kernel, HALVES),
        [picks, row_sums],
        [returned, picked, skip_wide, *half_picks, *more_picks],
        8 * rows * tok_rows,
        10 * rows * tok_rows,
        16 * MIB,
    )

    parts = [totals]
    for shift in range(1, chan_devices):
        ring = [(i, (i + shift) % chan_devices) for i in range(chan_devices)]
        parts.append(lax.ppermute(totals, "chan", ring))

    hidden, held = call(
        hidden_kernel,
        [sds((tok_rows, slab), bf16), pltpu.VMEM((tok_rows, slab), bf16)],
        [base, hidden_kept, onehot],
        2 * tok_rows * slab * rows,
        dense,
        16 * MIB,
        grid=(steps,),
        specs=[row_tile, picks_tile, whole(onehot.shape)],
        out_specs=[row_tile, row_tile],
    )
    (normed,) = call(
        functools.partial(norm_kernel, float(slab * chan_devices), len(parts)),
        [sds((tok_rows, slab), bf16)],
        parts + [held, gain_row],
        4 * tok_rows * slab,
        dense,
        16 * MIB,
        grid=(steps,),
        specs=[sums_tile] * len(parts) + [row_tile, whole(gain_row.shape)],
        out_specs=[row_tile],
    )
    return (hidden, normed)


def solution(mesh):
    positions = P(("seqo", "seqi"), "chan")
    in_specs = (
        positions,
        positions,
        positions,
        positions,
        P("chan", ("seqo", "seqi"), None, None),
        P("chan", None),
        P("chan", None),
        P("chan"),
        P("chan"),
    )
    return jax.shard_map(
        local, mesh=mesh, in_specs=in_specs, out_specs=(positions, positions), check_vma=False
    )
```

```python
import functools

import jax
import jax.numpy as jnp
import numpy as np
from jax import lax
from jax.experimental import pallas as pl
from jax.experimental.pallas import tpu as pltpu
from jax.sharding import PartitionSpec as P

LANES = 128
TILE = 256
CHUNK = 16
MIB = 1 << 20
norm_eps = 1e-06
f32 = jnp.float32
bf16 = jnp.bfloat16


def split_np(table):
    high = table.astype(jnp.bfloat16)
    low = (table - high.astype(np.float64)).astype(jnp.bfloat16)
    return high, low


def dft_tables(length):
    inner = LANES
    outer = length // inner
    a = np.arange(outer)
    b = np.arange(inner)
    quarter = np.arange(outer) + 0.25
    outer_angle = 2 * np.pi / outer * np.mod(quarter[:, None] * a[None, :], outer)
    turn_angle = 2 * np.pi / length * (quarter[:, None] * b[None, :])
    inner_angle = 2 * np.pi / inner * np.mod(b[:, None] * b[None, :], inner)
    outer_fwd = np.concatenate([np.cos(outer_angle), -np.sin(outer_angle)], axis=0)
    c, s = np.cos(inner_angle), np.sin(inner_angle)
    inner_fwd = np.concatenate(
        [np.concatenate([c, -s], axis=1), np.concatenate([s, c], axis=1)], axis=0
    )
    inner_back = np.concatenate(
        [np.concatenate([c, s], axis=1), np.concatenate([-s, c], axis=1)], axis=0
    )
    outer_back = np.concatenate([np.cos(outer_angle).T, -np.sin(outer_angle).T], axis=1) / length
    turn = np.concatenate([np.cos(turn_angle), np.sin(turn_angle)], axis=1).astype(np.float32)
    outer_fwd = np.concatenate(split_np(outer_fwd), axis=1)
    high, low = split_np(inner_fwd)
    inner_fwd = np.concatenate([high, high, low], axis=0)
    high, low = split_np(inner_back)
    inner_back = np.concatenate([high, high, low], axis=0)
    high, low = split_np(outer_back)
    outer_back = np.concatenate([high, high, low], axis=1)
    return outer_fwd, turn, inner_fwd, inner_back, outer_back


def split(value):
    high = value.astype(bf16)
    low = (value - high.astype(f32)).astype(bf16)
    return high, low


def dot(x, y):
    return jnp.dot(x, y, preferred_element_type=f32)


def dot_rows(x, y):
    return lax.dot_general(x, y, (((0,), (0,)), ((), ())), preferred_element_type=f32)


def to_spectrum(blocks, slots, outer_fwd, turn, inner_fwd):
    outer = blocks.shape[0]
    first = dot(outer_fwd[...], jnp.concatenate([blocks, blocks], axis=0))
    cos, sin = turn[:, :LANES], turn[:, LANES:]
    result = []
    for s in range(slots):
        re = first[:outer, s * LANES : (s + 1) * LANES]
        im = first[outer:, s * LANES : (s + 1) * LANES]
        turned = jnp.concatenate([re * cos + im * sin, im * cos - re * sin], axis=1)
        high, low = split(turned)
        result.append(dot(jnp.concatenate([high, low, high], axis=1), inner_fwd[...]))
    return result


def filter_kernel(filters, outer_fwd, turn, inner_fwd, spectra):
    slots, length = filters.shape
    outer = length // LANES
    wide = filters[...].astype(f32)
    blocks = [wide[s].reshape(outer, LANES) for s in range(slots)]
    blocks = jnp.concatenate(blocks, axis=1).astype(bf16)
    parts = to_spectrum(blocks, slots, outer_fwd, turn, inner_fwd)
    for s in range(slots):
        spectra[s] = parts[s]


def convolve_kernel(owner_count, *refs):
    signals = refs[:owner_count]
    spectra, outer_fwd, turn, inner_fwd, inner_back, outer_back = refs[owner_count : owner_count + 6]
    outs = refs[owner_count + 6 : 2 * owner_count + 6]
    blocks, result = refs[2 * owner_count + 6 :]
    slots, outer = spectra.shape[:2]
    piece = outer // owner_count
    me = my_place()
    places = [
        pl.ds(pl.multiple_of(partner(me, d, owner_count, -1) * piece, piece), piece)
        for d in range(owner_count)
    ]
    for d in range(owner_count):
        blocks[places[d], :] = signals[d][...]
    cos, sin = turn[:, :LANES], turn[:, LANES:]
    parts = to_spectrum(blocks[...], slots, outer_fwd, turn, inner_fwd)
    for s in range(slots):
        sig_re, sig_im = parts[s][:, :LANES], parts[s][:, LANES:]
        ker_re, ker_im = spectra[s, :, :LANES], spectra[s, :, LANES:]
        joint = jnp.concatenate(
            [sig_re * ker_re - sig_im * ker_im, sig_re * ker_im + sig_im * ker_re], axis=1
        )
        high, low = split(joint)
        back = dot(jnp.concatenate([high, low, high], axis=1), inner_back[...])
        re, im = back[:, :LANES], back[:, LANES:]
        turned = jnp.concatenate([re * cos - im * sin, im * cos + re * sin], axis=0)
        high, low = split(turned)
        causal = dot(outer_back[...], jnp.concatenate([high, low, high], axis=0))
        result[:, s * LANES : (s + 1) * LANES] = causal.astype(bf16)
    for d in range(owner_count):
        outs[d][...] = result[places[d], :]


def my_place():
    return lax.axis_index("seqo") * lax.axis_size("seqi") + lax.axis_index("seqi")


def partner(place, d, count, sign=1):
    if count & (count - 1) == 0:
        return lax.bitwise_xor(place, d) if not isinstance(place, int) else place ^ d
    return (place + sign * d + count) % count


def relative(owner, me, count):
    if count & (count - 1) == 0:
        return lax.bitwise_xor(owner, me)
    return lax.rem(owner - me + count, count)


def iota(shape, axis):
    return lax.broadcasted_iota(jnp.int32, shape, axis)


def to_column(row):
    size = row.shape[1]
    same = iota((size, size), 0) == iota((size, size), 1)
    return jnp.sum(jnp.where(same, row, 0), axis=1, keepdims=True)


def channel_of_row(index_row, owners_row, owner_count, rows):
    slots = owners_row.shape[1]
    owners_col = to_column(owners_row)
    index_col = to_column(index_row)
    earlier = (owners_col == owners_row) & (iota((slots, slots), 1) < iota((slots, slots), 0))
    rank_col = jnp.sum(earlier.astype(jnp.int32), axis=1, keepdims=True)
    place_col = relative(owners_col, jnp.full_like(owners_col, my_place()), owner_count)
    target_col = jnp.where(owners_col >= 0, rank_col * owner_count + place_col, -1)
    hit = target_col == iota((slots, rows), 1)
    return jnp.sum(jnp.where(hit, index_col + 1, 0), axis=0, keepdims=True) - 1


def pick_rows(tile, onehot_t, rows):
    picked = dot(tile, onehot_t).T
    return [picked[:rows, i : i + LANES] for i in range(0, tile.shape[0], LANES)]


def fetch(sources, stages, sems):
    tile = TILE if sources[0].shape[0] % TILE == 0 else LANES
    count = sources[0].shape[0] // tile

    def copies(i):
        rows = pl.ds(pl.multiple_of(i * tile, tile), tile)
        return [
            pltpu.make_async_copy(source.at[rows, :], stage.at[rows, :], sems.at[n, i])
            for n, (source, stage) in enumerate(zip(sources, stages))
        ]

    for i in range(count):
        for copy in copies(i):
            copy.start()

    def wait(i):
        for copy in copies(i):
            copy.wait()
        return pl.multiple_of(i * tile, tile)

    return wait, tile, count


def pick_kernel(owner_count, slots, index, owners, gate, value, *refs):
    gated, picked, channels, onehot_t = refs[:4]
    payload = refs[4 : 4 + owner_count]
    acc, gate_stage, value_stage, lists, list_sems, sems = refs[4 + owner_count :]
    rows = owner_count * slots
    list_copies = [
        pltpu.make_async_copy(source, lists.at[n], list_sems.at[n])
        for n, source in enumerate((index, owners))
    ]
    for copy in list_copies:
        copy.start()
    wait, tile, count = fetch((gate, value), (gate_stage, value_stage), sems)
    for copy in list_copies:
        copy.wait()
    row = channel_of_row(lists[0], lists[1], owner_count, onehot_t.shape[1])
    channels[...] = jnp.broadcast_to(row, channels.shape)
    onehot_t[...] = (iota(onehot_t.shape, 0) == row).astype(f32).astype(bf16)

    def step(i, _):
        first = wait(i)
        at = pl.ds(first, tile)
        gated[at, :] = gate_stage[at, :] * value_stage[at, :]
        for n, block in enumerate(pick_rows(gated[at, :], onehot_t[...], rows)):
            acc[i * (tile // LANES) + n] = block
            picked[i * (tile // LANES) + n] = block.astype(bf16)
        return 0

    lax.fori_loop(0, count, step, 0)
    for s in range(slots):
        part = jnp.swapaxes(acc[:, s * owner_count : (s + 1) * owner_count, :], 0, 1)
        part = part.astype(bf16)
        for d in range(owner_count):
            payload[d][:, s * LANES : (s + 1) * LANES] = part[d]


def place_kernel(channels, skip, onehot, others, skip_wide):
    hit = iota(onehot.shape, 1) == to_column(channels[0:1, :])[: onehot.shape[0]]
    onehot[...] = hit.astype(f32).astype(bf16)
    others[...] = jnp.broadcast_to(1.0 - jnp.max(hit.astype(f32), axis=0, keepdims=True), others.shape)
    skip_col = jnp.sum(jnp.where(hit, skip[...], 0.0), axis=1, keepdims=True)
    skip_wide[...] = jnp.broadcast_to(skip_col, skip_wide.shape)


def base_kernel(onehot_t, others, skip, gated, out_gate, residual, *refs):
    base, sums, picked_gate, picked_res, gate_stage, res_stage, partial, sems = refs
    rows = picked_gate.shape[1]
    slab = gated.shape[1]
    wait, tile, count = fetch((out_gate, residual), (gate_stage, res_stage), sems)

    def step(i, _):
        first = wait(i)
        for c in range(0, tile, CHUNK):
            at = pl.ds(first + c, CHUNK)
            total = jnp.zeros((CHUNK, LANES), f32)
            for j in range(0, slab, LANES):
                lanes = slice(j, j + LANES)
                mixed = skip[:, lanes] * gated[at, lanes].astype(f32)
                mixed = gate_stage[at, lanes].astype(f32) * mixed
                hidden = (res_stage[at, lanes].astype(f32) + mixed) * others[0:1, lanes]
                hidden = hidden.astype(bf16)
                base[at, lanes] = hidden
                hidden = hidden.astype(f32)
                total = total + hidden * hidden
            partial[c : c + CHUNK, :] = total
        total = jnp.sum(partial[...].T, axis=0, keepdims=True)
        at = pl.ds(first, tile)
        picks_gate = pick_rows(gate_stage[at, :], onehot_t[...], rows)
        picks_res = pick_rows(res_stage[at, :], onehot_t[...], rows)
        for n in range(tile // LANES):
            block = i * (tile // LANES) + n
            sums[block] = total[:, n * LANES : (n + 1) * LANES]
            picked_gate[block] = picks_gate[n].astype(bf16)
            picked_res[block] = picks_res[n].astype(bf16)
        return 0

    lax.fori_loop(0, count, step, 0)


def kept_kernel(owner_count, *refs):
    conv = refs[:owner_count]
    picked, skip_wide, sums, picked_gate, picked_res, hidden, totals, wide_conv = refs[owner_count:]
    blocks, rows = picked.shape[:2]
    for d in range(owner_count):
        wide_conv[d] = conv[d][...].astype(f32)
    total = jnp.zeros((blocks, LANES), f32)
    for s in range(rows // owner_count):
        at = slice(s * owner_count, (s + 1) * owner_count)
        wide = jnp.swapaxes(wide_conv[:, :, s * LANES : (s + 1) * LANES], 0, 1)
        wide = wide + skip_wide[at, :] * picked[:, at, :].astype(f32)
        value = picked_res[:, at, :].astype(f32) + picked_gate[:, at, :].astype(f32) * wide
        value = value.astype(bf16)
        hidden[:, at, :] = value
        value = value.astype(f32)
        total = total + jnp.sum(value * value, axis=1)
    for i in range(blocks):
        totals[i] = total[i : i + 1, :] + sums[i]


def hidden_kernel(base, hidden_kept, onehot, hidden, held, sems):
    slab = held.shape[1]
    wide = min(slab, 2 * LANES)

    def copy(i):
        rows = pl.ds(pl.multiple_of(i * LANES, LANES), LANES)
        return pltpu.make_async_copy(held.at[rows, :], hidden.at[rows, :], sems.at[i])

    def step(i, _):
        rows = pl.ds(pl.multiple_of(i * LANES, LANES), LANES)
        kept = hidden_kept[i].astype(f32).T.astype(bf16)
        for j in range(0, slab, wide):
            lanes = slice(j, j + wide)
            held[rows, lanes] = base[rows, lanes] + dot(kept, onehot[:, lanes]).astype(bf16)
        copy(i).start()
        return 0

    lax.fori_loop(0, sems.shape[0], step, 0)
    lax.fori_loop(0, sems.shape[0], lambda i, _: (copy(i).wait(), 0)[1], 0)


def norm_kernel(width, count, *refs):
    parts = refs[:count]
    held, gain, normed, stage, turned, sems = refs[count:]
    slab = held.shape[1]

    def copy(i):
        rows = pl.ds(pl.multiple_of(i * LANES, LANES), LANES)
        return pltpu.make_async_copy(stage.at[rows, :], normed.at[rows, :], sems.at[i])

    def step(i, _):
        total = parts[0][i]
        for part in parts[1:]:
            total = total + part[i]
        scale = lax.rsqrt(total / width + norm_eps)
        turned[...] = jnp.broadcast_to(scale, (LANES, LANES)).T
        first = pl.multiple_of(i * LANES, LANES)
        for c in range(0, LANES, CHUNK):
            at = pl.ds(first + c, CHUNK)
            scales = turned[c : c + CHUNK, :]
            for j in range(0, slab, LANES):
                lanes = slice(j, j + LANES)
                value = held[at, lanes].astype(f32) * scales * gain[:, lanes]
                stage[at, lanes] = value.astype(bf16)
        copy(i).start()
        return 0

    lax.fori_loop(0, sems.shape[0], step, 0)
    lax.fori_loop(0, sems.shape[0], lambda i, _: (copy(i).wait(), 0)[1], 0)


def in_hbm(x):
    return pltpu.with_memory_space_constraint(x, pltpu.HBM)


def in_vmem(x):
    return pltpu.with_memory_space_constraint(x, pltpu.VMEM)


def call(kernel, outs, ins, flops, moved, limit, scratch=(), far=(), far_outs=()):
    near = pl.BlockSpec(memory_space=pltpu.VMEM)
    away = pl.BlockSpec(memory_space=pl.ANY)
    return pl.pallas_call(
        kernel,
        out_shape=outs,
        in_specs=[away if n in far else near for n in range(len(ins))],
        out_specs=[away if n in far_outs else near for n in range(len(outs))],
        scratch_shapes=list(scratch),
        compiler_params=pltpu.CompilerParams(vmem_limit_bytes=limit),
        cost_estimate=pl.CostEstimate(flops=flops, bytes_accessed=moved, transcendentals=0),
    )(*ins)


def exchange(pieces, sign):
    count = len(pieces)
    result = [pieces[0]]
    for d in range(1, count):
        pairs = [(i, partner(i, d, count, sign)) for i in range(count)]
        result.append(lax.ppermute(pieces[d], ("seqo", "seqi"), pairs))
    return result


def local(
    gate_in, value_in, out_gate, residual, filters, kept_index, kept_owner, skip_bias, norm_gain
):
    tok_rows, slab = gate_in.shape
    slots, length = filters.shape[2:]
    chan_devices = lax.axis_size("chan")
    owner_count = lax.axis_size("seqo") * lax.axis_size("seqi")
    rows = slots * owner_count
    lanes_rows = -(-rows // LANES) * LANES
    blocks = tok_rows // LANES
    outer = length // LANES
    tiles = tok_rows // (TILE if tok_rows % TILE == 0 else LANES)
    dense = tok_rows * slab * 2
    sds = jax.ShapeDtypeStruct
    tables = [jnp.asarray(x) for x in dft_tables(length)]
    outer_fwd, turn, inner_fwd, inner_back, outer_back = tables
    skip_row = skip_bias[None, :]
    gain_row = norm_gain[None, :]
    gate_in, value_in, out_gate, residual = map(in_hbm, (gate_in, value_in, out_gate, residual))
    picks = sds((blocks, rows, LANES), bf16)
    row_sums = sds((blocks, 1, LANES), f32)
    piece = sds((blocks, slots * LANES), bf16)
    whole = (tok_rows, slab)

    outs = [
        pltpu.VMEM(whole, bf16),
        picks,
        sds((8, lanes_rows), jnp.int32),
        sds((slab, lanes_rows), bf16),
    ] + [piece] * owner_count
    gated, picked, channels, onehot_t, *payload = call(
        functools.partial(pick_kernel, owner_count, slots),
        outs,
        [in_hbm(kept_index), in_hbm(kept_owner), gate_in, value_in],
        2 * tok_rows * slab * rows,
        2 * dense,
        24 * MIB,
        scratch=[
            pltpu.VMEM((blocks, rows, LANES), f32),
            pltpu.VMEM(whole, bf16),
            pltpu.VMEM(whole, bf16),
            pltpu.VMEM((2,) + kept_index.shape, jnp.int32),
            pltpu.SemaphoreType.DMA((2,)),
            pltpu.SemaphoreType.DMA((2, tiles)),
        ],
        far=(0, 1, 2, 3),
    )

    incoming = exchange(payload, 1)

    (spectra,) = call(
        filter_kernel,
        [sds((slots, outer, 2 * LANES), f32)],
        [filters[0, 0], outer_fwd, turn, inner_fwd],
        2 * slots * length * 2 * (2 * outer + 6 * LANES),
        8 * MIB,
        16 * MIB,
    )
    onehot, others, skip_wide = call(
        place_kernel,
        [sds((rows, slab), bf16), sds((8, slab), f32), sds((rows, LANES), f32)],
        [channels, skip_row],
        rows * slab * 8,
        rows * slab * 2,
        8 * MIB,
    )
    base, sums, picked_gate, picked_res = call(
        base_kernel,
        [pltpu.VMEM(whole, bf16), row_sums, picks, picks],
        [onehot_t, others, skip_row, in_vmem(gated), out_gate, residual],
        4 * tok_rows * slab * rows,
        4 * dense,
        24 * MIB,
        scratch=[
            pltpu.VMEM(whole, bf16),
            pltpu.VMEM(whole, bf16),
            pltpu.VMEM((tok_rows // tiles, LANES), f32),
            pltpu.SemaphoreType.DMA((2, tiles)),
        ],
        far=(4, 5),
    )
    spectra, base = lax.optimization_barrier((spectra, base))

    convolved = call(
        functools.partial(convolve_kernel, owner_count),
        [piece] * owner_count,
        incoming + [spectra, outer_fwd, turn, inner_fwd, inner_back, outer_back],
        2 * slots * length * 2 * (5 * outer + 12 * LANES),
        8 * MIB,
        20 * MIB,
        scratch=[pltpu.VMEM((outer, slots * LANES), bf16)] * 2,
    )
    returned = exchange(list(convolved), -1)

    hidden_kept, totals = call(
        functools.partial(kept_kernel, owner_count),
        [picks, row_sums],
        returned + [picked, skip_wide, sums, picked_gate, picked_res],
        8 * rows * tok_rows,
        10 * rows * tok_rows,
        16 * MIB,
        scratch=[pltpu.VMEM((owner_count, blocks, slots * LANES), f32)],
    )

    parts = [totals]
    for shift in range(1, chan_devices):
        ring = [(i, (i + shift) % chan_devices) for i in range(chan_devices)]
        parts.append(lax.ppermute(totals, "chan", ring))

    hidden, held = call(
        hidden_kernel,
        [pltpu.HBM(whole, bf16), pltpu.VMEM(whole, bf16)],
        [in_vmem(base), hidden_kept, onehot],
        2 * tok_rows * slab * rows,
        2 * dense,
        8 * MIB,
        scratch=[pltpu.SemaphoreType.DMA((blocks,))],
        far_outs=(0,),
    )
    (normed,) = call(
        functools.partial(norm_kernel, float(slab * chan_devices), len(parts)),
        [pltpu.HBM(whole, bf16)],
        parts + [in_vmem(held), gain_row],
        4 * tok_rows * slab,
        2 * dense,
        16 * MIB,
        scratch=[
            pltpu.VMEM(whole, bf16),
            pltpu.VMEM((LANES, LANES), f32),
            pltpu.SemaphoreType.DMA((blocks,)),
        ],
        far_outs=(0,),
    )
    return (hidden, normed)


def solution(mesh):
    positions = P(("seqo", "seqi"), "chan")
    in_specs = (
        positions,
        positions,
        positions,
        positions,
        P("chan", ("seqo", "seqi"), None, None),
        P("chan", None),
        P("chan", None),
        P("chan"),
        P("chan"),
    )
    return jax.shard_map(
        local, mesh=mesh, in_specs=in_specs, out_specs=(positions, positions), check_vma=False
    )
```

```python
import functools

import jax
import jax.numpy as jnp
import numpy as np
from jax import lax
from jax.experimental import pallas as pl
from jax.experimental.pallas import tpu as pltpu
from jax.sharding import PartitionSpec as P

LANES = 128
TILE = 256
CHUNK = 16
AHEAD = 3
HALVES = 2
MIB = 1 << 20
norm_eps = 1e-06
f32 = jnp.float32
bf16 = jnp.bfloat16


def split_np(table):
    high = table.astype(jnp.bfloat16)
    low = (table - high.astype(np.float64)).astype(jnp.bfloat16)
    return high, low


def dft_tables(length):
    inner = LANES
    outer = length // inner
    a = np.arange(outer)
    b = np.arange(inner)
    quarter = np.arange(outer) + 0.25
    outer_angle = 2 * np.pi / outer * np.mod(quarter[:, None] * a[None, :], outer)
    turn_angle = 2 * np.pi / length * (quarter[:, None] * b[None, :])
    inner_angle = 2 * np.pi / inner * np.mod(b[:, None] * b[None, :], inner)
    outer_fwd = np.concatenate([np.cos(outer_angle), -np.sin(outer_angle)], axis=0)
    c, s = np.cos(inner_angle), np.sin(inner_angle)
    inner_fwd = np.concatenate(
        [np.concatenate([c, -s], axis=1), np.concatenate([s, c], axis=1)], axis=0
    )
    inner_back = np.concatenate(
        [np.concatenate([c, s], axis=1), np.concatenate([-s, c], axis=1)], axis=0
    )
    outer_back = np.concatenate([np.cos(outer_angle).T, -np.sin(outer_angle).T], axis=1) / length
    turn = np.concatenate([np.cos(turn_angle), np.sin(turn_angle)], axis=1).astype(np.float32)
    outer_fwd = np.concatenate(split_np(outer_fwd), axis=1)
    inner = np.concatenate(split_np(inner_fwd) + split_np(inner_back), axis=0)
    outer_back = np.concatenate(split_np(outer_back), axis=1)
    return outer_fwd, turn, inner, outer_back


def split(value):
    high = value.astype(bf16)
    low = (value - high.astype(f32)).astype(bf16)
    return high, low


def dot(x, y):
    return jnp.dot(x, y, preferred_element_type=f32)


def dot_rows(x, y):
    return lax.dot_general(x, y, (((0,), (0,)), ((), ())), preferred_element_type=f32)


def times_table(value, table):
    high, low = split(value)
    depth = value.shape[1]
    stacked = jnp.concatenate([table, table[:depth]], axis=0)
    return dot(jnp.concatenate([high, high, low], axis=1), stacked)


def table_times(table, value):
    high, low = split(value)
    depth = value.shape[0]
    stacked = jnp.concatenate([table, table[:, :depth]], axis=1)
    return dot(stacked, jnp.concatenate([high, high, low], axis=0))


def to_spectrum(blocks, slots, outer_fwd, turn, inner_fwd):
    outer = blocks.shape[0]
    first = dot(outer_fwd, jnp.concatenate([blocks, blocks], axis=0))
    turn, inner_fwd = turn(), inner_fwd()
    cos, sin = turn[:, :LANES], turn[:, LANES:]
    result = []
    for s in range(slots):
        re = first[:outer, s * LANES : (s + 1) * LANES]
        im = first[outer:, s * LANES : (s + 1) * LANES]
        turned = jnp.concatenate([re * cos + im * sin, im * cos - re * sin], axis=1)
        result.append(times_table(turned, inner_fwd))
    return result


def filter_kernel(filters, outer_fwd, turn, inner, spectra):
    slots, length = filters.shape
    outer = length // LANES
    wide = filters[...].astype(f32)
    blocks = [wide[s].reshape(outer, LANES) for s in range(slots)]
    blocks = jnp.concatenate(blocks, axis=1).astype(bf16)
    parts = to_spectrum(
        blocks, slots, outer_fwd[...], lambda: turn[...], lambda: inner[: 4 * LANES, :]
    )
    for s in range(slots):
        spectra[s] = parts[s]


def convolve_kernel(
    signals_far, outer_fwd_far, turn_far, inner_far, spectra_far, outer_back_far, out, *scratch
):
    sources = (signals_far, outer_fwd_far, turn_far, inner_far, spectra_far, outer_back_far)
    signals, outer_fwd, turn_ref, inner, spectra, outer_back, sems = scratch
    copies = [
        pltpu.make_async_copy(source, scratch[n], sems.at[n]) for n, source in enumerate(sources)
    ]
    for copy in copies[:4]:
        copy.start()
    slots, outer = spectra.shape[:2]

    def turn_now():
        copies[2].wait()
        return turn_ref[...]

    def inner_now():
        copies[3].wait()
        return inner[: 4 * LANES, :]

    copies[0].wait()
    copies[1].wait()
    for copy in copies[4:]:
        copy.start()
    blocks = signals[...].reshape(outer, slots * LANES)
    parts = to_spectrum(blocks, slots, outer_fwd[...], turn_now, inner_now)
    turn = turn_ref[...]
    cos, sin = turn[:, :LANES], turn[:, LANES:]
    copies[4].wait()
    turned = []
    for s in range(slots):
        sig_re, sig_im = parts[s][:, :LANES], parts[s][:, LANES:]
        ker_re, ker_im = spectra[s, :, :LANES], spectra[s, :, LANES:]
        joint = jnp.concatenate(
            [sig_re * ker_re - sig_im * ker_im, sig_re * ker_im + sig_im * ker_re], axis=1
        )
        back = times_table(joint, inner[4 * LANES :, :])
        re, im = back[:, :LANES], back[:, LANES:]
        turned.append(jnp.concatenate([re * cos - im * sin, im * cos + re * sin], axis=0))
    copies[5].wait()
    for s in range(0, slots, 2):
        pair = turned[s : s + 2]
        causal = table_times(outer_back[...], jnp.concatenate(pair, axis=1)).astype(bf16)
        lanes = slice(s * LANES, (s + len(pair)) * LANES)
        out[:, :, lanes] = causal.reshape(out.shape[:2] + (len(pair) * LANES,))


def iota(shape, axis):
    return lax.broadcasted_iota(jnp.int32, shape, axis)


def to_column(row):
    size = row.shape[1]
    same = iota((size, size), 0) == iota((size, size), 1)
    return jnp.sum(jnp.where(same, row, 0), axis=1, keepdims=True)


def channel_of_row(index_row, owners_row, owner_count, rows):
    slots = owners_row.shape[1]
    owners_col = to_column(owners_row)
    index_col = to_column(index_row)
    earlier = (owners_col == owners_row) & (iota((slots, slots), 1) < iota((slots, slots), 0))
    rank_col = jnp.sum(earlier.astype(jnp.int32), axis=1, keepdims=True)
    target_col = jnp.where(owners_col >= 0, rank_col * owner_count + owners_col, -1)
    hit = target_col == iota((slots, rows), 1)
    return jnp.sum(jnp.where(hit, index_col + 1, 0), axis=0, keepdims=True) - 1


def pick_rows(tile, onehot_t, rows):
    picked = dot(tile, onehot_t).T
    return [picked[:rows, i : i + LANES] for i in range(0, tile.shape[0], LANES)]


def fetch(sources, stages, sems, tile, first=0):
    count = stages[0].shape[0] // tile

    def copies(i):
        at = pl.multiple_of(i * tile, tile)
        return [
            pltpu.make_async_copy(
                source.at[pl.ds(first + at, tile), :], stage.at[pl.ds(at, tile), :], sems.at[n, i]
            )
            for n, (source, stage) in enumerate(zip(sources, stages))
        ]

    def start(i):
        for copy in copies(i):
            copy.start()

    for i in range(min(AHEAD, count)):
        start(i)

    def wait(i):
        for copy in copies(i):
            copy.wait()

        @pl.when(i + AHEAD < count)
        def _():
            start(i + AHEAD)

        return pl.multiple_of(i * tile, tile)

    return wait, count


def pick_kernel(owner_count, slots, index, owners, gate, value, *refs):
    payload, picked, channels, onehot_t = refs[:4]
    acc, gate_stage, value_stage, lists, list_sems, sems = refs[4:]
    rows = owner_count * slots
    tile = gate_stage.shape[0] // sems.shape[1]
    list_copies = [
        pltpu.make_async_copy(source, lists.at[n], list_sems.at[n])
        for n, source in enumerate((index, owners))
    ]
    for copy in list_copies:
        copy.start()
    wait, count = fetch((gate, value), (gate_stage, value_stage), sems, tile)
    for copy in list_copies:
        copy.wait()
    row = channel_of_row(lists[0], lists[1], owner_count, onehot_t.shape[1])
    channels[...] = jnp.broadcast_to(row, channels.shape)
    onehot_t[...] = (iota(onehot_t.shape, 0) == row).astype(f32).astype(bf16)

    def step(i, _):
        at = pl.ds(wait(i), tile)
        gated = gate_stage[at, :] * value_stage[at, :]
        for n, block in enumerate(pick_rows(gated, onehot_t[...], rows)):
            acc[i * (tile // LANES) + n] = block
            picked[i * (tile // LANES) + n] = block.astype(bf16)
        return 0

    lax.fori_loop(0, count, step, 0)
    for s in range(slots):
        part = jnp.swapaxes(acc[:, s * owner_count : (s + 1) * owner_count, :], 0, 1)
        payload[:, :, s * LANES : (s + 1) * LANES] = part.astype(bf16)


def place_kernel(channels, skip, onehot, others, skip_wide):
    hit = iota(onehot.shape, 1) == to_column(channels[0:1, :])[: onehot.shape[0]]
    onehot[...] = hit.astype(f32).astype(bf16)
    others[...] = jnp.broadcast_to(1.0 - jnp.max(hit.astype(f32), axis=0, keepdims=True), others.shape)
    skip_col = jnp.sum(jnp.where(hit, skip[...], 0.0), axis=1, keepdims=True)
    skip_wide[...] = jnp.broadcast_to(skip_col, skip_wide.shape)


def base_kernel(first, onehot_t, others, skip, gate, value, out_gate, residual, *refs):
    base, sums, picked_gate, picked_res = refs[-12:-8]
    stages = refs[-8:-4]
    base_stage, partial, base_sems, sems = refs[-4:]
    gate_stage, value_stage, out_stage, res_stage = stages
    rows = picked_gate.shape[1]
    slab = gate_stage.shape[1]
    tile = partial.shape[0]
    wait, count = fetch((gate, value, out_gate, residual), stages, sems, tile, first)

    def copy(i):
        at = pl.multiple_of(i * tile, tile)
        return pltpu.make_async_copy(
            base_stage.at[pl.ds(at, tile), :], base.at[pl.ds(first + at, tile), :], base_sems.at[i]
        )

    def step(i, _):
        start = wait(i)
        for c in range(0, tile, CHUNK):
            at = pl.ds(start + c, CHUNK)
            total = jnp.zeros((CHUNK, LANES), f32)
            for j in range(0, slab, LANES):
                lanes = slice(j, j + LANES)
                gated = (gate_stage[at, lanes] * value_stage[at, lanes]).astype(f32)
                mixed = out_stage[at, lanes].astype(f32) * (skip[:, lanes] * gated)
                hidden = (res_stage[at, lanes].astype(f32) + mixed) * others[0:1, lanes]
                hidden = hidden.astype(bf16)
                base_stage[at, lanes] = hidden
                hidden = hidden.astype(f32)
                total = total + hidden * hidden
            partial[c : c + CHUNK, :] = total
        copy(i).start()
        total = jnp.sum(partial[...].T, axis=0, keepdims=True)
        at = pl.ds(start, tile)
        picks_gate = pick_rows(out_stage[at, :], onehot_t[...], rows)
        picks_res = pick_rows(res_stage[at, :], onehot_t[...], rows)
        for n in range(tile // LANES):
            block = i * (tile // LANES) + n
            sums[block] = total[:, n * LANES : (n + 1) * LANES]
            picked_gate[block] = picks_gate[n].astype(bf16)
            picked_res[block] = picks_res[n].astype(bf16)
        return 0

    lax.fori_loop(0, count, step, 0)
    lax.fori_loop(0, count, lambda i, _: (copy(i).wait(), 0)[1], 0)


def kept_kernel(halves, conv, picked, skip_wide, *refs):
    hidden, totals = refs[-2:]
    owner_count, blocks = conv.shape[:2]
    size = blocks // halves
    for h in range(halves):
        sums, picked_gate, picked_res = refs[3 * h : 3 * h + 3]
        at_h = slice(h * size, (h + 1) * size)
        total = jnp.zeros((size, LANES), f32)
        for s in range(conv.shape[2] // LANES):
            at = slice(s * owner_count, (s + 1) * owner_count)
            conv_rows = conv[:, at_h, s * LANES : (s + 1) * LANES].astype(f32)
            conv_rows = jnp.swapaxes(conv_rows, 0, 1)
            wide = conv_rows + skip_wide[at, :] * picked[at_h, at, :].astype(f32)
            value = picked_res[:, at, :].astype(f32) + picked_gate[:, at, :].astype(f32) * wide
            value = value.astype(bf16)
            hidden[at_h, at, :] = value
            value = value.astype(f32)
            total = total + jnp.sum(value * value, axis=1)
        for i in range(size):
            totals[h * size + i] = total[i : i + 1, :] + sums[i]


def hidden_kernel(base, hidden_kept, onehot, hidden, held, base_stage, base_sems, sems):
    slab = held.shape[1]
    wide = min(slab, 2 * LANES)
    wait, count = fetch((base,), (base_stage,), base_sems, LANES)

    def copy(i):
        rows = pl.ds(pl.multiple_of(i * LANES, LANES), LANES)
        return pltpu.make_async_copy(held.at[rows, :], hidden.at[rows, :], sems.at[i])

    def step(i, _):
        kept = hidden_kept[i].astype(f32).T.astype(bf16)
        rows = pl.ds(wait(i), LANES)
        for j in range(0, slab, wide):
            lanes = slice(j, j + wide)
            placed = dot(kept, onehot[:, lanes]).astype(bf16)
            held[rows, lanes] = base_stage[rows, lanes] + placed
        copy(i).start()
        return 0

    lax.fori_loop(0, count, step, 0)
    lax.fori_loop(0, count, lambda i, _: (copy(i).wait(), 0)[1], 0)


def norm_kernel(width, count, *refs):
    parts = refs[:count]
    held, gain, normed, stage, turned, sems = refs[count:]
    slab = held.shape[1]

    def copy(i):
        rows = pl.ds(pl.multiple_of(i * LANES, LANES), LANES)
        return pltpu.make_async_copy(stage.at[rows, :], normed.at[rows, :], sems.at[i])

    def step(i, _):
        total = parts[0][i]
        for part in parts[1:]:
            total = total + part[i]
        scale = lax.rsqrt(total / width + norm_eps)
        turned[...] = jnp.broadcast_to(scale, (LANES, LANES)).T
        first = pl.multiple_of(i * LANES, LANES)
        for c in range(0, LANES, CHUNK):
            at = pl.ds(first + c, CHUNK)
            scales = turned[c : c + CHUNK, :]
            for j in range(0, slab, LANES):
                lanes = slice(j, j + LANES)
                value = held[at, lanes].astype(f32) * scales * gain[:, lanes]
                stage[at, lanes] = value.astype(bf16)
        copy(i).start()
        return 0

    lax.fori_loop(0, sems.shape[0], step, 0)
    lax.fori_loop(0, sems.shape[0], lambda i, _: (copy(i).wait(), 0)[1], 0)


def in_hbm(x):
    return pltpu.with_memory_space_constraint(x, pltpu.HBM)


def in_vmem(x):
    return pltpu.with_memory_space_constraint(x, pltpu.VMEM)


def call(kernel, outs, ins, flops, moved, limit, scratch=(), far=(), far_outs=(), alias=None):
    near = pl.BlockSpec(memory_space=pltpu.VMEM)
    away = pl.BlockSpec(memory_space=pl.ANY)
    return pl.pallas_call(
        kernel,
        out_shape=outs,
        in_specs=[away if n in far else near for n in range(len(ins))],
        out_specs=[away if n in far_outs else near for n in range(len(outs))],
        scratch_shapes=list(scratch),
        input_output_aliases=alias or {},
        compiler_params=pltpu.CompilerParams(vmem_limit_bytes=limit),
        cost_estimate=pl.CostEstimate(flops=flops, bytes_accessed=moved, transcendentals=0),
    )(*ins)


def local(
    gate_in, value_in, out_gate, residual, filters, kept_index, kept_owner, skip_bias, norm_gain
):
    tok_rows, slab = gate_in.shape
    slots, length = filters.shape[2:]
    chan_devices = lax.axis_size("chan")
    owner_count = lax.axis_size("seqo") * lax.axis_size("seqi")
    rows = slots * owner_count
    lanes_rows = -(-rows // LANES) * LANES
    blocks = tok_rows // LANES
    outer = length // LANES
    tile = TILE if tok_rows % TILE == 0 else LANES
    dense = tok_rows * slab * 2
    sds = jax.ShapeDtypeStruct
    tables = [in_hbm(jnp.asarray(x)) for x in dft_tables(length)]
    outer_fwd, turn, inner, outer_back = tables
    skip_row = skip_bias[None, :]
    gain_row = norm_gain[None, :]
    gate_in, value_in, out_gate, residual = map(in_hbm, (gate_in, value_in, out_gate, residual))
    picks = sds((blocks, rows, LANES), bf16)
    row_sums = sds((blocks, 1, LANES), f32)
    buffer = (owner_count, blocks, slots * LANES)
    whole = (tok_rows, slab)

    payload, picked, channels, onehot_t = call(
        functools.partial(pick_kernel, owner_count, slots),
        [sds(buffer, bf16), picks, sds((8, lanes_rows), jnp.int32), sds((slab, lanes_rows), bf16)],
        [in_hbm(kept_index), in_hbm(kept_owner), gate_in, value_in],
        2 * tok_rows * slab * rows,
        2 * dense,
        24 * MIB,
        scratch=[
            pltpu.VMEM((blocks, rows, LANES), f32),
            pltpu.VMEM(whole, bf16),
            pltpu.VMEM(whole, bf16),
            pltpu.VMEM((2,) + kept_index.shape, jnp.int32),
            pltpu.SemaphoreType.DMA((2,)),
            pltpu.SemaphoreType.DMA((2, tok_rows // tile)),
        ],
        far=(0, 1, 2, 3),
    )

    incoming = lax.all_to_all(payload, ("seqo", "seqi"), split_axis=0, concat_axis=0, tiled=True)

    (spectra,) = call(
        filter_kernel,
        [sds((slots, outer, 2 * LANES), f32)],
        [filters[0, 0]] + [jnp.asarray(x) for x in dft_tables(length)[:3]],
        2 * slots * length * 2 * (2 * outer + 6 * LANES),
        8 * MIB,
        16 * MIB,
    )
    onehot, others, skip_wide = call(
        place_kernel,
        [sds((rows, slab), bf16), sds((8, slab), f32), sds((rows, LANES), f32)],
        [channels, skip_row],
        rows * slab * 8,
        rows * slab * 2,
        8 * MIB,
    )

    def base_half(h, onehot_t, base):
        part = tok_rows // HALVES
        count = part // LANES
        ins = [onehot_t, others, skip_row, gate_in, value_in, out_gate, residual]
        outs = [
            pltpu.HBM(whole, bf16),
            sds((count, 1, LANES), f32),
            sds((count, rows, LANES), bf16),
            sds((count, rows, LANES), bf16),
        ]
        if base is not None:
            ins.append(base)
        return call(
            functools.partial(base_kernel, h * part),
            outs,
            ins,
            4 * tok_rows * slab * rows // HALVES,
            5 * dense // HALVES,
            24 * MIB,
            scratch=[pltpu.VMEM((part, slab), bf16)] * 5
            + [
                pltpu.VMEM((LANES, LANES), f32),
                pltpu.SemaphoreType.DMA((count,)),
                pltpu.SemaphoreType.DMA((4, count)),
            ],
            far=(3, 4, 5, 6, 7),
            far_outs=(0,),
            alias={} if base is None else {7: 0},
        )

    base, *half_picks = base_half(0, onehot_t, None)
    spectra, base = lax.optimization_barrier((spectra, base))

    conv_ins = [in_hbm(incoming), outer_fwd, turn, inner, in_hbm(spectra), outer_back]
    (convolved,) = call(
        convolve_kernel,
        [sds(buffer, bf16)],
        conv_ins,
        2 * slots * length * 2 * (5 * outer + 12 * LANES),
        8 * MIB,
        20 * MIB,
        scratch=[pltpu.VMEM(x.shape, x.dtype) for x in conv_ins]
        + [pltpu.SemaphoreType.DMA((len(conv_ins),))],
        far=tuple(range(len(conv_ins))),
    )
    convolved, onehot_t = lax.optimization_barrier((convolved, onehot_t))

    returned = lax.all_to_all(convolved, ("seqo", "seqi"), split_axis=0, concat_axis=0, tiled=True)

    base, *more_picks = base_half(1, onehot_t, base)

    hidden_kept, totals = call(
        functools.partial(kept_kernel, HALVES),
        [picks, row_sums],
        [returned, picked, skip_wide, *half_picks, *more_picks],
        8 * rows * tok_rows,
        10 * rows * tok_rows,
        16 * MIB,
    )

    parts = [totals]
    for shift in range(1, chan_devices):
        ring = [(i, (i + shift) % chan_devices) for i in range(chan_devices)]
        parts.append(lax.ppermute(totals, "chan", ring))

    hidden, held = call(
        hidden_kernel,
        [pltpu.HBM(whole, bf16), pltpu.VMEM(whole, bf16)],
        [in_hbm(base), hidden_kept, onehot],
        2 * tok_rows * slab * rows,
        2 * dense,
        16 * MIB,
        scratch=[
            pltpu.VMEM(whole, bf16),
            pltpu.SemaphoreType.DMA((1, blocks)),
            pltpu.SemaphoreType.DMA((blocks,)),
        ],
        far=(0,),
        far_outs=(0,),
    )
    (normed,) = call(
        functools.partial(norm_kernel, float(slab * chan_devices), len(parts)),
        [pltpu.HBM(whole, bf16)],
        parts + [in_vmem(held), gain_row],
        4 * tok_rows * slab,
        2 * dense,
        16 * MIB,
        scratch=[
            pltpu.VMEM(whole, bf16),
            pltpu.VMEM((LANES, LANES), f32),
            pltpu.SemaphoreType.DMA((blocks,)),
        ],
        far_outs=(0,),
    )
    return (hidden, normed)


def solution(mesh):
    positions = P(("seqo", "seqi"), "chan")
    in_specs = (
        positions,
        positions,
        positions,
        positions,
        P("chan", ("seqo", "seqi"), None, None),
        P("chan", None),
        P("chan", None),
        P("chan"),
        P("chan"),
    )
    return jax.shard_map(
        local, mesh=mesh, in_specs=in_specs, out_specs=(positions, positions), check_vma=False
    )
```

```python
import functools

import jax
import jax.numpy as jnp
import numpy as np
from jax import lax
from jax.experimental import pallas as pl
from jax.experimental.pallas import tpu as pltpu
from jax.sharding import PartitionSpec as P

LANES = 128
TILE = 256
CHUNK = 16
AHEAD = 3
EARLY = 7
MIB = 1 << 20
norm_eps = 1e-06
f32 = jnp.float32
bf16 = jnp.bfloat16


def split_np(table):
    high = table.astype(jnp.bfloat16)
    low = (table - high.astype(np.float64)).astype(jnp.bfloat16)
    return high, low


def dft_tables(length):
    inner = LANES
    outer = length // inner
    a = np.arange(outer)
    b = np.arange(inner)
    quarter = np.arange(outer) + 0.25
    outer_angle = 2 * np.pi / outer * np.mod(quarter[:, None] * a[None, :], outer)
    turn_angle = 2 * np.pi / length * (quarter[:, None] * b[None, :])
    inner_angle = 2 * np.pi / inner * np.mod(b[:, None] * b[None, :], inner)
    outer_fwd = np.concatenate([np.cos(outer_angle), -np.sin(outer_angle)], axis=0)
    c, s = np.cos(inner_angle), np.sin(inner_angle)
    inner_fwd = np.concatenate(
        [np.concatenate([c, -s], axis=1), np.concatenate([s, c], axis=1)], axis=0
    )
    inner_back = np.concatenate(
        [np.concatenate([c, s], axis=1), np.concatenate([-s, c], axis=1)], axis=0
    )
    outer_back = np.concatenate([np.cos(outer_angle).T, -np.sin(outer_angle).T], axis=1) / length
    turn = np.concatenate([np.cos(turn_angle), np.sin(turn_angle)], axis=1).astype(np.float32)
    outer_fwd = np.concatenate(split_np(outer_fwd), axis=1)
    inner = np.concatenate(split_np(inner_fwd) + split_np(inner_back), axis=0)
    outer_back = np.concatenate(split_np(outer_back), axis=1)
    return outer_fwd, turn, inner, outer_back


def split(value):
    high = value.astype(bf16)
    low = (value - high.astype(f32)).astype(bf16)
    return high, low


def dot(x, y):
    return jnp.dot(x, y, preferred_element_type=f32)


def dot_rows(x, y):
    return lax.dot_general(x, y, (((0,), (0,)), ((), ())), preferred_element_type=f32)


def times_table(value, table):
    high, low = split(value)
    depth = value.shape[1]
    stacked = jnp.concatenate([table, table[:depth]], axis=0)
    return dot(jnp.concatenate([high, high, low], axis=1), stacked)


def table_times(table, value):
    high, low = split(value)
    depth = value.shape[0]
    stacked = jnp.concatenate([table, table[:, :depth]], axis=1)
    return dot(stacked, jnp.concatenate([high, high, low], axis=0))


def to_spectrum(blocks, slots, outer_fwd, turn, inner_fwd):
    outer = blocks.shape[0]
    first = dot(outer_fwd, jnp.concatenate([blocks, blocks], axis=0))
    turn, inner_fwd = turn(), inner_fwd()
    cos, sin = turn[:, :LANES], turn[:, LANES:]
    result = []
    for s in range(slots):
        re = first[:outer, s * LANES : (s + 1) * LANES]
        im = first[outer:, s * LANES : (s + 1) * LANES]
        turned = jnp.concatenate([re * cos + im * sin, im * cos - re * sin], axis=1)
        result.append(times_table(turned, inner_fwd))
    return result


def filter_kernel(filters, outer_fwd, turn, inner, spectra):
    slots, length = filters.shape
    outer = length // LANES
    wide = filters[...].astype(f32)
    blocks = [wide[s].reshape(outer, LANES) for s in range(slots)]
    blocks = jnp.concatenate(blocks, axis=1).astype(bf16)
    parts = to_spectrum(
        blocks, slots, outer_fwd[...], lambda: turn[...], lambda: inner[: 4 * LANES, :]
    )
    for s in range(slots):
        spectra[s] = parts[s]


def convolve_kernel(
    signals, outer_fwd_far, turn_far, inner_far, spectra_far, outer_back_far, out, *scratch
):
    sources = (outer_fwd_far, turn_far, inner_far, spectra_far, outer_back_far)
    outer_fwd, turn_ref, inner, spectra, outer_back, sems = scratch
    copies = [
        pltpu.make_async_copy(source, scratch[n], sems.at[n]) for n, source in enumerate(sources)
    ]
    for copy in copies[:3]:
        copy.start()
    slots, outer = spectra.shape[:2]

    def turn_now():
        copies[1].wait()
        return turn_ref[...]

    def inner_now():
        copies[2].wait()
        return inner[: 4 * LANES, :]

    copies[0].wait()
    for copy in copies[3:]:
        copy.start()
    blocks = signals[...].reshape(outer, slots * LANES)
    parts = to_spectrum(blocks, slots, outer_fwd[...], turn_now, inner_now)
    turn = turn_ref[...]
    cos, sin = turn[:, :LANES], turn[:, LANES:]
    copies[3].wait()
    turned = []
    for s in range(slots):
        sig_re, sig_im = parts[s][:, :LANES], parts[s][:, LANES:]
        ker_re, ker_im = spectra[s, :, :LANES], spectra[s, :, LANES:]
        joint = jnp.concatenate(
            [sig_re * ker_re - sig_im * ker_im, sig_re * ker_im + sig_im * ker_re], axis=1
        )
        back = times_table(joint, inner[4 * LANES :, :])
        re, im = back[:, :LANES], back[:, LANES:]
        turned.append(jnp.concatenate([re * cos - im * sin, im * cos + re * sin], axis=0))
    copies[4].wait()
    for s in range(0, slots, 2):
        pair = turned[s : s + 2]
        causal = table_times(outer_back[...], jnp.concatenate(pair, axis=1)).astype(bf16)
        lanes = slice(s * LANES, (s + len(pair)) * LANES)
        out[:, :, lanes] = causal.reshape(out.shape[:2] + (len(pair) * LANES,))


def iota(shape, axis):
    return lax.broadcasted_iota(jnp.int32, shape, axis)


def to_column(row):
    size = row.shape[1]
    same = iota((size, size), 0) == iota((size, size), 1)
    return jnp.sum(jnp.where(same, row, 0), axis=1, keepdims=True)


def channel_of_row(index_row, owners_row, owner_count, rows):
    slots = owners_row.shape[1]
    owners_col = to_column(owners_row)
    index_col = to_column(index_row)
    earlier = (owners_col == owners_row) & (iota((slots, slots), 1) < iota((slots, slots), 0))
    rank_col = jnp.sum(earlier.astype(jnp.int32), axis=1, keepdims=True)
    target_col = jnp.where(owners_col >= 0, rank_col * owner_count + owners_col, -1)
    hit = target_col == iota((slots, rows), 1)
    return jnp.sum(jnp.where(hit, index_col + 1, 0), axis=0, keepdims=True) - 1


def pick_rows(tile, onehot_t, rows):
    picked = dot(tile, onehot_t).T
    return [picked[:rows, i : i + LANES] for i in range(0, tile.shape[0], LANES)]


def fetch(sources, stages, sems, tile, first=0):
    count = stages[0].shape[0] // tile

    def copies(i):
        at = pl.multiple_of(i * tile, tile)
        return [
            pltpu.make_async_copy(
                source.at[pl.ds(first + at, tile), :], stage.at[pl.ds(at, tile), :], sems.at[n, i]
            )
            for n, (source, stage) in enumerate(zip(sources, stages))
        ]

    def start(i):
        for copy in copies(i):
            copy.start()

    for i in range(min(AHEAD, count)):
        start(i)

    def wait(i):
        for copy in copies(i):
            copy.wait()

        @pl.when(i + AHEAD < count)
        def _():
            start(i + AHEAD)

        return pl.multiple_of(i * tile, tile)

    return wait, count


def pick_kernel(owner_count, slots, index, owners, gate, value, *refs):
    payload, channels, onehot_far = refs[:3]
    acc, gate_stage, value_stage, onehot_t, lists, list_sems, sems = refs[3:]
    rows = owner_count * slots
    tile = gate_stage.shape[0] // sems.shape[1]
    list_copies = [
        pltpu.make_async_copy(source, lists.at[n], list_sems.at[n])
        for n, source in enumerate((index, owners))
    ]
    for copy in list_copies:
        copy.start()
    wait, count = fetch((gate, value), (gate_stage, value_stage), sems, tile)
    for copy in list_copies:
        copy.wait()
    row = channel_of_row(lists[0], lists[1], owner_count, onehot_t.shape[1])
    channels[...] = jnp.broadcast_to(row, channels.shape)
    onehot_t[...] = (iota(onehot_t.shape, 0) == row).astype(f32).astype(bf16)
    onehot_copy = pltpu.make_async_copy(onehot_t, onehot_far, list_sems.at[2])
    onehot_copy.start()

    def step(i, _):
        at = pl.ds(wait(i), tile)
        gated = gate_stage[at, :] * value_stage[at, :]
        for n, block in enumerate(pick_rows(gated, onehot_t[...], rows)):
            acc[i * (tile // LANES) + n] = block
        return 0

    lax.fori_loop(0, count, step, 0)
    for s in range(slots):
        part = jnp.swapaxes(acc[:, s * owner_count : (s + 1) * owner_count, :], 0, 1)
        payload[:, :, s * LANES : (s + 1) * LANES] = part.astype(bf16)
    onehot_copy.wait()


def place_kernel(channels, skip, onehot, others, skip_wide):
    hit = iota(onehot.shape, 1) == to_column(channels[0:1, :])[: onehot.shape[0]]
    onehot[...] = hit.astype(f32).astype(bf16)
    others[...] = jnp.broadcast_to(1.0 - jnp.max(hit.astype(f32), axis=0, keepdims=True), others.shape)
    skip_col = jnp.sum(jnp.where(hit, skip[...], 0.0), axis=1, keepdims=True)
    skip_wide[...] = jnp.broadcast_to(skip_col, skip_wide.shape)


def base_kernel(first, onehot_t, others, skip, gate, value, out_gate, residual, *refs):
    base, sums, picked_gate, picked_res = refs[-12:-8]
    stages = refs[-8:-4]
    base_stage, partial, base_sems, sems = refs[-4:]
    gate_stage, value_stage, out_stage, res_stage = stages
    rows = picked_gate.shape[1]
    slab = gate_stage.shape[1]
    tile = partial.shape[0]
    wait, count = fetch((gate, value, out_gate, residual), stages, sems, tile, first)

    def copy(i):
        at = pl.multiple_of(i * tile, tile)
        return pltpu.make_async_copy(
            base_stage.at[pl.ds(at, tile), :], base.at[pl.ds(first + at, tile), :], base_sems.at[i]
        )

    def step(i, _):
        start = wait(i)
        for c in range(0, tile, CHUNK):
            at = pl.ds(start + c, CHUNK)
            total = jnp.zeros((CHUNK, LANES), f32)
            for j in range(0, slab, LANES):
                lanes = slice(j, j + LANES)
                gated = (gate_stage[at, lanes] * value_stage[at, lanes]).astype(f32)
                mixed = out_stage[at, lanes].astype(f32) * (skip[:, lanes] * gated)
                hidden = (res_stage[at, lanes].astype(f32) + mixed) * others[0:1, lanes]
                hidden = hidden.astype(bf16)
                base_stage[at, lanes] = hidden
                hidden = hidden.astype(f32)
                total = total + hidden * hidden
            partial[c : c + CHUNK, :] = total
        copy(i).start()
        total = jnp.sum(partial[...].T, axis=0, keepdims=True)
        at = pl.ds(start, tile)
        picks_gate = pick_rows(out_stage[at, :], onehot_t[...], rows)
        picks_res = pick_rows(res_stage[at, :], onehot_t[...], rows)
        for n in range(tile // LANES):
            block = i * (tile // LANES) + n
            sums[block] = total[:, n * LANES : (n + 1) * LANES]
            picked_gate[block] = picks_gate[n].astype(bf16)
            picked_res[block] = picks_res[n].astype(bf16)
        return 0

    lax.fori_loop(0, count, step, 0)
    lax.fori_loop(0, count, lambda i, _: (copy(i).wait(), 0)[1], 0)


def kept_kernel(conv, payload, skip_wide, *refs):
    hidden, totals = refs[-2:]
    owner_count, blocks = conv.shape[:2]
    first = 0
    for n in range(0, len(refs) - 2, 3):
        sums, picked_gate, picked_res = refs[n : n + 3]
        size = sums.shape[0]
        at_h = slice(first, first + size)
        total = jnp.zeros((size, LANES), f32)
        for s in range(conv.shape[2] // LANES):
            at = slice(s * owner_count, (s + 1) * owner_count)
            lanes = slice(s * LANES, (s + 1) * LANES)
            gated = jnp.swapaxes(payload[:, at_h, lanes].astype(f32), 0, 1)
            wide = jnp.swapaxes(conv[:, at_h, lanes].astype(f32), 0, 1)
            wide = wide + skip_wide[at, :] * gated
            value = picked_res[:, at, :].astype(f32) + picked_gate[:, at, :].astype(f32) * wide
            value = value.astype(bf16)
            hidden[at_h, at, :] = value
            value = value.astype(f32)
            total = total + jnp.sum(value * value, axis=1)
        for i in range(size):
            totals[first + i] = total[i : i + 1, :] + sums[i]
        first = first + size


def hidden_kernel(base, hidden_kept, onehot, hidden, held, base_stage, base_sems, sems):
    slab = held.shape[1]
    wide = min(slab, 2 * LANES)
    count = sems.shape[0]
    tile = held.shape[0] // count
    wait, _ = fetch((base,), (base_stage,), base_sems, tile)

    def copy(i):
        rows = pl.ds(pl.multiple_of(i * tile, tile), tile)
        return pltpu.make_async_copy(held.at[rows, :], hidden.at[rows, :], sems.at[i])

    def step(i, _):
        blocks = range(tile // LANES)
        kept = [hidden_kept[i * (tile // LANES) + n].astype(f32).T.astype(bf16) for n in blocks]
        kept = jnp.concatenate(kept, axis=0)
        rows = pl.ds(wait(i), tile)
        for j in range(0, slab, wide):
            lanes = slice(j, j + wide)
            placed = dot(kept, onehot[:, lanes]).astype(bf16)
            held[rows, lanes] = base_stage[rows, lanes] + placed
        copy(i).start()
        return 0

    lax.fori_loop(0, count, step, 0)
    lax.fori_loop(0, count, lambda i, _: (copy(i).wait(), 0)[1], 0)


def norm_kernel(width, count, *refs):
    parts = refs[:count]
    held, gain, normed, stage, turned, sems = refs[count:]
    slab = held.shape[1]

    def copy(i):
        rows = pl.ds(pl.multiple_of(i * LANES, LANES), LANES)
        return pltpu.make_async_copy(stage.at[rows, :], normed.at[rows, :], sems.at[i])

    def step(i, _):
        total = parts[0][i]
        for part in parts[1:]:
            total = total + part[i]
        scale = lax.rsqrt(total / width + norm_eps)
        turned[...] = jnp.broadcast_to(scale, (LANES, LANES)).T
        first = pl.multiple_of(i * LANES, LANES)
        for c in range(0, LANES, CHUNK):
            at = pl.ds(first + c, CHUNK)
            scales = turned[c : c + CHUNK, :]
            for j in range(0, slab, LANES):
                lanes = slice(j, j + LANES)
                value = held[at, lanes].astype(f32) * scales * gain[:, lanes]
                stage[at, lanes] = value.astype(bf16)
        copy(i).start()
        return 0

    lax.fori_loop(0, sems.shape[0], step, 0)
    lax.fori_loop(0, sems.shape[0], lambda i, _: (copy(i).wait(), 0)[1], 0)


def in_hbm(x):
    return pltpu.with_memory_space_constraint(x, pltpu.HBM)


def in_vmem(x):
    return pltpu.with_memory_space_constraint(x, pltpu.VMEM)


def call(kernel, outs, ins, flops, moved, limit, scratch=(), far=(), far_outs=(), alias=None):
    near = pl.BlockSpec(memory_space=pltpu.VMEM)
    away = pl.BlockSpec(memory_space=pl.ANY)
    return pl.pallas_call(
        kernel,
        out_shape=outs,
        in_specs=[away if n in far else near for n in range(len(ins))],
        out_specs=[away if n in far_outs else near for n in range(len(outs))],
        scratch_shapes=list(scratch),
        input_output_aliases=alias or {},
        compiler_params=pltpu.CompilerParams(vmem_limit_bytes=limit),
        cost_estimate=pl.CostEstimate(flops=flops, bytes_accessed=moved, transcendentals=0),
    )(*ins)


def local(
    gate_in, value_in, out_gate, residual, filters, kept_index, kept_owner, skip_bias, norm_gain
):
    tok_rows, slab = gate_in.shape
    slots, length = filters.shape[2:]
    chan_devices = lax.axis_size("chan")
    owner_count = lax.axis_size("seqo") * lax.axis_size("seqi")
    rows = slots * owner_count
    lanes_rows = -(-rows // LANES) * LANES
    blocks = tok_rows // LANES
    outer = length // LANES
    tile = TILE if tok_rows % TILE == 0 else LANES
    dense = tok_rows * slab * 2
    sds = jax.ShapeDtypeStruct
    tables = [in_hbm(jnp.asarray(x)) for x in dft_tables(length)]
    outer_fwd, turn, inner, outer_back = tables
    skip_row = skip_bias[None, :]
    gain_row = norm_gain[None, :]
    gate_in, value_in, out_gate, residual = map(in_hbm, (gate_in, value_in, out_gate, residual))
    picks = sds((blocks, rows, LANES), bf16)
    row_sums = sds((blocks, 1, LANES), f32)
    buffer = (owner_count, blocks, slots * LANES)
    whole = (tok_rows, slab)

    payload, channels, onehot_t = call(
        functools.partial(pick_kernel, owner_count, slots),
        [
            sds(buffer, bf16),
            sds((8, lanes_rows), jnp.int32),
            pltpu.HBM((slab, lanes_rows), bf16),
        ],
        [in_hbm(kept_index), in_hbm(kept_owner), gate_in, value_in],
        2 * tok_rows * slab * rows,
        2 * dense,
        24 * MIB,
        scratch=[
            pltpu.VMEM((blocks, rows, LANES), f32),
            pltpu.VMEM(whole, bf16),
            pltpu.VMEM(whole, bf16),
            pltpu.VMEM((slab, lanes_rows), bf16),
            pltpu.VMEM((2,) + kept_index.shape, jnp.int32),
            pltpu.SemaphoreType.DMA((3,)),
            pltpu.SemaphoreType.DMA((2, tok_rows // tile)),
        ],
        far=(0, 1, 2, 3),
        far_outs=(2,),
    )

    incoming = lax.all_to_all(payload, ("seqo", "seqi"), split_axis=0, concat_axis=0, tiled=True)

    (spectra,) = call(
        filter_kernel,
        [pltpu.HBM((slots, outer, 2 * LANES), f32)],
        [filters[0, 0]] + [jnp.asarray(x) for x in dft_tables(length)[:3]],
        2 * slots * length * 2 * (2 * outer + 6 * LANES),
        8 * MIB,
        16 * MIB,
    )
    onehot, others, skip_wide = call(
        place_kernel,
        [sds((rows, slab), bf16), sds((8, slab), f32), sds((rows, LANES), f32)],
        [channels, skip_row],
        rows * slab * 8,
        rows * slab * 2,
        8 * MIB,
    )

    def base_part(first, count, onehot_t, base):
        part = count * LANES
        ins = [onehot_t, others, skip_row, gate_in, value_in, out_gate, residual]
        outs = [
            pltpu.HBM(whole, bf16),
            sds((count, 1, LANES), f32),
            sds((count, rows, LANES), bf16),
            sds((count, rows, LANES), bf16),
        ]
        if base is not None:
            ins.append(base)
        return call(
            functools.partial(base_kernel, first * LANES),
            outs,
            ins,
            4 * part * slab * rows,
            10 * part * slab,
            24 * MIB,
            scratch=[pltpu.VMEM((part, slab), bf16)] * 5
            + [
                pltpu.VMEM((LANES, LANES), f32),
                pltpu.SemaphoreType.DMA((count,)),
                pltpu.SemaphoreType.DMA((4, count)),
            ],
            far=(3, 4, 5, 6, 7),
            far_outs=(0,),
            alias={} if base is None else {7: 0},
        )

    early = max(1, blocks * EARLY // 16)
    base, *half_picks = base_part(0, early, onehot_t, None)
    spectra, base = lax.optimization_barrier((spectra, base))

    conv_ins = [incoming, outer_fwd, turn, inner, in_hbm(spectra), outer_back]
    (convolved,) = call(
        convolve_kernel,
        [sds(buffer, bf16)],
        conv_ins,
        2 * slots * length * 2 * (5 * outer + 12 * LANES),
        8 * MIB,
        20 * MIB,
        scratch=[pltpu.VMEM(x.shape, x.dtype) for x in conv_ins[1:]]
        + [pltpu.SemaphoreType.DMA((len(conv_ins) - 1,))],
        far=tuple(range(1, len(conv_ins))),
    )
    convolved, onehot_t = lax.optimization_barrier((convolved, onehot_t))

    returned = lax.all_to_all(convolved, ("seqo", "seqi"), split_axis=0, concat_axis=0, tiled=True)

    base, *more_picks = base_part(early, blocks - early, onehot_t, base)

    hidden_kept, totals = call(
        kept_kernel,
        [picks, row_sums],
        [returned, payload, skip_wide, *half_picks, *more_picks],
        8 * rows * tok_rows,
        10 * rows * tok_rows,
        16 * MIB,
    )

    parts = [totals]
    for shift in range(1, chan_devices):
        ring = [(i, (i + shift) % chan_devices) for i in range(chan_devices)]
        parts.append(lax.ppermute(totals, "chan", ring))

    hidden, held = call(
        hidden_kernel,
        [pltpu.HBM(whole, bf16), pltpu.VMEM(whole, bf16)],
        [in_hbm(base), hidden_kept, onehot],
        2 * tok_rows * slab * rows,
        2 * dense,
        16 * MIB,
        scratch=[
            pltpu.VMEM(whole, bf16),
            pltpu.SemaphoreType.DMA((1, tok_rows // tile)),
            pltpu.SemaphoreType.DMA((tok_rows // tile,)),
        ],
        far=(0,),
        far_outs=(0,),
    )
    (normed,) = call(
        functools.partial(norm_kernel, float(slab * chan_devices), len(parts)),
        [pltpu.HBM(whole, bf16)],
        parts + [in_vmem(held), gain_row],
        4 * tok_rows * slab,
        2 * dense,
        16 * MIB,
        scratch=[
            pltpu.VMEM(whole, bf16),
            pltpu.VMEM((LANES, LANES), f32),
            pltpu.SemaphoreType.DMA((blocks,)),
        ],
        far_outs=(0,),
    )
    return (hidden, normed)


def solution(mesh):
    positions = P(("seqo", "seqi"), "chan")
    in_specs = (
        positions,
        positions,
        positions,
        positions,
        P("chan", ("seqo", "seqi"), None, None),
        P("chan", None),
        P("chan", None),
        P("chan"),
        P("chan"),
    )
    return jax.shard_map(
        local, mesh=mesh, in_specs=in_specs, out_specs=(positions, positions), check_vma=False
    )
```

```python
import functools

import jax
import jax.numpy as jnp
import numpy as np
from jax import lax
from jax.experimental import pallas as pl
from jax.experimental.pallas import tpu as pltpu
from jax.sharding import PartitionSpec as P

LANES = 128
TILE = 256
CHUNK = 16
GROUP = 3
AHEAD = 3
EARLY = 7
MIB = 1 << 20
norm_eps = 1e-06
f32 = jnp.float32
bf16 = jnp.bfloat16


def split_np(table):
    high = table.astype(jnp.bfloat16)
    low = (table - high.astype(np.float64)).astype(jnp.bfloat16)
    return high, low


def dft_tables(length):
    inner = LANES
    outer = length // inner
    a = np.arange(outer)
    b = np.arange(inner)
    quarter = np.arange(outer) + 0.25
    outer_angle = 2 * np.pi / outer * np.mod(quarter[:, None] * a[None, :], outer)
    turn_angle = 2 * np.pi / length * (quarter[:, None] * b[None, :])
    inner_angle = 2 * np.pi / inner * np.mod(b[:, None] * b[None, :], inner)
    outer_fwd = np.concatenate([np.cos(outer_angle), -np.sin(outer_angle)], axis=0)
    c, s = np.cos(inner_angle), np.sin(inner_angle)
    inner_fwd = np.concatenate(
        [np.concatenate([c, -s], axis=1), np.concatenate([s, c], axis=1)], axis=0
    )
    inner_back = np.concatenate(
        [np.concatenate([c, s], axis=1), np.concatenate([-s, c], axis=1)], axis=0
    )
    outer_back = np.concatenate([np.cos(outer_angle).T, -np.sin(outer_angle).T], axis=1) / length
    turn = np.concatenate([np.cos(turn_angle), np.sin(turn_angle)], axis=1).astype(np.float32)
    outer_fwd = np.concatenate(split_np(outer_fwd), axis=1)
    inner = np.concatenate(split_np(inner_fwd) + split_np(inner_back), axis=0)
    outer_back = np.concatenate(split_np(outer_back), axis=1)
    return outer_fwd, turn, inner, outer_back


def split(value):
    high = value.astype(bf16)
    low = (value - high.astype(f32)).astype(bf16)
    return high, low


def dot(x, y):
    return jnp.dot(x, y, preferred_element_type=f32)


def dot_rows(x, y):
    return lax.dot_general(x, y, (((0,), (0,)), ((), ())), preferred_element_type=f32)


def times_table(value, table):
    high, low = split(value)
    depth = value.shape[1]
    stacked = jnp.concatenate([table, table[:depth]], axis=0)
    return dot(jnp.concatenate([high, high, low], axis=1), stacked)


def table_times(table, value):
    high, low = split(value)
    depth = value.shape[0]
    stacked = jnp.concatenate([table, table[:, :depth]], axis=1)
    return dot(stacked, jnp.concatenate([high, high, low], axis=0))


def to_spectrum(blocks, slots, outer_fwd, turn, inner_fwd):
    outer = blocks.shape[0]
    first = dot(outer_fwd, jnp.concatenate([blocks, blocks], axis=0))
    turn, inner_fwd = turn(), inner_fwd()
    cos, sin = turn[:, :LANES], turn[:, LANES:]
    turned = []
    for s in range(slots):
        re = first[:outer, s * LANES : (s + 1) * LANES]
        im = first[outer:, s * LANES : (s + 1) * LANES]
        turned.append(jnp.concatenate([re * cos + im * sin, im * cos - re * sin], axis=1))
    return grouped(turned, inner_fwd)


def grouped(values, table):
    result = []
    for s in range(0, len(values), GROUP):
        part = values[s : s + GROUP]
        size = part[0].shape[0]
        product = times_table(jnp.concatenate(part, axis=0), table)
        result += [product[n * size : (n + 1) * size] for n in range(len(part))]
    return result


def filter_spectra(filters, outer_fwd, turn, inner):
    slots, length = filters.shape
    outer = length // LANES
    wide = filters[...].astype(f32)
    blocks = [wide[s].reshape(outer, LANES) for s in range(slots)]
    blocks = jnp.concatenate(blocks, axis=1).astype(bf16)
    return to_spectrum(
        blocks, slots, outer_fwd[...], lambda: turn[...], lambda: inner[: 4 * LANES, :]
    )


def convolve_kernel(
    signals, outer_fwd_far, turn_far, inner_far, spectra_far, outer_back_far, out, *scratch
):
    sources = (outer_fwd_far, turn_far, inner_far, spectra_far, outer_back_far)
    outer_fwd, turn_ref, inner, spectra, outer_back, result, sems = scratch
    copies = [
        pltpu.make_async_copy(source, scratch[n], sems.at[n]) for n, source in enumerate(sources)
    ]
    for copy in copies[:3]:
        copy.start()
    slots, outer = spectra.shape[:2]

    def turn_now():
        copies[1].wait()
        return turn_ref[...]

    def inner_now():
        copies[2].wait()
        return inner[: 4 * LANES, :]

    copies[0].wait()
    for copy in copies[3:]:
        copy.start()
    blocks = signals[...].reshape(outer, slots * LANES)
    parts = to_spectrum(blocks, slots, outer_fwd[...], turn_now, inner_now)
    turn = turn_ref[...]
    cos, sin = turn[:, :LANES], turn[:, LANES:]
    copies[3].wait()
    joint = []
    for s in range(slots):
        sig_re, sig_im = parts[s][:, :LANES], parts[s][:, LANES:]
        ker_re, ker_im = spectra[s, :, :LANES], spectra[s, :, LANES:]
        joint.append(
            jnp.concatenate(
                [sig_re * ker_re - sig_im * ker_im, sig_re * ker_im + sig_im * ker_re], axis=1
            )
        )
    turned = []
    for back in grouped(joint, inner[4 * LANES :, :]):
        re, im = back[:, :LANES], back[:, LANES:]
        turned.append(jnp.concatenate([re * cos - im * sin, im * cos + re * sin], axis=0))
    copies[4].wait()
    sends = []
    for s in range(0, slots, 2):
        pair = turned[s : s + 2]
        causal = table_times(outer_back[...], jnp.concatenate(pair, axis=1)).astype(bf16)
        lanes = pl.ds(s * LANES, len(pair) * LANES)
        result[:, :, lanes] = causal.reshape(out.shape[:2] + (len(pair) * LANES,))
        sends.append(
            pltpu.make_async_copy(
                result.at[:, :, lanes], out.at[:, :, lanes], sems.at[len(copies) + len(sends)]
            )
        )
        sends[-1].start()
    for send in sends:
        send.wait()


def iota(shape, axis):
    return lax.broadcasted_iota(jnp.int32, shape, axis)


def to_column(row):
    size = row.shape[1]
    same = iota((size, size), 0) == iota((size, size), 1)
    return jnp.sum(jnp.where(same, row, 0), axis=1, keepdims=True)


def channel_of_row(index_row, owners_row, owner_count, rows):
    slots = owners_row.shape[1]
    owners_col = to_column(owners_row)
    index_col = to_column(index_row)
    earlier = (owners_col == owners_row) & (iota((slots, slots), 1) < iota((slots, slots), 0))
    rank_col = jnp.sum(earlier.astype(jnp.int32), axis=1, keepdims=True)
    target_col = jnp.where(owners_col >= 0, rank_col * owner_count + owners_col, -1)
    hit = target_col == iota((slots, rows), 1)
    return jnp.sum(jnp.where(hit, index_col + 1, 0), axis=0, keepdims=True) - 1


def pick_rows(tile, onehot_t, rows):
    picked = dot(tile, onehot_t).T
    return [picked[:rows, i : i + LANES] for i in range(0, tile.shape[0], LANES)]


def fetch(sources, stages, sems, tile, first=0):
    count = stages[0].shape[0] // tile

    def copies(i):
        at = pl.multiple_of(i * tile, tile)
        return [
            pltpu.make_async_copy(
                source.at[pl.ds(first + at, tile), :], stage.at[pl.ds(at, tile), :], sems.at[n, i]
            )
            for n, (source, stage) in enumerate(zip(sources, stages))
        ]

    def start(i):
        for copy in copies(i):
            copy.start()

    for i in range(min(AHEAD, count)):
        start(i)

    def wait(i):
        for copy in copies(i):
            copy.wait()

        @pl.when(i + AHEAD < count)
        def _():
            start(i + AHEAD)

        return pl.multiple_of(i * tile, tile)

    return wait, count


def pick_kernel(owner_count, slots, index, owners, gate, value, *refs):
    payload, picked, channels, onehot_far = refs[:4]
    acc, gate_stage, value_stage, onehot_t, lists, list_sems, sems = refs[4:]
    rows = owner_count * slots
    tile = gate_stage.shape[0] // sems.shape[1]
    list_copies = [
        pltpu.make_async_copy(source, lists.at[n], list_sems.at[n])
        for n, source in enumerate((index, owners))
    ]
    for copy in list_copies:
        copy.start()
    wait, count = fetch((gate, value), (gate_stage, value_stage), sems, tile)
    for copy in list_copies:
        copy.wait()
    row = channel_of_row(lists[0], lists[1], owner_count, onehot_t.shape[1])
    channels[...] = jnp.broadcast_to(row, channels.shape)
    onehot_t[...] = (iota(onehot_t.shape, 0) == row).astype(f32).astype(bf16)
    onehot_copy = pltpu.make_async_copy(onehot_t, onehot_far, list_sems.at[2])
    onehot_copy.start()

    def step(i, _):
        at = pl.ds(wait(i), tile)
        gated = gate_stage[at, :] * value_stage[at, :]
        for n, block in enumerate(pick_rows(gated, onehot_t[...], rows)):
            acc[i * (tile // LANES) + n] = block
            picked[i * (tile // LANES) + n] = block.astype(bf16)
        return 0

    lax.fori_loop(0, count, step, 0)
    for s in range(slots):
        part = jnp.swapaxes(acc[:, s * owner_count : (s + 1) * owner_count, :], 0, 1)
        payload[:, :, s * LANES : (s + 1) * LANES] = part.astype(bf16)
    onehot_copy.wait()


def first_kernel(channels, filters_far, outer_fwd_far, turn_far, inner_far, *refs):
    onehot_t, skip, *dense = refs[:6]
    onehot, others, skip_wide, spectra, *outs = refs[6:14]
    filters, outer_fwd, turn, inner, spectra_stage, table_sems = refs[14:20]
    tables = [
        pltpu.make_async_copy(source, stage, table_sems.at[n])
        for n, (source, stage) in enumerate(
            (
                (filters_far, filters),
                (outer_fwd_far, outer_fwd),
                (turn_far, turn),
                (inner_far, inner),
            )
        )
    ]
    for copy in tables:
        copy.start()

    def beside():
        hit = iota(onehot.shape, 1) == to_column(channels[0:1, :])[: onehot.shape[0]]
        onehot[...] = hit.astype(f32).astype(bf16)
        kept = jnp.max(hit.astype(f32), axis=0, keepdims=True)
        others[...] = jnp.broadcast_to(1.0 - kept, others.shape)
        skip_col = jnp.sum(jnp.where(hit, skip[...], 0.0), axis=1, keepdims=True)
        skip_wide[...] = jnp.broadcast_to(skip_col, skip_wide.shape)
        for copy in tables:
            copy.wait()
        for s, part in enumerate(filter_spectra(filters, outer_fwd, turn, inner)):
            spectra_stage[s] = part
            send(s).start()

    def send(s):
        return pltpu.make_async_copy(
            spectra_stage.at[s], spectra.at[s], table_sems.at[len(tables) + s]
        )

    base_pass(0, onehot_t, others, skip, dense, outs, refs[20:], beside)
    for s in range(spectra.shape[0]):
        send(s).wait()


def second_kernel(first, onehot_t, others, skip, *refs):
    base_pass(first, onehot_t, others, skip, refs[:4], refs[5:9], refs[9:])


def base_pass(first, onehot_t, others, skip, dense, outs, scratch, beside=None):
    base, sums, picked_gate, picked_res = outs
    stages = scratch[:4]
    base_stage, partial, base_sems, sems = scratch[4:]
    gate_stage, value_stage, out_stage, res_stage = stages
    rows = picked_gate.shape[1]
    slab = gate_stage.shape[1]
    tile = partial.shape[0]
    wait, count = fetch(dense, stages, sems, tile, first)
    if beside is not None:
        beside()

    def copy(i):
        at = pl.multiple_of(i * tile, tile)
        return pltpu.make_async_copy(
            base_stage.at[pl.ds(at, tile), :], base.at[pl.ds(first + at, tile), :], base_sems.at[i]
        )

    def step(i, _):
        start = wait(i)
        for c in range(0, tile, CHUNK):
            at = pl.ds(start + c, CHUNK)
            total = jnp.zeros((CHUNK, LANES), f32)
            for j in range(0, slab, LANES):
                lanes = slice(j, j + LANES)
                gated = (gate_stage[at, lanes] * value_stage[at, lanes]).astype(f32)
                mixed = out_stage[at, lanes].astype(f32) * (skip[:, lanes] * gated)
                hidden = (res_stage[at, lanes].astype(f32) + mixed) * others[0:1, lanes]
                hidden = hidden.astype(bf16)
                base_stage[at, lanes] = hidden
                hidden = hidden.astype(f32)
                total = total + hidden * hidden
            partial[c : c + CHUNK, :] = total
        copy(i).start()
        total = jnp.sum(partial[...].T, axis=0, keepdims=True)
        at = pl.ds(start, tile)
        picks_gate = pick_rows(out_stage[at, :], onehot_t[...], rows)
        picks_res = pick_rows(res_stage[at, :], onehot_t[...], rows)
        for n in range(tile // LANES):
            block = i * (tile // LANES) + n
            sums[block] = total[:, n * LANES : (n + 1) * LANES]
            picked_gate[block] = picks_gate[n].astype(bf16)
            picked_res[block] = picks_res[n].astype(bf16)
        return 0

    lax.fori_loop(0, count, step, 0)
    lax.fori_loop(0, count, lambda i, _: (copy(i).wait(), 0)[1], 0)


def kept_kernel(conv, picked, skip_wide, *refs):
    hidden, totals = refs[-2:]
    owner_count, blocks = conv.shape[:2]
    first = 0
    for n in range(0, len(refs) - 2, 3):
        sums, picked_gate, picked_res = refs[n : n + 3]
        size = sums.shape[0]
        at_h = slice(first, first + size)
        total = jnp.zeros((size, LANES), f32)
        for s in range(conv.shape[2] // LANES):
            at = slice(s * owner_count, (s + 1) * owner_count)
            lanes = slice(s * LANES, (s + 1) * LANES)
            wide = jnp.swapaxes(conv[:, at_h, lanes].astype(f32), 0, 1)
            wide = wide + skip_wide[at, :] * picked[at_h, at, :].astype(f32)
            value = picked_res[:, at, :].astype(f32) + picked_gate[:, at, :].astype(f32) * wide
            value = value.astype(bf16)
            hidden[at_h, at, :] = value
            value = value.astype(f32)
            total = total + jnp.sum(value * value, axis=1)
        for i in range(size):
            totals[first + i] = total[i : i + 1, :] + sums[i]
        first = first + size


def hidden_kernel(base, hidden_kept, onehot, hidden, held, base_stage, base_sems, sems):
    slab = held.shape[1]
    wide = min(slab, 2 * LANES)
    count = sems.shape[0]
    tile = held.shape[0] // count
    wait, _ = fetch((base,), (base_stage,), base_sems, tile)

    def copy(i):
        rows = pl.ds(pl.multiple_of(i * tile, tile), tile)
        return pltpu.make_async_copy(held.at[rows, :], hidden.at[rows, :], sems.at[i])

    def step(i, _):
        blocks = range(tile // LANES)
        kept = [hidden_kept[i * (tile // LANES) + n].astype(f32).T.astype(bf16) for n in blocks]
        kept = jnp.concatenate(kept, axis=0)
        rows = pl.ds(wait(i), tile)
        for j in range(0, slab, wide):
            lanes = slice(j, j + wide)
            placed = dot(kept, onehot[:, lanes]).astype(bf16)
            held[rows, lanes] = base_stage[rows, lanes] + placed
        copy(i).start()
        return 0

    lax.fori_loop(0, count, step, 0)
    lax.fori_loop(0, count, lambda i, _: (copy(i).wait(), 0)[1], 0)


def norm_kernel(width, count, *refs):
    parts = refs[:count]
    held, gain, normed, stage, turned, sems = refs[count:]
    slab = held.shape[1]

    def copy(i):
        rows = pl.ds(pl.multiple_of(i * LANES, LANES), LANES)
        return pltpu.make_async_copy(stage.at[rows, :], normed.at[rows, :], sems.at[i])

    def step(i, _):
        total = parts[0][i]
        for part in parts[1:]:
            total = total + part[i]
        scale = lax.rsqrt(total / width + norm_eps)
        turned[...] = jnp.broadcast_to(scale, (LANES, LANES)).T
        first = pl.multiple_of(i * LANES, LANES)
        for c in range(0, LANES, CHUNK):
            at = pl.ds(first + c, CHUNK)
            scales = turned[c : c + CHUNK, :]
            for j in range(0, slab, LANES):
                lanes = slice(j, j + LANES)
                value = held[at, lanes].astype(f32) * scales * gain[:, lanes]
                stage[at, lanes] = value.astype(bf16)
        copy(i).start()
        return 0

    lax.fori_loop(0, sems.shape[0], step, 0)
    lax.fori_loop(0, sems.shape[0], lambda i, _: (copy(i).wait(), 0)[1], 0)


def in_hbm(x):
    return pltpu.with_memory_space_constraint(x, pltpu.HBM)


def in_vmem(x):
    return pltpu.with_memory_space_constraint(x, pltpu.VMEM)


def call(kernel, outs, ins, flops, moved, limit, scratch=(), far=(), far_outs=(), alias=None):
    near = pl.BlockSpec(memory_space=pltpu.VMEM)
    away = pl.BlockSpec(memory_space=pl.ANY)
    return pl.pallas_call(
        kernel,
        out_shape=outs,
        in_specs=[away if n in far else near for n in range(len(ins))],
        out_specs=[away if n in far_outs else near for n in range(len(outs))],
        scratch_shapes=list(scratch),
        input_output_aliases=alias or {},
        compiler_params=pltpu.CompilerParams(vmem_limit_bytes=limit),
        cost_estimate=pl.CostEstimate(flops=flops, bytes_accessed=moved, transcendentals=0),
    )(*ins)


def local(
    gate_in, value_in, out_gate, residual, filters, kept_index, kept_owner, skip_bias, norm_gain
):
    tok_rows, slab = gate_in.shape
    slots, length = filters.shape[2:]
    chan_devices = lax.axis_size("chan")
    owner_count = lax.axis_size("seqo") * lax.axis_size("seqi")
    rows = slots * owner_count
    lanes_rows = -(-rows // LANES) * LANES
    blocks = tok_rows // LANES
    outer = length // LANES
    tile = TILE if tok_rows % TILE == 0 else LANES
    dense = tok_rows * slab * 2
    sds = jax.ShapeDtypeStruct
    tables = [in_hbm(jnp.asarray(x)) for x in dft_tables(length)]
    outer_fwd, turn, inner, outer_back = tables
    skip_row = skip_bias[None, :]
    gain_row = norm_gain[None, :]
    gate_in, value_in, out_gate, residual = map(in_hbm, (gate_in, value_in, out_gate, residual))
    picks = sds((blocks, rows, LANES), bf16)
    row_sums = sds((blocks, 1, LANES), f32)
    buffer = (owner_count, blocks, slots * LANES)
    whole = (tok_rows, slab)

    payload, picked, channels, onehot_t = call(
        functools.partial(pick_kernel, owner_count, slots),
        [
            sds(buffer, bf16),
            picks,
            sds((8, lanes_rows), jnp.int32),
            pltpu.HBM((slab, lanes_rows), bf16),
        ],
        [in_hbm(kept_index), in_hbm(kept_owner), gate_in, value_in],
        2 * tok_rows * slab * rows,
        2 * dense,
        24 * MIB,
        scratch=[
            pltpu.VMEM((blocks, rows, LANES), f32),
            pltpu.VMEM(whole, bf16),
            pltpu.VMEM(whole, bf16),
            pltpu.VMEM((slab, lanes_rows), bf16),
            pltpu.VMEM((2,) + kept_index.shape, jnp.int32),
            pltpu.SemaphoreType.DMA((3,)),
            pltpu.SemaphoreType.DMA((2, tok_rows // tile)),
        ],
        far=(0, 1, 2, 3),
        far_outs=(3,),
    )

    incoming = lax.all_to_all(payload, ("seqo", "seqi"), split_axis=0, concat_axis=0, tiled=True)

    dense_ins = [gate_in, value_in, out_gate, residual]

    def base_parts(count):
        part = count * LANES
        outs = [
            pltpu.HBM(whole, bf16),
            sds((count, 1, LANES), f32),
            sds((count, rows, LANES), bf16),
            sds((count, rows, LANES), bf16),
        ]
        scratch = [pltpu.VMEM((part, slab), bf16)] * 5 + [
            pltpu.VMEM((LANES, LANES), f32),
            pltpu.SemaphoreType.DMA((count,)),
            pltpu.SemaphoreType.DMA((4, count)),
        ]
        return outs, scratch, 4 * part * slab * rows, 10 * part * slab

    early = max(1, blocks * EARLY // 16)
    outs, scratch, flops, moved = base_parts(early)
    spectrum = (slots, outer, 2 * LANES)
    table_ins = [in_hbm(filters[0, 0]), outer_fwd, turn, inner]
    onehot, others, skip_wide, spectra, base, *first_picks = call(
        first_kernel,
        [
            sds((rows, slab), bf16),
            sds((8, slab), f32),
            sds((rows, LANES), f32),
            pltpu.HBM(spectrum, f32),
        ]
        + outs,
        [channels] + table_ins + [onehot_t, skip_row] + dense_ins,
        flops,
        moved,
        36 * MIB,
        scratch=[pltpu.VMEM(x.shape, x.dtype) for x in table_ins]
        + [pltpu.VMEM(spectrum, f32), pltpu.SemaphoreType.DMA((len(table_ins) + slots,))]
        + scratch,
        far=(1, 2, 3, 4, 7, 8, 9, 10),
        far_outs=(3, 4),
    )

    conv_ins = [incoming, outer_fwd, turn, inner, in_hbm(spectra), outer_back]
    (convolved,) = call(
        convolve_kernel,
        [pltpu.HBM(buffer, bf16)],
        conv_ins,
        2 * slots * length * 2 * (5 * outer + 12 * LANES),
        8 * MIB,
        20 * MIB,
        scratch=[pltpu.VMEM(x.shape, x.dtype) for x in conv_ins[1:]]
        + [pltpu.VMEM(buffer, bf16), pltpu.SemaphoreType.DMA((len(conv_ins) - 1 + slots,))],
        far=tuple(range(1, len(conv_ins))),
        far_outs=(0,),
    )
    convolved, onehot_t = lax.optimization_barrier((convolved, onehot_t))

    returned = lax.all_to_all(convolved, ("seqo", "seqi"), split_axis=0, concat_axis=0, tiled=True)

    outs, scratch, flops, moved = base_parts(blocks - early)
    base, *more_picks = call(
        functools.partial(second_kernel, early * LANES),
        outs,
        [onehot_t, others, skip_row] + dense_ins + [base],
        flops,
        moved,
        36 * MIB,
        scratch=scratch,
        far=(3, 4, 5, 6, 7),
        far_outs=(0,),
        alias={7: 0},
    )

    hidden_kept, totals = call(
        kept_kernel,
        [picks, row_sums],
        [returned, picked, skip_wide, *first_picks, *more_picks],
        8 * rows * tok_rows,
        10 * rows * tok_rows,
        16 * MIB,
    )

    parts = [totals]
    for shift in range(1, chan_devices):
        ring = [(i, (i + shift) % chan_devices) for i in range(chan_devices)]
        parts.append(lax.ppermute(totals, "chan", ring))

    hidden, held = call(
        hidden_kernel,
        [pltpu.HBM(whole, bf16), pltpu.VMEM(whole, bf16)],
        [in_hbm(base), hidden_kept, onehot],
        2 * tok_rows * slab * rows,
        2 * dense,
        16 * MIB,
        scratch=[
            pltpu.VMEM(whole, bf16),
            pltpu.SemaphoreType.DMA((1, tok_rows // tile)),
            pltpu.SemaphoreType.DMA((tok_rows // tile,)),
        ],
        far=(0,),
        far_outs=(0,),
    )
    (normed,) = call(
        functools.partial(norm_kernel, float(slab * chan_devices), len(parts)),
        [pltpu.HBM(whole, bf16)],
        parts + [in_vmem(held), gain_row],
        4 * tok_rows * slab,
        2 * dense,
        16 * MIB,
        scratch=[
            pltpu.VMEM(whole, bf16),
            pltpu.VMEM((LANES, LANES), f32),
            pltpu.SemaphoreType.DMA((blocks,)),
        ],
        far_outs=(0,),
    )
    return (hidden, normed)


def solution(mesh):
    positions = P(("seqo", "seqi"), "chan")
    in_specs = (
        positions,
        positions,
        positions,
        positions,
        P("chan", ("seqo", "seqi"), None, None),
        P("chan", None),
        P("chan", None),
        P("chan"),
        P("chan"),
    )
    return jax.shard_map(
        local, mesh=mesh, in_specs=in_specs, out_specs=(positions, positions), check_vma=False
    )
```

```python
import functools

import jax
import jax.numpy as jnp
import numpy as np
from jax import lax
from jax.experimental import pallas as pl
from jax.experimental.pallas import tpu as pltpu
from jax.sharding import PartitionSpec as P

LANES = 128
TILE = 256
CHUNK = 16
GROUP = 3
EARLY = 7
MIB = 1 << 20
norm_eps = 1e-06
f32 = jnp.float32
bf16 = jnp.bfloat16


def split_np(table):
    high = table.astype(jnp.bfloat16)
    low = (table - high.astype(np.float64)).astype(jnp.bfloat16)
    return high, low


def dft_tables(length):
    inner = LANES
    outer = length // inner
    a = np.arange(outer)
    b = np.arange(inner)
    quarter = np.arange(outer) + 0.25
    outer_angle = 2 * np.pi / outer * np.mod(quarter[:, None] * a[None, :], outer)
    turn_angle = 2 * np.pi / length * (quarter[:, None] * b[None, :])
    inner_angle = 2 * np.pi / inner * np.mod(b[:, None] * b[None, :], inner)
    outer_fwd = np.concatenate([np.cos(outer_angle), -np.sin(outer_angle)], axis=0)
    c, s = np.cos(inner_angle), np.sin(inner_angle)
    inner_fwd = np.concatenate(
        [np.concatenate([c, -s], axis=1), np.concatenate([s, c], axis=1)], axis=0
    )
    inner_back = np.concatenate(
        [np.concatenate([c, s], axis=1), np.concatenate([-s, c], axis=1)], axis=0
    )
    outer_back = np.concatenate([np.cos(outer_angle).T, -np.sin(outer_angle).T], axis=1) / length
    turn = np.concatenate([np.cos(turn_angle), np.sin(turn_angle)], axis=1).astype(np.float32)
    outer_fwd = np.concatenate(split_np(outer_fwd), axis=1)
    inner = np.concatenate(split_np(inner_fwd) + split_np(inner_back), axis=0)
    outer_back = np.concatenate(split_np(outer_back), axis=1)
    return outer_fwd, turn, inner, outer_back


def split(value):
    high = value.astype(bf16)
    low = (value - high.astype(f32)).astype(bf16)
    return high, low


def dot(x, y):
    return jnp.dot(x, y, preferred_element_type=f32)


def dot_rows(x, y):
    return lax.dot_general(x, y, (((0,), (0,)), ((), ())), preferred_element_type=f32)


def times_table(value, table):
    high, low = split(value)
    depth = value.shape[1]
    stacked = jnp.concatenate([table, table[:depth]], axis=0)
    return dot(jnp.concatenate([high, high, low], axis=1), stacked)


def table_times(table, value):
    high, low = split(value)
    depth = value.shape[0]
    stacked = jnp.concatenate([table, table[:, :depth]], axis=1)
    return dot(stacked, jnp.concatenate([high, high, low], axis=0))


def to_spectrum(blocks, slots, outer_fwd, turn, inner_fwd):
    outer = blocks.shape[0]
    first = dot(outer_fwd, jnp.concatenate([blocks, blocks], axis=0))
    turn, inner_fwd = turn(), inner_fwd()
    cos, sin = turn[:, :LANES], turn[:, LANES:]
    turned = []
    for s in range(slots):
        re = first[:outer, s * LANES : (s + 1) * LANES]
        im = first[outer:, s * LANES : (s + 1) * LANES]
        turned.append(jnp.concatenate([re * cos + im * sin, im * cos - re * sin], axis=1))
    return grouped(turned, inner_fwd)


def grouped(values, table):
    result = []
    for s in range(0, len(values), GROUP):
        part = values[s : s + GROUP]
        size = part[0].shape[0]
        product = times_table(jnp.concatenate(part, axis=0), table)
        result += [product[n * size : (n + 1) * size] for n in range(len(part))]
    return result


def filter_spectra(filters, outer_fwd, turn, inner):
    slots, length = filters.shape
    outer = length // LANES
    wide = filters[...].astype(f32)
    blocks = [wide[s].reshape(outer, LANES) for s in range(slots)]
    blocks = jnp.concatenate(blocks, axis=1).astype(bf16)
    return to_spectrum(
        blocks, slots, outer_fwd[...], lambda: turn[...], lambda: inner[: 4 * LANES, :]
    )


def convolve_kernel(
    signals, outer_fwd_far, turn_far, inner_far, spectra_far, outer_back_far, out, *scratch
):
    sources = (outer_fwd_far, turn_far, inner_far, spectra_far, outer_back_far)
    outer_fwd, turn_ref, inner, spectra, outer_back, result, sems = scratch
    copies = [
        pltpu.make_async_copy(source, scratch[n], sems.at[n]) for n, source in enumerate(sources)
    ]
    copies[0].start()
    slots, outer = spectra.shape[:2]

    def turn_now():
        copies[1].wait()
        return turn_ref[...]

    def inner_now():
        copies[2].wait()
        return inner[: 4 * LANES, :]

    copies[0].wait()
    for copy in copies[1:]:
        copy.start()
    blocks = signals[...].reshape(outer, slots * LANES)
    parts = to_spectrum(blocks, slots, outer_fwd[...], turn_now, inner_now)
    turn = turn_ref[...]
    cos, sin = turn[:, :LANES], turn[:, LANES:]
    copies[3].wait()
    joint = []
    for s in range(slots):
        sig_re, sig_im = parts[s][:, :LANES], parts[s][:, LANES:]
        ker_re, ker_im = spectra[s, :, :LANES], spectra[s, :, LANES:]
        joint.append(
            jnp.concatenate(
                [sig_re * ker_re - sig_im * ker_im, sig_re * ker_im + sig_im * ker_re], axis=1
            )
        )
    turned = []
    for back in grouped(joint, inner[4 * LANES :, :]):
        re, im = back[:, :LANES], back[:, LANES:]
        turned.append(jnp.concatenate([re * cos - im * sin, im * cos + re * sin], axis=0))
    copies[4].wait()
    sends = []
    for s in range(0, slots, 2):
        pair = turned[s : s + 2]
        causal = table_times(outer_back[...], jnp.concatenate(pair, axis=1)).astype(bf16)
        lanes = pl.ds(s * LANES, len(pair) * LANES)
        result[:, :, lanes] = causal.reshape(out.shape[:2] + (len(pair) * LANES,))
        sends.append(
            pltpu.make_async_copy(
                result.at[:, :, lanes], out.at[:, :, lanes], sems.at[len(copies) + len(sends)]
            )
        )
        sends[-1].start()
    for send in sends:
        send.wait()


def iota(shape, axis):
    return lax.broadcasted_iota(jnp.int32, shape, axis)


def to_column(row):
    size = row.shape[1]
    same = iota((size, size), 0) == iota((size, size), 1)
    return jnp.sum(jnp.where(same, row, 0), axis=1, keepdims=True)


def channel_of_row(index_row, owners_row, owner_count, rows):
    slots = owners_row.shape[1]
    owners_col = to_column(owners_row)
    index_col = to_column(index_row)
    earlier = (owners_col == owners_row) & (iota((slots, slots), 1) < iota((slots, slots), 0))
    rank_col = jnp.sum(earlier.astype(jnp.int32), axis=1, keepdims=True)
    target_col = jnp.where(owners_col >= 0, rank_col * owner_count + owners_col, -1)
    hit = target_col == iota((slots, rows), 1)
    return jnp.sum(jnp.where(hit, index_col + 1, 0), axis=0, keepdims=True) - 1


def pick_rows(tile, onehot_t, rows):
    picked = dot(tile, onehot_t).T
    return [picked[:rows, i : i + LANES] for i in range(0, tile.shape[0], LANES)]


def fetch(sources, stages, sems, tile, first=0, ahead=2):
    count = stages[0].shape[0] // tile

    def copies(i):
        at = pl.multiple_of(i * tile, tile)
        return [
            pltpu.make_async_copy(
                source.at[pl.ds(first + at, tile), :], stage.at[pl.ds(at, tile), :], sems.at[n, i]
            )
            for n, (source, stage) in enumerate(zip(sources, stages))
        ]

    def start(i):
        for copy in copies(i):
            copy.start()

    for i in range(min(ahead, count)):
        start(i)

    def wait(i):
        for copy in copies(i):
            copy.wait()

        @pl.when(i + ahead < count)
        def _():
            start(i + ahead)

        return pl.multiple_of(i * tile, tile)

    return wait, count


def pick_kernel(owner_count, slots, index, owners, gate, value, *refs):
    payload, picked, channels, onehot_far = refs[:4]
    acc, gate_stage, value_stage, onehot_t, lists, list_sems, sems = refs[4:]
    rows = owner_count * slots
    tile = gate_stage.shape[0] // sems.shape[1]
    list_copies = [
        pltpu.make_async_copy(source, lists.at[n], list_sems.at[n])
        for n, source in enumerate((index, owners))
    ]
    for copy in list_copies:
        copy.start()
    wait, count = fetch((gate, value), (gate_stage, value_stage), sems, tile)
    for copy in list_copies:
        copy.wait()
    row = channel_of_row(lists[0], lists[1], owner_count, onehot_t.shape[1])
    channels[...] = jnp.broadcast_to(row, channels.shape)
    onehot_t[...] = (iota(onehot_t.shape, 0) == row).astype(f32).astype(bf16)
    onehot_copy = pltpu.make_async_copy(onehot_t, onehot_far, list_sems.at[2])
    onehot_copy.start()

    def step(i, _):
        at = pl.ds(wait(i), tile)
        gated = gate_stage[at, :] * value_stage[at, :]
        for n, block in enumerate(pick_rows(gated, onehot_t[...], rows)):
            acc[i * (tile // LANES) + n] = block
            picked[i * (tile // LANES) + n] = block.astype(bf16)
        return 0

    lax.fori_loop(0, count, step, 0)
    for s in range(slots):
        part = jnp.swapaxes(acc[:, s * owner_count : (s + 1) * owner_count, :], 0, 1)
        payload[:, :, s * LANES : (s + 1) * LANES] = part.astype(bf16)
    onehot_copy.wait()


def first_kernel(channels, filters_far, outer_fwd_far, turn_far, inner_far, *refs):
    onehot_far, skip, *dense = refs[:6]
    onehot, others, skip_wide, spectra, *outs = refs[6:14]
    filters, outer_fwd, turn, inner, onehot_t, spectra_stage, table_sems = refs[14:21]
    sources = (filters_far, outer_fwd_far, turn_far, inner_far, onehot_far)
    stages = (filters, outer_fwd, turn, inner, onehot_t)
    tables = [
        pltpu.make_async_copy(source, stage, table_sems.at[n])
        for n, (source, stage) in enumerate(zip(sources, stages))
    ]
    for copy in tables:
        copy.start()
    hit = iota(onehot.shape, 1) == to_column(channels[0:1, :])[: onehot.shape[0]]
    onehot[...] = hit.astype(f32).astype(bf16)
    kept = jnp.max(hit.astype(f32), axis=0, keepdims=True)
    others[...] = jnp.broadcast_to(1.0 - kept, others.shape)
    skip_col = jnp.sum(jnp.where(hit, skip[...], 0.0), axis=1, keepdims=True)
    skip_wide[...] = jnp.broadcast_to(skip_col, skip_wide.shape)

    def send(s):
        return pltpu.make_async_copy(
            spectra_stage.at[s], spectra.at[s], table_sems.at[len(tables) + s]
        )

    def beside():
        for copy in tables:
            copy.wait()
        for s, part in enumerate(filter_spectra(filters, outer_fwd, turn, inner)):
            spectra_stage[s] = part
            send(s).start()

    base_pass(0, onehot_t, others, skip, dense, outs, refs[21:], beside, 3)
    for s in range(spectra.shape[0]):
        send(s).wait()


def second_kernel(first, onehot_far, others, skip, *refs):
    onehot_t, onehot_sem = refs[9:11]
    copy = pltpu.make_async_copy(onehot_far, onehot_t, onehot_sem.at[0])
    copy.start()
    base_pass(first, onehot_t, others, skip, refs[:4], refs[5:9], refs[11:], copy.wait, 2)


def base_pass(first, onehot_t, others, skip, dense, outs, scratch, beside, ahead):
    base, sums, picked_gate, picked_res = outs
    stages = scratch[:4]
    base_stage, partial, base_sems, sems = scratch[4:]
    gate_stage, value_stage, out_stage, res_stage = stages
    rows = picked_gate.shape[1]
    slab = gate_stage.shape[1]
    tile = partial.shape[0]
    wait, count = fetch(dense, stages, sems, tile, first, ahead)
    beside()

    def copy(i):
        at = pl.multiple_of(i * tile, tile)
        return pltpu.make_async_copy(
            base_stage.at[pl.ds(at, tile), :], base.at[pl.ds(first + at, tile), :], base_sems.at[i]
        )

    def step(i, _):
        start = wait(i)
        for c in range(0, tile, CHUNK):
            at = pl.ds(start + c, CHUNK)
            total = jnp.zeros((CHUNK, LANES), f32)
            for j in range(0, slab, LANES):
                lanes = slice(j, j + LANES)
                gated = (gate_stage[at, lanes] * value_stage[at, lanes]).astype(f32)
                mixed = out_stage[at, lanes].astype(f32) * (skip[:, lanes] * gated)
                hidden = (res_stage[at, lanes].astype(f32) + mixed) * others[0:1, lanes]
                hidden = hidden.astype(bf16)
                base_stage[at, lanes] = hidden
                hidden = hidden.astype(f32)
                total = total + hidden * hidden
            partial[c : c + CHUNK, :] = total
        copy(i).start()
        total = jnp.sum(partial[...].T, axis=0, keepdims=True)
        at = pl.ds(start, tile)
        picks_gate = pick_rows(out_stage[at, :], onehot_t[...], rows)
        picks_res = pick_rows(res_stage[at, :], onehot_t[...], rows)
        for n in range(tile // LANES):
            block = i * (tile // LANES) + n
            sums[block] = total[:, n * LANES : (n + 1) * LANES]
            picked_gate[block] = picks_gate[n].astype(bf16)
            picked_res[block] = picks_res[n].astype(bf16)
        return 0

    lax.fori_loop(0, count, step, 0)
    lax.fori_loop(0, count, lambda i, _: (copy(i).wait(), 0)[1], 0)


def kept_kernel(conv, picked, skip_wide, *refs):
    hidden, totals = refs[-2:]
    owner_count, blocks = conv.shape[:2]
    first = 0
    for n in range(0, len(refs) - 2, 3):
        sums, picked_gate, picked_res = refs[n : n + 3]
        size = sums.shape[0]
        at_h = slice(first, first + size)
        total = jnp.zeros((size, LANES), f32)
        for s in range(conv.shape[2] // LANES):
            at = slice(s * owner_count, (s + 1) * owner_count)
            lanes = slice(s * LANES, (s + 1) * LANES)
            wide = jnp.swapaxes(conv[:, at_h, lanes].astype(f32), 0, 1)
            wide = wide + skip_wide[at, :] * picked[at_h, at, :].astype(f32)
            value = picked_res[:, at, :].astype(f32) + picked_gate[:, at, :].astype(f32) * wide
            value = value.astype(bf16)
            hidden[at_h, at, :] = value
            value = value.astype(f32)
            total = total + jnp.sum(value * value, axis=1)
        for i in range(size):
            totals[first + i] = total[i : i + 1, :] + sums[i]
        first = first + size


def hidden_kernel(base, hidden_kept, onehot, hidden, held, base_stage, base_sems, sems):
    slab = held.shape[1]
    wide = min(slab, 2 * LANES)
    count = sems.shape[0]
    tile = held.shape[0] // count
    wait, _ = fetch((base,), (base_stage,), base_sems, tile, 0, 3)

    def copy(i):
        rows = pl.ds(pl.multiple_of(i * tile, tile), tile)
        return pltpu.make_async_copy(held.at[rows, :], hidden.at[rows, :], sems.at[i])

    def step(i, _):
        blocks = range(tile // LANES)
        kept = [hidden_kept[i * (tile // LANES) + n].astype(f32).T.astype(bf16) for n in blocks]
        kept = jnp.concatenate(kept, axis=0)
        rows = pl.ds(wait(i), tile)
        for j in range(0, slab, wide):
            lanes = slice(j, j + wide)
            placed = dot(kept, onehot[:, lanes]).astype(bf16)
            held[rows, lanes] = base_stage[rows, lanes] + placed
        copy(i).start()
        return 0

    lax.fori_loop(0, count, step, 0)
    lax.fori_loop(0, count, lambda i, _: (copy(i).wait(), 0)[1], 0)


def norm_kernel(width, count, *refs):
    parts = refs[:count]
    held, gain, normed, stage, turned, sems = refs[count:]
    slab = held.shape[1]

    def copy(i):
        rows = pl.ds(pl.multiple_of(i * LANES, LANES), LANES)
        return pltpu.make_async_copy(stage.at[rows, :], normed.at[rows, :], sems.at[i])

    def step(i, _):
        total = parts[0][i]
        for part in parts[1:]:
            total = total + part[i]
        scale = lax.rsqrt(total / width + norm_eps)
        turned[...] = jnp.broadcast_to(scale, (LANES, LANES)).T
        first = pl.multiple_of(i * LANES, LANES)
        for c in range(0, LANES, CHUNK):
            at = pl.ds(first + c, CHUNK)
            scales = turned[c : c + CHUNK, :]
            for j in range(0, slab, LANES):
                lanes = slice(j, j + LANES)
                value = held[at, lanes].astype(f32) * scales * gain[:, lanes]
                stage[at, lanes] = value.astype(bf16)
        copy(i).start()
        return 0

    lax.fori_loop(0, sems.shape[0], step, 0)
    lax.fori_loop(0, sems.shape[0], lambda i, _: (copy(i).wait(), 0)[1], 0)


def in_hbm(x):
    return pltpu.with_memory_space_constraint(x, pltpu.HBM)


def in_vmem(x):
    return pltpu.with_memory_space_constraint(x, pltpu.VMEM)


def call(kernel, outs, ins, flops, moved, limit, scratch=(), far=(), far_outs=(), alias=None):
    near = pl.BlockSpec(memory_space=pltpu.VMEM)
    away = pl.BlockSpec(memory_space=pl.ANY)
    return pl.pallas_call(
        kernel,
        out_shape=outs,
        in_specs=[away if n in far else near for n in range(len(ins))],
        out_specs=[away if n in far_outs else near for n in range(len(outs))],
        scratch_shapes=list(scratch),
        input_output_aliases=alias or {},
        compiler_params=pltpu.CompilerParams(vmem_limit_bytes=limit),
        cost_estimate=pl.CostEstimate(flops=flops, bytes_accessed=moved, transcendentals=0),
    )(*ins)


def local(
    gate_in, value_in, out_gate, residual, filters, kept_index, kept_owner, skip_bias, norm_gain
):
    tok_rows, slab = gate_in.shape
    slots, length = filters.shape[2:]
    chan_devices = lax.axis_size("chan")
    owner_count = lax.axis_size("seqo") * lax.axis_size("seqi")
    rows = slots * owner_count
    lanes_rows = -(-rows // LANES) * LANES
    blocks = tok_rows // LANES
    outer = length // LANES
    tile = TILE if tok_rows % TILE == 0 else LANES
    dense = tok_rows * slab * 2
    sds = jax.ShapeDtypeStruct
    tables = [in_hbm(jnp.asarray(x)) for x in dft_tables(length)]
    outer_fwd, turn, inner, outer_back = tables
    skip_row = skip_bias[None, :]
    gain_row = norm_gain[None, :]
    gate_in, value_in, out_gate, residual = map(in_hbm, (gate_in, value_in, out_gate, residual))
    picks = sds((blocks, rows, LANES), bf16)
    row_sums = sds((blocks, 1, LANES), f32)
    buffer = (owner_count, blocks, slots * LANES)
    whole = (tok_rows, slab)

    payload, picked, channels, onehot_t = call(
        functools.partial(pick_kernel, owner_count, slots),
        [
            sds(buffer, bf16),
            picks,
            sds((8, lanes_rows), jnp.int32),
            pltpu.HBM((slab, lanes_rows), bf16),
        ],
        [in_hbm(kept_index), in_hbm(kept_owner), gate_in, value_in],
        2 * tok_rows * slab * rows,
        2 * dense,
        24 * MIB,
        scratch=[
            pltpu.VMEM((blocks, rows, LANES), f32),
            pltpu.VMEM(whole, bf16),
            pltpu.VMEM(whole, bf16),
            pltpu.VMEM((slab, lanes_rows), bf16),
            pltpu.VMEM((2,) + kept_index.shape, jnp.int32),
            pltpu.SemaphoreType.DMA((3,)),
            pltpu.SemaphoreType.DMA((2, tok_rows // tile)),
        ],
        far=(0, 1, 2, 3),
        far_outs=(3,),
    )

    incoming = lax.all_to_all(payload, ("seqo", "seqi"), split_axis=0, concat_axis=0, tiled=True)

    dense_ins = [gate_in, value_in, out_gate, residual]

    def base_parts(count):
        part = count * LANES
        outs = [
            pltpu.HBM(whole, bf16),
            sds((count, 1, LANES), f32),
            sds((count, rows, LANES), bf16),
            sds((count, rows, LANES), bf16),
        ]
        scratch = [pltpu.VMEM((part, slab), bf16)] * 5 + [
            pltpu.VMEM((LANES, LANES), f32),
            pltpu.SemaphoreType.DMA((count,)),
            pltpu.SemaphoreType.DMA((4, count)),
        ]
        return outs, scratch, 4 * part * slab * rows, 10 * part * slab

    early = max(1, blocks * EARLY // 16)
    outs, scratch, flops, moved = base_parts(early)
    spectrum = (slots, outer, 2 * LANES)
    onehot_t = in_hbm(onehot_t)
    table_ins = [in_hbm(filters[0, 0]), outer_fwd, turn, inner, onehot_t]
    onehot, others, skip_wide, spectra, base, *first_picks = call(
        first_kernel,
        [
            sds((rows, slab), bf16),
            sds((8, slab), f32),
            sds((rows, LANES), f32),
            pltpu.HBM(spectrum, f32),
        ]
        + outs,
        [channels] + table_ins + [skip_row] + dense_ins,
        flops,
        moved,
        36 * MIB,
        scratch=[pltpu.VMEM(x.shape, x.dtype) for x in table_ins]
        + [pltpu.VMEM(spectrum, f32), pltpu.SemaphoreType.DMA((len(table_ins) + slots,))]
        + scratch,
        far=(1, 2, 3, 4, 5, 7, 8, 9, 10),
        far_outs=(3, 4),
    )

    conv_ins = [incoming, outer_fwd, turn, inner, in_hbm(spectra), outer_back]
    (convolved,) = call(
        convolve_kernel,
        [pltpu.HBM(buffer, bf16)],
        conv_ins,
        2 * slots * length * 2 * (5 * outer + 12 * LANES),
        8 * MIB,
        20 * MIB,
        scratch=[pltpu.VMEM(x.shape, x.dtype) for x in conv_ins[1:]]
        + [pltpu.VMEM(buffer, bf16), pltpu.SemaphoreType.DMA((len(conv_ins) - 1 + slots,))],
        far=tuple(range(1, len(conv_ins))),
        far_outs=(0,),
    )
    convolved, onehot_t = lax.optimization_barrier((convolved, onehot_t))

    returned = lax.all_to_all(convolved, ("seqo", "seqi"), split_axis=0, concat_axis=0, tiled=True)

    outs, scratch, flops, moved = base_parts(blocks - early)
    base, *more_picks = call(
        functools.partial(second_kernel, early * LANES),
        outs,
        [in_hbm(onehot_t), others, skip_row] + dense_ins + [base],
        flops,
        moved,
        36 * MIB,
        scratch=[pltpu.VMEM(onehot_t.shape, bf16), pltpu.SemaphoreType.DMA((1,))] + scratch,
        far=(0, 3, 4, 5, 6, 7),
        far_outs=(0,),
        alias={7: 0},
    )

    hidden_kept, totals = call(
        kept_kernel,
        [picks, row_sums],
        [returned, picked, skip_wide, *first_picks, *more_picks],
        8 * rows * tok_rows,
        10 * rows * tok_rows,
        16 * MIB,
    )

    parts = [totals]
    for shift in range(1, chan_devices):
        ring = [(i, (i + shift) % chan_devices) for i in range(chan_devices)]
        parts.append(lax.ppermute(totals, "chan", ring))

    hidden, held = call(
        hidden_kernel,
        [pltpu.HBM(whole, bf16), pltpu.VMEM(whole, bf16)],
        [in_hbm(base), hidden_kept, onehot],
        2 * tok_rows * slab * rows,
        2 * dense,
        16 * MIB,
        scratch=[
            pltpu.VMEM(whole, bf16),
            pltpu.SemaphoreType.DMA((1, tok_rows // tile)),
            pltpu.SemaphoreType.DMA((tok_rows // tile,)),
        ],
        far=(0,),
        far_outs=(0,),
    )
    (normed,) = call(
        functools.partial(norm_kernel, float(slab * chan_devices), len(parts)),
        [pltpu.HBM(whole, bf16)],
        parts + [in_vmem(held), gain_row],
        4 * tok_rows * slab,
        2 * dense,
        16 * MIB,
        scratch=[
            pltpu.VMEM(whole, bf16),
            pltpu.VMEM((LANES, LANES), f32),
            pltpu.SemaphoreType.DMA((blocks,)),
        ],
        far_outs=(0,),
    )
    return (hidden, normed)


def solution(mesh):
    positions = P(("seqo", "seqi"), "chan")
    in_specs = (
        positions,
        positions,
        positions,
        positions,
        P("chan", ("seqo", "seqi"), None, None),
        P("chan", None),
        P("chan", None),
        P("chan"),
        P("chan"),
    )
    return jax.shard_map(
        local, mesh=mesh, in_specs=in_specs, out_specs=(positions, positions), check_vma=False
    )
```

```python
import functools

import jax
import jax.numpy as jnp
import numpy as np
from jax import lax
from jax.experimental import pallas as pl
from jax.experimental.pallas import tpu as pltpu
from jax.sharding import PartitionSpec as P

LANES = 128
TILE = 256
CHUNK = 16
GROUP = 3
EARLY = 7
MIB = 1 << 20
norm_eps = 1e-06
f32 = jnp.float32
bf16 = jnp.bfloat16


def split_np(table):
    high = table.astype(jnp.bfloat16)
    low = (table - high.astype(np.float64)).astype(jnp.bfloat16)
    return high, low


def dft_tables(length):
    inner = LANES
    outer = length // inner
    a = np.arange(outer)
    b = np.arange(inner)
    quarter = np.arange(outer) + 0.25
    outer_angle = 2 * np.pi / outer * np.mod(quarter[:, None] * a[None, :], outer)
    turn_angle = 2 * np.pi / length * (quarter[:, None] * b[None, :])
    inner_angle = 2 * np.pi / inner * np.mod(b[:, None] * b[None, :], inner)
    outer_fwd = np.concatenate([np.cos(outer_angle), -np.sin(outer_angle)], axis=0)
    c, s = np.cos(inner_angle), np.sin(inner_angle)
    inner_fwd = np.concatenate(
        [np.concatenate([c, -s], axis=1), np.concatenate([s, c], axis=1)], axis=0
    )
    inner_back = np.concatenate(
        [np.concatenate([c, s], axis=1), np.concatenate([-s, c], axis=1)], axis=0
    )
    outer_back = np.concatenate([np.cos(outer_angle).T, -np.sin(outer_angle).T], axis=1) / length
    turn = np.concatenate([np.cos(turn_angle), np.sin(turn_angle)], axis=1).astype(np.float32)
    outer_fwd = np.concatenate(split_np(outer_fwd), axis=1)
    inner = np.concatenate(split_np(inner_fwd) + split_np(inner_back), axis=0)
    outer_back = np.concatenate(split_np(outer_back), axis=1)
    return outer_fwd, turn, inner, outer_back


def split(value):
    high = value.astype(bf16)
    low = (value - high.astype(f32)).astype(bf16)
    return high, low


def dot(x, y):
    return jnp.dot(x, y, preferred_element_type=f32)


def dot_rows(x, y):
    return lax.dot_general(x, y, (((0,), (0,)), ((), ())), preferred_element_type=f32)


def times_table(value, table):
    high, low = split(value)
    depth = value.shape[1]
    stacked = jnp.concatenate([table, table[:depth]], axis=0)
    return dot(jnp.concatenate([high, high, low], axis=1), stacked)


def table_times(table, value):
    high, low = split(value)
    depth = value.shape[0]
    stacked = jnp.concatenate([table, table[:, :depth]], axis=1)
    return dot(stacked, jnp.concatenate([high, high, low], axis=0))


def to_spectrum(blocks, slots, outer_fwd, turn, inner_fwd):
    outer = blocks.shape[0]
    first = dot(outer_fwd, jnp.concatenate([blocks, blocks], axis=0))
    turn, inner_fwd = turn(), inner_fwd()
    cos, sin = turn[:, :LANES], turn[:, LANES:]
    turned = []
    for s in range(slots):
        re = first[:outer, s * LANES : (s + 1) * LANES]
        im = first[outer:, s * LANES : (s + 1) * LANES]
        turned.append(jnp.concatenate([re * cos + im * sin, im * cos - re * sin], axis=1))
    return grouped(turned, inner_fwd)


def grouped(values, table):
    result = []
    for s in range(0, len(values), GROUP):
        part = values[s : s + GROUP]
        size = part[0].shape[0]
        product = times_table(jnp.concatenate(part, axis=0), table)
        result += [product[n * size : (n + 1) * size] for n in range(len(part))]
    return result


def filter_spectra(filters, outer_fwd, turn, inner):
    slots, length = filters.shape
    outer = length // LANES
    wide = filters[...].astype(f32)
    blocks = [wide[s].reshape(outer, LANES) for s in range(slots)]
    blocks = jnp.concatenate(blocks, axis=1).astype(bf16)
    return to_spectrum(
        blocks, slots, outer_fwd[...], lambda: turn[...], lambda: inner[: 4 * LANES, :]
    )


def convolve_kernel(
    signals, outer_fwd_far, turn_far, inner_far, spectra_far, outer_back_far, out, *scratch
):
    sources = (outer_fwd_far, turn_far, inner_far, spectra_far, outer_back_far)
    outer_fwd, turn_ref, inner, spectra, outer_back, result, sems = scratch
    copies = [
        pltpu.make_async_copy(source, scratch[n], sems.at[n]) for n, source in enumerate(sources)
    ]
    for copy in copies:
        copy.start()
    slots, outer = spectra.shape[:2]

    def turn_now():
        copies[1].wait()
        return turn_ref[...]

    def inner_now():
        copies[2].wait()
        return inner[: 4 * LANES, :]

    copies[0].wait()
    blocks = signals[...].reshape(outer, slots * LANES)
    parts = to_spectrum(blocks, slots, outer_fwd[...], turn_now, inner_now)
    turn = turn_ref[...]
    cos, sin = turn[:, :LANES], turn[:, LANES:]
    copies[3].wait()
    joint = []
    for s in range(slots):
        sig_re, sig_im = parts[s][:, :LANES], parts[s][:, LANES:]
        ker_re, ker_im = spectra[s, :, :LANES], spectra[s, :, LANES:]
        joint.append(
            jnp.concatenate(
                [sig_re * ker_re - sig_im * ker_im, sig_re * ker_im + sig_im * ker_re], axis=1
            )
        )
    turned = []
    for back in grouped(joint, inner[4 * LANES :, :]):
        re, im = back[:, :LANES], back[:, LANES:]
        turned.append(jnp.concatenate([re * cos - im * sin, im * cos + re * sin], axis=0))
    copies[4].wait()
    sends = []
    for s in range(0, slots, 2):
        pair = turned[s : s + 2]
        causal = table_times(outer_back[...], jnp.concatenate(pair, axis=1)).astype(bf16)
        lanes = pl.ds(s * LANES, len(pair) * LANES)
        result[:, :, lanes] = causal.reshape(out.shape[:2] + (len(pair) * LANES,))
        sends.append(
            pltpu.make_async_copy(
                result.at[:, :, lanes], out.at[:, :, lanes], sems.at[len(copies) + len(sends)]
            )
        )
        sends[-1].start()
    for send in sends:
        send.wait()


def iota(shape, axis):
    return lax.broadcasted_iota(jnp.int32, shape, axis)


def to_column(row):
    size = row.shape[1]
    same = iota((size, size), 0) == iota((size, size), 1)
    return jnp.sum(jnp.where(same, row, 0), axis=1, keepdims=True)


def channel_of_row(index_row, owners_row, owner_count, rows):
    slots = owners_row.shape[1]
    owners_col = to_column(owners_row)
    index_col = to_column(index_row)
    earlier = (owners_col == owners_row) & (iota((slots, slots), 1) < iota((slots, slots), 0))
    rank_col = jnp.sum(earlier.astype(jnp.int32), axis=1, keepdims=True)
    target_col = jnp.where(owners_col >= 0, rank_col * owner_count + owners_col, -1)
    hit = target_col == iota((slots, rows), 1)
    return jnp.sum(jnp.where(hit, index_col + 1, 0), axis=0, keepdims=True) - 1


def pick_rows(tile, onehot_t, rows):
    picked = dot(tile, onehot_t).T
    return [picked[:rows, i : i + LANES] for i in range(0, tile.shape[0], LANES)]


def fetch(sources, stages, sems, tile, first=0, ahead=4):
    count = stages[0].shape[0] // tile

    def copies(i):
        at = pl.multiple_of(i * tile, tile)
        return [
            pltpu.make_async_copy(
                source.at[pl.ds(first + at, tile), :], stage.at[pl.ds(at, tile), :], sems.at[n, i]
            )
            for n, (source, stage) in enumerate(zip(sources, stages))
        ]

    def start(i):
        for copy in copies(i):
            copy.start()

    for i in range(min(ahead, count)):
        start(i)

    def wait(i):
        for copy in copies(i):
            copy.wait()

        @pl.when(i + ahead < count)
        def _():
            start(i + ahead)

        return pl.multiple_of(i * tile, tile)

    return wait, count


def pick_kernel(owner_count, slots, index, owners, gate, value, *refs):
    payload, picked, channels, onehot_far = refs[:4]
    acc, gate_stage, value_stage, onehot_t, lists, list_sems, sems = refs[4:]
    rows = owner_count * slots
    tile = gate_stage.shape[0] // sems.shape[1]
    list_copies = [
        pltpu.make_async_copy(source, lists.at[n], list_sems.at[n])
        for n, source in enumerate((index, owners))
    ]
    for copy in list_copies:
        copy.start()
    wait, count = fetch((gate, value), (gate_stage, value_stage), sems, tile)
    for copy in list_copies:
        copy.wait()
    row = channel_of_row(lists[0], lists[1], owner_count, onehot_t.shape[1])
    channels[...] = jnp.broadcast_to(row, channels.shape)
    onehot_t[...] = (iota(onehot_t.shape, 0) == row).astype(f32).astype(bf16)
    onehot_copy = pltpu.make_async_copy(onehot_t, onehot_far, list_sems.at[2])
    onehot_copy.start()

    def step(i, _):
        at = pl.ds(wait(i), tile)
        gated = gate_stage[at, :] * value_stage[at, :]
        for n, block in enumerate(pick_rows(gated, onehot_t[...], rows)):
            acc[i * (tile // LANES) + n] = block
            picked[i * (tile // LANES) + n] = block.astype(bf16)
        return 0

    lax.fori_loop(0, count, step, 0)
    for s in range(slots):
        part = jnp.swapaxes(acc[:, s * owner_count : (s + 1) * owner_count, :], 0, 1)
        payload[:, :, s * LANES : (s + 1) * LANES] = part.astype(bf16)
    onehot_copy.wait()


def first_kernel(channels, filters_far, outer_fwd_far, turn_far, inner_far, *refs):
    onehot_far, skip, *dense = refs[:6]
    onehot, others, skip_wide, spectra, *outs = refs[6:14]
    filters, outer_fwd, turn, inner, onehot_t, spectra_stage, table_sems = refs[14:21]
    sources = (filters_far, outer_fwd_far, turn_far, inner_far, onehot_far)
    stages = (filters, outer_fwd, turn, inner, onehot_t)
    tables = [
        pltpu.make_async_copy(source, stage, table_sems.at[n])
        for n, (source, stage) in enumerate(zip(sources, stages))
    ]
    for copy in tables:
        copy.start()
    hit = iota(onehot.shape, 1) == to_column(channels[0:1, :])[: onehot.shape[0]]
    onehot[...] = hit.astype(f32).astype(bf16)
    kept = jnp.max(hit.astype(f32), axis=0, keepdims=True)
    others[...] = jnp.broadcast_to(1.0 - kept, others.shape)
    skip_col = jnp.sum(jnp.where(hit, skip[...], 0.0), axis=1, keepdims=True)
    skip_wide[...] = jnp.broadcast_to(skip_col, skip_wide.shape)

    def send(s):
        return pltpu.make_async_copy(
            spectra_stage.at[s], spectra.at[s], table_sems.at[len(tables) + s]
        )

    def beside():
        for copy in tables:
            copy.wait()
        for s, part in enumerate(filter_spectra(filters, outer_fwd, turn, inner)):
            spectra_stage[s] = part
            send(s).start()

    base_pass(0, onehot_t, others, skip, dense, outs, refs[21:], beside, 4)
    for s in range(spectra.shape[0]):
        send(s).wait()


def second_kernel(first, onehot_far, others, skip, *refs):
    onehot_t, onehot_sem = refs[9:11]
    copy = pltpu.make_async_copy(onehot_far, onehot_t, onehot_sem.at[0])
    copy.start()
    base_pass(first, onehot_t, others, skip, refs[:4], refs[5:9], refs[11:], copy.wait, 4)


def base_pass(first, onehot_t, others, skip, dense, outs, scratch, beside, ahead):
    base, sums, picked_gate, picked_res = outs
    stages = scratch[:4]
    base_stage, partial, base_sems, sems = scratch[4:]
    gate_stage, value_stage, out_stage, res_stage = stages
    rows = picked_gate.shape[1]
    slab = gate_stage.shape[1]
    tile = partial.shape[0]
    wait, count = fetch(dense, stages, sems, tile, first, ahead)
    beside()

    def copy(i):
        at = pl.multiple_of(i * tile, tile)
        return pltpu.make_async_copy(
            base_stage.at[pl.ds(at, tile), :], base.at[pl.ds(first + at, tile), :], base_sems.at[i]
        )

    def step(i, _):
        start = wait(i)
        for c in range(0, tile, CHUNK):
            at = pl.ds(start + c, CHUNK)
            total = jnp.zeros((CHUNK, LANES), f32)
            for j in range(0, slab, LANES):
                lanes = slice(j, j + LANES)
                gated = (gate_stage[at, lanes] * value_stage[at, lanes]).astype(f32)
                mixed = out_stage[at, lanes].astype(f32) * (skip[:, lanes] * gated)
                hidden = (res_stage[at, lanes].astype(f32) + mixed) * others[0:1, lanes]
                hidden = hidden.astype(bf16)
                base_stage[at, lanes] = hidden
                hidden = hidden.astype(f32)
                total = total + hidden * hidden
            partial[c : c + CHUNK, :] = total
        copy(i).start()
        total = jnp.sum(partial[...].T, axis=0, keepdims=True)
        at = pl.ds(start, tile)
        picks_gate = pick_rows(out_stage[at, :], onehot_t[...], rows)
        picks_res = pick_rows(res_stage[at, :], onehot_t[...], rows)
        for n in range(tile // LANES):
            block = i * (tile // LANES) + n
            sums[block] = total[:, n * LANES : (n + 1) * LANES]
            picked_gate[block] = picks_gate[n].astype(bf16)
            picked_res[block] = picks_res[n].astype(bf16)
        return 0

    lax.fori_loop(0, count, step, 0)
    lax.fori_loop(0, count, lambda i, _: (copy(i).wait(), 0)[1], 0)


def kept_kernel(conv, picked, skip_wide, *refs):
    hidden, totals = refs[-2:]
    owner_count, blocks = conv.shape[:2]
    first = 0
    for n in range(0, len(refs) - 2, 3):
        sums, picked_gate, picked_res = refs[n : n + 3]
        size = sums.shape[0]
        at_h = slice(first, first + size)
        total = jnp.zeros((size, LANES), f32)
        for s in range(conv.shape[2] // LANES):
            at = slice(s * owner_count, (s + 1) * owner_count)
            lanes = slice(s * LANES, (s + 1) * LANES)
            wide = jnp.swapaxes(conv[:, at_h, lanes].astype(f32), 0, 1)
            wide = wide + skip_wide[at, :] * picked[at_h, at, :].astype(f32)
            value = picked_res[:, at, :].astype(f32) + picked_gate[:, at, :].astype(f32) * wide
            value = value.astype(bf16)
            hidden[at_h, at, :] = value
            value = value.astype(f32)
            total = total + jnp.sum(value * value, axis=1)
        for i in range(size):
            totals[first + i] = total[i : i + 1, :] + sums[i]
        first = first + size


def hidden_kernel(base, hidden_kept, onehot, hidden, held, base_stage, base_sems, sems):
    slab = held.shape[1]
    wide = min(slab, 2 * LANES)
    count = sems.shape[0]
    tile = held.shape[0] // count
    wait, _ = fetch((base,), (base_stage,), base_sems, tile)

    def copy(i):
        rows = pl.ds(pl.multiple_of(i * tile, tile), tile)
        return pltpu.make_async_copy(held.at[rows, :], hidden.at[rows, :], sems.at[i])

    def step(i, _):
        blocks = range(tile // LANES)
        kept = [hidden_kept[i * (tile // LANES) + n].astype(f32).T.astype(bf16) for n in blocks]
        kept = jnp.concatenate(kept, axis=0)
        rows = pl.ds(wait(i), tile)
        for j in range(0, slab, wide):
            lanes = slice(j, j + wide)
            placed = dot(kept, onehot[:, lanes]).astype(bf16)
            held[rows, lanes] = base_stage[rows, lanes] + placed
        copy(i).start()
        return 0

    lax.fori_loop(0, count, step, 0)
    lax.fori_loop(0, count, lambda i, _: (copy(i).wait(), 0)[1], 0)


def norm_kernel(width, count, *refs):
    parts = refs[:count]
    held, gain, normed, stage, turned, sems = refs[count:]
    slab = held.shape[1]

    def copy(i):
        rows = pl.ds(pl.multiple_of(i * LANES, LANES), LANES)
        return pltpu.make_async_copy(stage.at[rows, :], normed.at[rows, :], sems.at[i])

    def step(i, _):
        total = parts[0][i]
        for part in parts[1:]:
            total = total + part[i]
        scale = lax.rsqrt(total / width + norm_eps)
        turned[...] = jnp.broadcast_to(scale, (LANES, LANES)).T
        first = pl.multiple_of(i * LANES, LANES)
        for c in range(0, LANES, CHUNK):
            at = pl.ds(first + c, CHUNK)
            scales = turned[c : c + CHUNK, :]
            for j in range(0, slab, LANES):
                lanes = slice(j, j + LANES)
                value = held[at, lanes].astype(f32) * scales * gain[:, lanes]
                stage[at, lanes] = value.astype(bf16)
        copy(i).start()
        return 0

    lax.fori_loop(0, sems.shape[0], step, 0)
    lax.fori_loop(0, sems.shape[0], lambda i, _: (copy(i).wait(), 0)[1], 0)


def in_hbm(x):
    return pltpu.with_memory_space_constraint(x, pltpu.HBM)


def in_vmem(x):
    return pltpu.with_memory_space_constraint(x, pltpu.VMEM)


def call(kernel, outs, ins, flops, moved, limit, scratch=(), far=(), far_outs=(), alias=None):
    near = pl.BlockSpec(memory_space=pltpu.VMEM)
    away = pl.BlockSpec(memory_space=pl.ANY)
    return pl.pallas_call(
        kernel,
        out_shape=outs,
        in_specs=[away if n in far else near for n in range(len(ins))],
        out_specs=[away if n in far_outs else near for n in range(len(outs))],
        scratch_shapes=list(scratch),
        input_output_aliases=alias or {},
        compiler_params=pltpu.CompilerParams(vmem_limit_bytes=limit),
        cost_estimate=pl.CostEstimate(flops=flops, bytes_accessed=moved, transcendentals=0),
    )(*ins)


def local(
    gate_in, value_in, out_gate, residual, filters, kept_index, kept_owner, skip_bias, norm_gain
):
    tok_rows, slab = gate_in.shape
    slots, length = filters.shape[2:]
    chan_devices = lax.axis_size("chan")
    owner_count = lax.axis_size("seqo") * lax.axis_size("seqi")
    rows = slots * owner_count
    lanes_rows = -(-rows // LANES) * LANES
    blocks = tok_rows // LANES
    outer = length // LANES
    tile = TILE if tok_rows % TILE == 0 else LANES
    dense = tok_rows * slab * 2
    sds = jax.ShapeDtypeStruct
    tables = [in_hbm(jnp.asarray(x)) for x in dft_tables(length)]
    outer_fwd, turn, inner, outer_back = tables
    skip_row = skip_bias[None, :]
    gain_row = norm_gain[None, :]
    gate_in, value_in, out_gate, residual = map(in_hbm, (gate_in, value_in, out_gate, residual))
    picks = sds((blocks, rows, LANES), bf16)
    row_sums = sds((blocks, 1, LANES), f32)
    buffer = (owner_count, blocks, slots * LANES)
    whole = (tok_rows, slab)

    payload, picked, channels, onehot_t = call(
        functools.partial(pick_kernel, owner_count, slots),
        [
            sds(buffer, bf16),
            picks,
            sds((8, lanes_rows), jnp.int32),
            pltpu.HBM((slab, lanes_rows), bf16),
        ],
        [in_hbm(kept_index), in_hbm(kept_owner), gate_in, value_in],
        2 * tok_rows * slab * rows,
        2 * dense,
        24 * MIB,
        scratch=[
            pltpu.VMEM((blocks, rows, LANES), f32),
            pltpu.VMEM(whole, bf16),
            pltpu.VMEM(whole, bf16),
            pltpu.VMEM((slab, lanes_rows), bf16),
            pltpu.VMEM((2,) + kept_index.shape, jnp.int32),
            pltpu.SemaphoreType.DMA((3,)),
            pltpu.SemaphoreType.DMA((2, tok_rows // tile)),
        ],
        far=(0, 1, 2, 3),
        far_outs=(3,),
    )

    incoming = lax.all_to_all(payload, ("seqo", "seqi"), split_axis=0, concat_axis=0, tiled=True)

    dense_ins = [gate_in, value_in, out_gate, residual]

    def base_parts(count):
        part = count * LANES
        outs = [
            pltpu.HBM(whole, bf16),
            sds((count, 1, LANES), f32),
            sds((count, rows, LANES), bf16),
            sds((count, rows, LANES), bf16),
        ]
        scratch = [pltpu.VMEM((part, slab), bf16)] * 5 + [
            pltpu.VMEM((LANES, LANES), f32),
            pltpu.SemaphoreType.DMA((count,)),
            pltpu.SemaphoreType.DMA((4, count)),
        ]
        return outs, scratch, 4 * part * slab * rows, 10 * part * slab

    early = max(1, blocks * EARLY // 16)
    outs, scratch, flops, moved = base_parts(early)
    spectrum = (slots, outer, 2 * LANES)
    onehot_t = in_hbm(onehot_t)
    table_ins = [in_hbm(filters[0, 0]), outer_fwd, turn, inner, onehot_t]
    onehot, others, skip_wide, spectra, base, *first_picks = call(
        first_kernel,
        [
            sds((rows, slab), bf16),
            sds((8, slab), f32),
            sds((rows, LANES), f32),
            pltpu.HBM(spectrum, f32),
        ]
        + outs,
        [channels] + table_ins + [skip_row] + dense_ins,
        flops,
        moved,
        36 * MIB,
        scratch=[pltpu.VMEM(x.shape, x.dtype) for x in table_ins]
        + [pltpu.VMEM(spectrum, f32), pltpu.SemaphoreType.DMA((len(table_ins) + slots,))]
        + scratch,
        far=(1, 2, 3, 4, 5, 7, 8, 9, 10),
        far_outs=(3, 4),
    )

    conv_ins = [incoming, outer_fwd, turn, inner, in_hbm(spectra), outer_back]
    (convolved,) = call(
        convolve_kernel,
        [pltpu.HBM(buffer, bf16)],
        conv_ins,
        2 * slots * length * 2 * (5 * outer + 12 * LANES),
        8 * MIB,
        20 * MIB,
        scratch=[pltpu.VMEM(x.shape, x.dtype) for x in conv_ins[1:]]
        + [pltpu.VMEM(buffer, bf16), pltpu.SemaphoreType.DMA((len(conv_ins) - 1 + slots,))],
        far=tuple(range(1, len(conv_ins))),
        far_outs=(0,),
    )
    convolved, onehot_t = lax.optimization_barrier((convolved, onehot_t))

    returned = lax.all_to_all(convolved, ("seqo", "seqi"), split_axis=0, concat_axis=0, tiled=True)

    outs, scratch, flops, moved = base_parts(blocks - early)
    base, *more_picks = call(
        functools.partial(second_kernel, early * LANES),
        outs,
        [in_hbm(onehot_t), others, skip_row] + dense_ins + [base],
        flops,
        moved,
        36 * MIB,
        scratch=[pltpu.VMEM(onehot_t.shape, bf16), pltpu.SemaphoreType.DMA((1,))] + scratch,
        far=(0, 3, 4, 5, 6, 7),
        far_outs=(0,),
        alias={7: 0},
    )

    hidden_kept, totals = call(
        kept_kernel,
        [picks, row_sums],
        [returned, picked, skip_wide, *first_picks, *more_picks],
        8 * rows * tok_rows,
        10 * rows * tok_rows,
        16 * MIB,
    )

    parts = [totals]
    for shift in range(1, chan_devices):
        ring = [(i, (i + shift) % chan_devices) for i in range(chan_devices)]
        parts.append(lax.ppermute(totals, "chan", ring))

    hidden, held = call(
        hidden_kernel,
        [pltpu.HBM(whole, bf16), pltpu.VMEM(whole, bf16)],
        [in_hbm(base), hidden_kept, onehot],
        2 * tok_rows * slab * rows,
        2 * dense,
        16 * MIB,
        scratch=[
            pltpu.VMEM(whole, bf16),
            pltpu.SemaphoreType.DMA((1, tok_rows // tile)),
            pltpu.SemaphoreType.DMA((tok_rows // tile,)),
        ],
        far=(0,),
        far_outs=(0,),
    )
    (normed,) = call(
        functools.partial(norm_kernel, float(slab * chan_devices), len(parts)),
        [pltpu.HBM(whole, bf16)],
        parts + [in_vmem(held), gain_row],
        4 * tok_rows * slab,
        2 * dense,
        16 * MIB,
        scratch=[
            pltpu.VMEM(whole, bf16),
            pltpu.VMEM((LANES, LANES), f32),
            pltpu.SemaphoreType.DMA((blocks,)),
        ],
        far_outs=(0,),
    )
    return (hidden, normed)


def solution(mesh):
    positions = P(("seqo", "seqi"), "chan")
    in_specs = (
        positions,
        positions,
        positions,
        positions,
        P("chan", ("seqo", "seqi"), None, None),
        P("chan", None),
        P("chan", None),
        P("chan"),
        P("chan"),
    )
    return jax.shard_map(
        local, mesh=mesh, in_specs=in_specs, out_specs=(positions, positions), check_vma=False
    )
```

```python
import functools

import jax
import jax.numpy as jnp
import numpy as np
from jax import lax
from jax.experimental import pallas as pl
from jax.experimental.pallas import tpu as pltpu
from jax.sharding import PartitionSpec as P

LANES = 128
TILE = 256
CHUNK = 16
GROUP = 3
EARLY = 7
MIB = 1 << 20
norm_eps = 1e-06
f32 = jnp.float32
bf16 = jnp.bfloat16


def split_np(table):
    high = table.astype(jnp.bfloat16)
    low = (table - high.astype(np.float64)).astype(jnp.bfloat16)
    return high, low


def dft_tables(length):
    inner = LANES
    outer = length // inner
    a = np.arange(outer)
    b = np.arange(inner)
    quarter = np.arange(outer) + 0.25
    outer_angle = 2 * np.pi / outer * np.mod(quarter[:, None] * a[None, :], outer)
    turn_angle = 2 * np.pi / length * (quarter[:, None] * b[None, :])
    inner_angle = 2 * np.pi / inner * np.mod(b[:, None] * b[None, :], inner)
    outer_fwd = np.concatenate([np.cos(outer_angle), -np.sin(outer_angle)], axis=0)
    c, s = np.cos(inner_angle), np.sin(inner_angle)
    inner_fwd = np.concatenate(
        [np.concatenate([c, -s], axis=1), np.concatenate([s, c], axis=1)], axis=0
    )
    inner_back = np.concatenate(
        [np.concatenate([c, s], axis=1), np.concatenate([-s, c], axis=1)], axis=0
    )
    outer_back = np.concatenate([np.cos(outer_angle).T, -np.sin(outer_angle).T], axis=1) / length
    turn = np.concatenate([np.cos(turn_angle), np.sin(turn_angle)], axis=1).astype(np.float32)
    outer_fwd = np.concatenate(split_np(outer_fwd), axis=1)
    inner = np.concatenate(split_np(inner_fwd) + split_np(inner_back), axis=0)
    outer_back = np.concatenate(split_np(outer_back), axis=1)
    return outer_fwd, turn, inner, outer_back


def split(value):
    high = value.astype(bf16)
    low = (value - high.astype(f32)).astype(bf16)
    return high, low


def dot(x, y):
    return jnp.dot(x, y, preferred_element_type=f32)


def dot_rows(x, y):
    return lax.dot_general(x, y, (((0,), (0,)), ((), ())), preferred_element_type=f32)


def times_table(value, table):
    high, low = split(value)
    depth = value.shape[1]
    stacked = jnp.concatenate([table, table[:depth]], axis=0)
    return dot(jnp.concatenate([high, high, low], axis=1), stacked)


def table_times(table, value):
    high, low = split(value)
    depth = value.shape[0]
    stacked = jnp.concatenate([table, table[:, :depth]], axis=1)
    return dot(stacked, jnp.concatenate([high, high, low], axis=0))


def to_spectrum(blocks, slots, outer_fwd, turn, inner_fwd):
    outer = blocks.shape[0]
    first = dot(outer_fwd, jnp.concatenate([blocks, blocks], axis=0))
    turn, inner_fwd = turn(), inner_fwd()
    cos, sin = turn[:, :LANES], turn[:, LANES:]
    turned = []
    for s in range(slots):
        re = first[:outer, s * LANES : (s + 1) * LANES]
        im = first[outer:, s * LANES : (s + 1) * LANES]
        turned.append(jnp.concatenate([re * cos + im * sin, im * cos - re * sin], axis=1))
    return grouped(turned, inner_fwd)


def grouped(values, table):
    result = []
    for s in range(0, len(values), GROUP):
        part = values[s : s + GROUP]
        size = part[0].shape[0]
        product = times_table(jnp.concatenate(part, axis=0), table)
        result += [product[n * size : (n + 1) * size] for n in range(len(part))]
    return result


def filter_spectra(filters, outer_fwd, turn, inner):
    slots, length = filters.shape
    outer = length // LANES
    wide = filters[...].astype(f32)
    blocks = [wide[s].reshape(outer, LANES) for s in range(slots)]
    blocks = jnp.concatenate(blocks, axis=1).astype(bf16)
    return to_spectrum(
        blocks, slots, outer_fwd[...], lambda: turn[...], lambda: inner[: 4 * LANES, :]
    )


def convolve_kernel(
    signals, outer_fwd_far, turn_far, inner_far, spectra_far, outer_back_far, out, *scratch
):
    sources = (outer_fwd_far, turn_far, inner_far, spectra_far, outer_back_far)
    outer_fwd, turn_ref, inner, spectra, outer_back, result, sems = scratch
    copies = [
        pltpu.make_async_copy(source, scratch[n], sems.at[n]) for n, source in enumerate(sources)
    ]
    for copy in copies:
        copy.start()
    slots, outer = spectra.shape[:2]

    def turn_now():
        copies[1].wait()
        return turn_ref[...]

    def inner_now():
        copies[2].wait()
        return inner[: 4 * LANES, :]

    copies[0].wait()
    blocks = signals[...].reshape(outer, slots * LANES)
    parts = to_spectrum(blocks, slots, outer_fwd[...], turn_now, inner_now)
    turn = turn_ref[...]
    cos, sin = turn[:, :LANES], turn[:, LANES:]
    copies[3].wait()
    joint = []
    for s in range(slots):
        sig_re, sig_im = parts[s][:, :LANES], parts[s][:, LANES:]
        ker_re, ker_im = spectra[s, :, :LANES], spectra[s, :, LANES:]
        joint.append(
            jnp.concatenate(
                [sig_re * ker_re - sig_im * ker_im, sig_re * ker_im + sig_im * ker_re], axis=1
            )
        )
    turned = []
    for back in grouped(joint, inner[4 * LANES :, :]):
        re, im = back[:, :LANES], back[:, LANES:]
        turned.append(jnp.concatenate([re * cos - im * sin, im * cos + re * sin], axis=0))
    copies[4].wait()
    sends = []
    for s in range(0, slots, 2):
        pair = turned[s : s + 2]
        causal = table_times(outer_back[...], jnp.concatenate(pair, axis=1)).astype(bf16)
        lanes = pl.ds(s * LANES, len(pair) * LANES)
        result[:, :, lanes] = causal.reshape(out.shape[:2] + (len(pair) * LANES,))
        sends.append(
            pltpu.make_async_copy(
                result.at[:, :, lanes], out.at[:, :, lanes], sems.at[len(copies) + len(sends)]
            )
        )
        sends[-1].start()
    for send in sends:
        send.wait()


def iota(shape, axis):
    return lax.broadcasted_iota(jnp.int32, shape, axis)


def to_column(row):
    size = row.shape[1]
    same = iota((size, size), 0) == iota((size, size), 1)
    return jnp.sum(jnp.where(same, row, 0), axis=1, keepdims=True)


def channel_of_row(index_row, owners_row, owner_count, rows):
    slots = owners_row.shape[1]
    owners_col = to_column(owners_row)
    index_col = to_column(index_row)
    earlier = (owners_col == owners_row) & (iota((slots, slots), 1) < iota((slots, slots), 0))
    rank_col = jnp.sum(earlier.astype(jnp.int32), axis=1, keepdims=True)
    target_col = jnp.where(owners_col >= 0, rank_col * owner_count + owners_col, -1)
    hit = target_col == iota((slots, rows), 1)
    return jnp.sum(jnp.where(hit, index_col + 1, 0), axis=0, keepdims=True) - 1


def pick_rows(tile, onehot_t, rows):
    picked = dot(tile, onehot_t).T
    return [picked[:rows, i : i + LANES] for i in range(0, tile.shape[0], LANES)]


def fetch(sources, stages, sems, tile, first=0, ahead=4):
    count = stages[0].shape[0] // tile

    def copies(i):
        at = pl.multiple_of(i * tile, tile)
        return [
            pltpu.make_async_copy(
                source.at[pl.ds(first + at, tile), :], stage.at[pl.ds(at, tile), :], sems.at[n, i]
            )
            for n, (source, stage) in enumerate(zip(sources, stages))
        ]

    def start(i):
        for copy in copies(i):
            copy.start()

    for i in range(min(ahead, count)):
        start(i)

    def wait(i):
        for copy in copies(i):
            copy.wait()

        @pl.when(i + ahead < count)
        def _():
            start(i + ahead)

        return pl.multiple_of(i * tile, tile)

    return wait, count


def pick_kernel(owner_count, slots, index, owners, gate, value, *refs):
    payload, picked, channels, onehot_t = refs[:4]
    acc, gate_stage, value_stage, lists, list_sems, sems = refs[4:]
    rows = owner_count * slots
    tile = gate_stage.shape[0] // sems.shape[1]
    list_copies = [
        pltpu.make_async_copy(source, lists.at[n], list_sems.at[n])
        for n, source in enumerate((index, owners))
    ]
    for copy in list_copies:
        copy.start()
    wait, count = fetch((gate, value), (gate_stage, value_stage), sems, tile)
    for copy in list_copies:
        copy.wait()
    row = channel_of_row(lists[0], lists[1], owner_count, onehot_t.shape[1])
    channels[...] = jnp.broadcast_to(row, channels.shape)
    onehot_t[...] = (iota(onehot_t.shape, 0) == row).astype(f32).astype(bf16)

    def step(i, _):
        at = pl.ds(wait(i), tile)
        gated = gate_stage[at, :] * value_stage[at, :]
        for n, block in enumerate(pick_rows(gated, onehot_t[...], rows)):
            acc[i * (tile // LANES) + n] = block
            picked[i * (tile // LANES) + n] = block.astype(bf16)
        return 0

    lax.fori_loop(0, count, step, 0)
    for s in range(slots):
        part = jnp.swapaxes(acc[:, s * owner_count : (s + 1) * owner_count, :], 0, 1)
        payload[:, :, s * LANES : (s + 1) * LANES] = part.astype(bf16)


def first_kernel(channels, filters_far, outer_fwd_far, turn_far, inner_far, *refs):
    onehot_t, skip, *dense = refs[:6]
    onehot, others, skip_wide, spectra, *outs = refs[6:14]
    filters, outer_fwd, turn, inner, spectra_stage, table_sems = refs[14:20]
    sources = (filters_far, outer_fwd_far, turn_far, inner_far)
    stages = (filters, outer_fwd, turn, inner)
    tables = [
        pltpu.make_async_copy(source, stage, table_sems.at[n])
        for n, (source, stage) in enumerate(zip(sources, stages))
    ]
    for copy in tables:
        copy.start()
    hit = iota(onehot.shape, 1) == to_column(channels[0:1, :])[: onehot.shape[0]]
    onehot[...] = hit.astype(f32).astype(bf16)
    kept = jnp.max(hit.astype(f32), axis=0, keepdims=True)
    others[...] = jnp.broadcast_to(1.0 - kept, others.shape)
    skip_col = jnp.sum(jnp.where(hit, skip[...], 0.0), axis=1, keepdims=True)
    skip_wide[...] = jnp.broadcast_to(skip_col, skip_wide.shape)

    def send(s):
        return pltpu.make_async_copy(
            spectra_stage.at[s], spectra.at[s], table_sems.at[len(tables) + s]
        )

    def beside():
        for copy in tables:
            copy.wait()
        for s, part in enumerate(filter_spectra(filters, outer_fwd, turn, inner)):
            spectra_stage[s] = part
            send(s).start()

    base_pass(0, onehot_t, others, skip, dense, outs, refs[20:], beside, 4)
    for s in range(spectra.shape[0]):
        send(s).wait()


def second_kernel(first, onehot_t, others, skip, *refs):
    base_pass(first, onehot_t, others, skip, refs[:4], refs[5:9], refs[9:], None, 4)


def base_pass(first, onehot_t, others, skip, dense, outs, scratch, beside, ahead):
    base, sums, picked_gate, picked_res = outs
    stages = scratch[:4]
    base_stage, partial, base_sems, sems = scratch[4:]
    gate_stage, value_stage, out_stage, res_stage = stages
    rows = picked_gate.shape[1]
    slab = gate_stage.shape[1]
    tile = partial.shape[0]
    wait, count = fetch(dense, stages, sems, tile, first, ahead)
    if beside is not None:
        beside()

    def copy(i):
        at = pl.multiple_of(i * tile, tile)
        return pltpu.make_async_copy(
            base_stage.at[pl.ds(at, tile), :], base.at[pl.ds(first + at, tile), :], base_sems.at[i]
        )

    def step(i, _):
        start = wait(i)
        chunks = range(0, tile, CHUNK)
        totals = [jnp.zeros((CHUNK, LANES), f32) for _ in chunks]
        for j in range(0, slab, LANES):
            lanes = slice(j, j + LANES)
            skips = skip[:, lanes]
            mask = others[0:1, lanes].astype(bf16)
            for n, c in enumerate(chunks):
                at = pl.ds(start + c, CHUNK)
                gated = (gate_stage[at, lanes] * value_stage[at, lanes]).astype(f32)
                mixed = out_stage[at, lanes].astype(f32) * (skips * gated)
                hidden = (res_stage[at, lanes].astype(f32) + mixed).astype(bf16) * mask
                base_stage[at, lanes] = hidden
                hidden = hidden.astype(f32)
                totals[n] = totals[n] + hidden * hidden
        copy(i).start()
        for n, c in enumerate(chunks):
            partial[c : c + CHUNK, :] = totals[n]
        total = jnp.sum(partial[...].T, axis=0, keepdims=True)
        at = pl.ds(start, tile)
        both = jnp.concatenate([out_stage[at, :], res_stage[at, :]], axis=0)
        both = pick_rows(both, onehot_t[...], rows)
        picks_gate, picks_res = both[: tile // LANES], both[tile // LANES :]
        for n in range(tile // LANES):
            block = i * (tile // LANES) + n
            sums[block] = total[:, n * LANES : (n + 1) * LANES]
            picked_gate[block] = picks_gate[n].astype(bf16)
            picked_res[block] = picks_res[n].astype(bf16)
        return 0

    lax.fori_loop(0, count, step, 0)
    lax.fori_loop(0, count, lambda i, _: (copy(i).wait(), 0)[1], 0)


def kept_kernel(conv, picked, skip_wide, *refs):
    hidden, totals = refs[-2:]
    owner_count, blocks = conv.shape[:2]
    first = 0
    for n in range(0, len(refs) - 2, 3):
        sums, picked_gate, picked_res = refs[n : n + 3]
        size = sums.shape[0]
        at_h = slice(first, first + size)
        total = jnp.zeros((size, LANES), f32)
        for s in range(conv.shape[2] // LANES):
            at = slice(s * owner_count, (s + 1) * owner_count)
            lanes = slice(s * LANES, (s + 1) * LANES)
            wide = jnp.swapaxes(conv[:, at_h, lanes].astype(f32), 0, 1)
            wide = wide + skip_wide[at, :] * picked[at_h, at, :].astype(f32)
            value = picked_res[:, at, :].astype(f32) + picked_gate[:, at, :].astype(f32) * wide
            value = value.astype(bf16)
            hidden[at_h, at, :] = value
            value = value.astype(f32)
            total = total + jnp.sum(value * value, axis=1)
        for i in range(size):
            totals[first + i] = total[i : i + 1, :] + sums[i]
        first = first + size


def hidden_kernel(base, hidden_kept, onehot, hidden, held, base_stage, base_sems, sems):
    slab = held.shape[1]
    wide = min(slab, 2 * LANES)
    count = sems.shape[0]
    tile = held.shape[0] // count
    wait, _ = fetch((base,), (base_stage,), base_sems, tile)

    def copy(i):
        rows = pl.ds(pl.multiple_of(i * tile, tile), tile)
        return pltpu.make_async_copy(held.at[rows, :], hidden.at[rows, :], sems.at[i])

    def step(i, _):
        blocks = range(tile // LANES)
        kept = [hidden_kept[i * (tile // LANES) + n].astype(f32).T.astype(bf16) for n in blocks]
        kept = jnp.concatenate(kept, axis=0)
        rows = pl.ds(wait(i), tile)
        for j in range(0, slab, wide):
            lanes = slice(j, j + wide)
            placed = dot(kept, onehot[:, lanes]).astype(bf16)
            held[rows, lanes] = base_stage[rows, lanes] + placed
        copy(i).start()
        return 0

    lax.fori_loop(0, count, step, 0)
    lax.fori_loop(0, count, lambda i, _: (copy(i).wait(), 0)[1], 0)


def norm_kernel(width, count, *refs):
    parts = refs[:count]
    held, gain, normed, stage, turned, sems = refs[count:]
    slab = held.shape[1]

    def copy(i):
        rows = pl.ds(pl.multiple_of(i * LANES, LANES), LANES)
        return pltpu.make_async_copy(stage.at[rows, :], normed.at[rows, :], sems.at[i])

    def step(i, _):
        total = parts[0][i]
        for part in parts[1:]:
            total = total + part[i]
        scale = lax.rsqrt(total / width + norm_eps)
        turned[...] = jnp.broadcast_to(scale, (LANES, LANES)).T
        first = pl.multiple_of(i * LANES, LANES)
        for c in range(0, LANES, CHUNK):
            at = pl.ds(first + c, CHUNK)
            scales = turned[c : c + CHUNK, :]
            for j in range(0, slab, LANES):
                lanes = slice(j, j + LANES)
                value = held[at, lanes].astype(f32) * scales * gain[:, lanes]
                stage[at, lanes] = value.astype(bf16)
        copy(i).start()
        return 0

    lax.fori_loop(0, sems.shape[0], step, 0)
    lax.fori_loop(0, sems.shape[0], lambda i, _: (copy(i).wait(), 0)[1], 0)


def in_hbm(x):
    return pltpu.with_memory_space_constraint(x, pltpu.HBM)


def in_vmem(x):
    return pltpu.with_memory_space_constraint(x, pltpu.VMEM)


def call(kernel, outs, ins, flops, moved, limit, scratch=(), far=(), far_outs=(), alias=None):
    near = pl.BlockSpec(memory_space=pltpu.VMEM)
    away = pl.BlockSpec(memory_space=pl.ANY)
    return pl.pallas_call(
        kernel,
        out_shape=outs,
        in_specs=[away if n in far else near for n in range(len(ins))],
        out_specs=[away if n in far_outs else near for n in range(len(outs))],
        scratch_shapes=list(scratch),
        input_output_aliases=alias or {},
        compiler_params=pltpu.CompilerParams(vmem_limit_bytes=limit),
        cost_estimate=pl.CostEstimate(flops=flops, bytes_accessed=moved, transcendentals=0),
    )(*ins)


def local(
    gate_in, value_in, out_gate, residual, filters, kept_index, kept_owner, skip_bias, norm_gain
):
    tok_rows, slab = gate_in.shape
    slots, length = filters.shape[2:]
    chan_devices = lax.axis_size("chan")
    owner_count = lax.axis_size("seqo") * lax.axis_size("seqi")
    rows = slots * owner_count
    lanes_rows = -(-rows // LANES) * LANES
    blocks = tok_rows // LANES
    outer = length // LANES
    tile = TILE if tok_rows % TILE == 0 else LANES
    dense = tok_rows * slab * 2
    sds = jax.ShapeDtypeStruct
    tables = [in_hbm(jnp.asarray(x)) for x in dft_tables(length)]
    outer_fwd, turn, inner, outer_back = tables
    skip_row = skip_bias[None, :]
    gain_row = norm_gain[None, :]
    gate_in, value_in, out_gate, residual = map(in_hbm, (gate_in, value_in, out_gate, residual))
    picks = sds((blocks, rows, LANES), bf16)
    row_sums = sds((blocks, 1, LANES), f32)
    buffer = (owner_count, blocks, slots * LANES)
    whole = (tok_rows, slab)

    payload, picked, channels, onehot_t = call(
        functools.partial(pick_kernel, owner_count, slots),
        [
            sds(buffer, bf16),
            picks,
            sds((8, lanes_rows), jnp.int32),
            sds((slab, lanes_rows), bf16),
        ],
        [in_hbm(kept_index), in_hbm(kept_owner), gate_in, value_in],
        2 * tok_rows * slab * rows,
        2 * dense,
        24 * MIB,
        scratch=[
            pltpu.VMEM((blocks, rows, LANES), f32),
            pltpu.VMEM(whole, bf16),
            pltpu.VMEM(whole, bf16),
            pltpu.VMEM((2,) + kept_index.shape, jnp.int32),
            pltpu.SemaphoreType.DMA((2,)),
            pltpu.SemaphoreType.DMA((2, tok_rows // tile)),
        ],
        far=(0, 1, 2, 3),
    )

    incoming = lax.all_to_all(payload, ("seqo", "seqi"), split_axis=0, concat_axis=0, tiled=True)

    dense_ins = [gate_in, value_in, out_gate, residual]

    def base_parts(count):
        part = count * LANES
        outs = [
            pltpu.HBM(whole, bf16),
            sds((count, 1, LANES), f32),
            sds((count, rows, LANES), bf16),
            sds((count, rows, LANES), bf16),
        ]
        scratch = [pltpu.VMEM((part, slab), bf16)] * 5 + [
            pltpu.VMEM((LANES, LANES), f32),
            pltpu.SemaphoreType.DMA((count,)),
            pltpu.SemaphoreType.DMA((4, count)),
        ]
        return outs, scratch, 4 * part * slab * rows, 10 * part * slab

    early = max(1, blocks * EARLY // 16)
    outs, scratch, flops, moved = base_parts(early)
    spectrum = (slots, outer, 2 * LANES)
    table_ins = [in_hbm(filters[0, 0]), outer_fwd, turn, inner]
    onehot, others, skip_wide, spectra, base, *first_picks = call(
        first_kernel,
        [
            sds((rows, slab), bf16),
            sds((8, slab), f32),
            sds((rows, LANES), f32),
            pltpu.HBM(spectrum, f32),
        ]
        + outs,
        [channels] + table_ins + [onehot_t, skip_row] + dense_ins,
        flops,
        moved,
        36 * MIB,
        scratch=[pltpu.VMEM(x.shape, x.dtype) for x in table_ins]
        + [pltpu.VMEM(spectrum, f32), pltpu.SemaphoreType.DMA((len(table_ins) + slots,))]
        + scratch,
        far=(1, 2, 3, 4, 7, 8, 9, 10),
        far_outs=(3, 4),
    )

    conv_ins = [incoming, outer_fwd, turn, inner, in_hbm(spectra), outer_back]
    (convolved,) = call(
        convolve_kernel,
        [pltpu.HBM(buffer, bf16)],
        conv_ins,
        2 * slots * length * 2 * (5 * outer + 12 * LANES),
        8 * MIB,
        20 * MIB,
        scratch=[pltpu.VMEM(x.shape, x.dtype) for x in conv_ins[1:]]
        + [pltpu.VMEM(buffer, bf16), pltpu.SemaphoreType.DMA((len(conv_ins) - 1 + slots,))],
        far=tuple(range(1, len(conv_ins))),
        far_outs=(0,),
    )
    convolved, onehot_t = lax.optimization_barrier((convolved, onehot_t))

    returned = lax.all_to_all(convolved, ("seqo", "seqi"), split_axis=0, concat_axis=0, tiled=True)

    outs, scratch, flops, moved = base_parts(blocks - early)
    base, *more_picks = call(
        functools.partial(second_kernel, early * LANES),
        outs,
        [onehot_t, others, skip_row] + dense_ins + [base],
        flops,
        moved,
        36 * MIB,
        scratch=scratch,
        far=(3, 4, 5, 6, 7),
        far_outs=(0,),
        alias={7: 0},
    )

    hidden_kept, totals = call(
        kept_kernel,
        [picks, row_sums],
        [returned, picked, skip_wide, *first_picks, *more_picks],
        8 * rows * tok_rows,
        10 * rows * tok_rows,
        16 * MIB,
    )

    parts = [totals]
    for shift in range(1, chan_devices):
        ring = [(i, (i + shift) % chan_devices) for i in range(chan_devices)]
        parts.append(lax.ppermute(totals, "chan", ring))

    hidden, held = call(
        hidden_kernel,
        [pltpu.HBM(whole, bf16), pltpu.VMEM(whole, bf16)],
        [in_hbm(base), hidden_kept, onehot],
        2 * tok_rows * slab * rows,
        2 * dense,
        16 * MIB,
        scratch=[
            pltpu.VMEM(whole, bf16),
            pltpu.SemaphoreType.DMA((1, tok_rows // tile)),
            pltpu.SemaphoreType.DMA((tok_rows // tile,)),
        ],
        far=(0,),
        far_outs=(0,),
    )
    (normed,) = call(
        functools.partial(norm_kernel, float(slab * chan_devices), len(parts)),
        [pltpu.HBM(whole, bf16)],
        parts + [in_vmem(held), gain_row],
        4 * tok_rows * slab,
        2 * dense,
        16 * MIB,
        scratch=[
            pltpu.VMEM(whole, bf16),
            pltpu.VMEM((LANES, LANES), f32),
            pltpu.SemaphoreType.DMA((blocks,)),
        ],
        far_outs=(0,),
    )
    return (hidden, normed)


def solution(mesh):
    positions = P(("seqo", "seqi"), "chan")
    in_specs = (
        positions,
        positions,
        positions,
        positions,
        P("chan", ("seqo", "seqi"), None, None),
        P("chan", None),
        P("chan", None),
        P("chan"),
        P("chan"),
    )
    return jax.shard_map(
        local, mesh=mesh, in_specs=in_specs, out_specs=(positions, positions), check_vma=False
    )
```

```python
import functools

import jax
import jax.numpy as jnp
import numpy as np
from jax import lax
from jax.experimental import pallas as pl
from jax.experimental.pallas import tpu as pltpu
from jax.sharding import PartitionSpec as P

LANES = 128
TILE = 256
CHUNK = 16
GROUP = 3
EARLY = 7
MIB = 1 << 20
norm_eps = 1e-06
f32 = jnp.float32
bf16 = jnp.bfloat16


def split_np(table):
    high = table.astype(jnp.bfloat16)
    low = (table - high.astype(np.float64)).astype(jnp.bfloat16)
    return high, low


def dft_tables(length):
    inner = LANES
    outer = length // inner
    a = np.arange(outer)
    b = np.arange(inner)
    quarter = np.arange(outer) + 0.25
    outer_angle = 2 * np.pi / outer * np.mod(quarter[:, None] * a[None, :], outer)
    turn_angle = 2 * np.pi / length * (quarter[:, None] * b[None, :])
    inner_angle = 2 * np.pi / inner * np.mod(b[:, None] * b[None, :], inner)
    outer_fwd = np.concatenate([np.cos(outer_angle), -np.sin(outer_angle)], axis=0)
    c, s = np.cos(inner_angle), np.sin(inner_angle)
    inner_fwd = np.concatenate(
        [np.concatenate([c, -s], axis=1), np.concatenate([s, c], axis=1)], axis=0
    )
    inner_back = np.concatenate(
        [np.concatenate([c, s], axis=1), np.concatenate([-s, c], axis=1)], axis=0
    )
    outer_back = np.concatenate([np.cos(outer_angle).T, -np.sin(outer_angle).T], axis=1) / length
    turn = np.concatenate([np.cos(turn_angle), np.sin(turn_angle)], axis=1).astype(np.float32)
    outer_fwd = np.concatenate(split_np(outer_fwd), axis=1)
    inner = np.concatenate(split_np(inner_fwd) + split_np(inner_back), axis=0)
    outer_back = np.concatenate(split_np(outer_back), axis=1)
    return outer_fwd, turn, inner, outer_back


def split(value):
    high = value.astype(bf16)
    low = (value - high.astype(f32)).astype(bf16)
    return high, low


def dot(x, y):
    return jnp.dot(x, y, preferred_element_type=f32)


def dot_rows(x, y):
    return lax.dot_general(x, y, (((0,), (0,)), ((), ())), preferred_element_type=f32)


def times_table(value, table):
    high, low = split(value)
    depth = value.shape[1]
    stacked = jnp.concatenate([table, table[:depth]], axis=0)
    return dot(jnp.concatenate([high, high, low], axis=1), stacked)


def table_times(table, value):
    high, low = split(value)
    depth = value.shape[0]
    stacked = jnp.concatenate([table, table[:, :depth]], axis=1)
    return dot(stacked, jnp.concatenate([high, high, low], axis=0))


def to_spectrum(blocks, slots, outer_fwd, turn, inner_fwd):
    outer = blocks.shape[0]
    first = dot(outer_fwd, jnp.concatenate([blocks, blocks], axis=0))
    turn, inner_fwd = turn(), inner_fwd()
    cos, sin = turn[:, :LANES], turn[:, LANES:]
    turned = []
    for s in range(slots):
        re = first[:outer, s * LANES : (s + 1) * LANES]
        im = first[outer:, s * LANES : (s + 1) * LANES]
        turned.append(jnp.concatenate([re * cos + im * sin, im * cos - re * sin], axis=1))
    return grouped(turned, inner_fwd)


def grouped(values, table):
    result = []
    for s in range(0, len(values), GROUP):
        part = values[s : s + GROUP]
        size = part[0].shape[0]
        product = times_table(jnp.concatenate(part, axis=0), table)
        result += [product[n * size : (n + 1) * size] for n in range(len(part))]
    return result


def filter_spectra(filters, outer_fwd, turn, inner):
    slots, length = filters.shape
    outer = length // LANES
    wide = filters[...].astype(f32)
    blocks = [wide[s].reshape(outer, LANES) for s in range(slots)]
    blocks = jnp.concatenate(blocks, axis=1).astype(bf16)
    return to_spectrum(
        blocks, slots, outer_fwd[...], lambda: turn[...], lambda: inner[: 4 * LANES, :]
    )


def convolve_kernel(
    signals, outer_fwd_far, turn_far, inner_far, spectra_far, outer_back_far, out, *scratch
):
    sources = (outer_fwd_far, turn_far, inner_far, spectra_far, outer_back_far)
    outer_fwd, turn_ref, inner, spectra, outer_back, result, sems = scratch
    copies = [
        pltpu.make_async_copy(source, scratch[n], sems.at[n]) for n, source in enumerate(sources)
    ]
    for copy in copies:
        copy.start()
    slots, outer = spectra.shape[:2]

    def turn_now():
        copies[1].wait()
        return turn_ref[...]

    def inner_now():
        copies[2].wait()
        return inner[: 4 * LANES, :]

    copies[0].wait()
    blocks = signals[...].reshape(outer, slots * LANES)
    parts = to_spectrum(blocks, slots, outer_fwd[...], turn_now, inner_now)
    turn = turn_ref[...]
    cos, sin = turn[:, :LANES], turn[:, LANES:]
    copies[3].wait()
    joint = []
    for s in range(slots):
        sig_re, sig_im = parts[s][:, :LANES], parts[s][:, LANES:]
        ker_re, ker_im = spectra[s, :, :LANES], spectra[s, :, LANES:]
        joint.append(
            jnp.concatenate(
                [sig_re * ker_re - sig_im * ker_im, sig_re * ker_im + sig_im * ker_re], axis=1
            )
        )
    turned = []
    for back in grouped(joint, inner[4 * LANES :, :]):
        re, im = back[:, :LANES], back[:, LANES:]
        turned.append(jnp.concatenate([re * cos - im * sin, im * cos + re * sin], axis=0))
    copies[4].wait()
    sends = []
    for s in range(0, slots, 2):
        pair = turned[s : s + 2]
        causal = table_times(outer_back[...], jnp.concatenate(pair, axis=1)).astype(bf16)
        lanes = pl.ds(s * LANES, len(pair) * LANES)
        result[:, :, lanes] = causal.reshape(out.shape[:2] + (len(pair) * LANES,))
        sends.append(
            pltpu.make_async_copy(
                result.at[:, :, lanes], out.at[:, :, lanes], sems.at[len(copies) + len(sends)]
            )
        )
        sends[-1].start()
    for send in sends:
        send.wait()


def iota(shape, axis):
    return lax.broadcasted_iota(jnp.int32, shape, axis)


def to_column(row):
    size = row.shape[1]
    same = iota((size, size), 0) == iota((size, size), 1)
    return jnp.sum(jnp.where(same, row, 0), axis=1, keepdims=True)


def channel_of_row(index_row, owners_row, owner_count, rows):
    slots = owners_row.shape[1]
    owners_col = to_column(owners_row)
    index_col = to_column(index_row)
    earlier = (owners_col == owners_row) & (iota((slots, slots), 1) < iota((slots, slots), 0))
    rank_col = jnp.sum(earlier.astype(jnp.int32), axis=1, keepdims=True)
    target_col = jnp.where(owners_col >= 0, rank_col * owner_count + owners_col, -1)
    hit = target_col == iota((slots, rows), 1)
    return jnp.sum(jnp.where(hit, index_col + 1, 0), axis=0, keepdims=True) - 1


def pick_rows(tile, onehot_t, rows):
    picked = dot(tile, onehot_t).T
    return [picked[:rows, i : i + LANES] for i in range(0, tile.shape[0], LANES)]


def fetch(sources, stages, sems, tile, first=0, ahead=3):
    count = stages[0].shape[0] // tile

    def copies(i):
        at = pl.multiple_of(i * tile, tile)
        return [
            pltpu.make_async_copy(
                source.at[pl.ds(first + at, tile), :], stage.at[pl.ds(at, tile), :], sems.at[n, i]
            )
            for n, (source, stage) in enumerate(zip(sources, stages))
        ]

    def start(i):
        for copy in copies(i):
            copy.start()

    for i in range(min(ahead, count)):
        start(i)

    def wait(i):
        for copy in copies(i):
            copy.wait()

        @pl.when(i + ahead < count)
        def _():
            start(i + ahead)

        return pl.multiple_of(i * tile, tile)

    return wait, count


def build_onehot(onehot_t, row):
    onehot_t[...] = (iota(onehot_t.shape, 0) == row).astype(f32).astype(bf16)


def pick_kernel(owner_count, slots, index, owners, gate, value, *refs):
    payload, picked, channels, gated_head = refs[:4]
    acc, gate_stage, value_stage, onehot_t, lists, list_sems, sems = refs[4:]
    head_tiles = gated_head.shape[0] // (gate_stage.shape[0] // sems.shape[1])
    rows = owner_count * slots
    tile = gate_stage.shape[0] // sems.shape[1]
    list_copies = [
        pltpu.make_async_copy(source, lists.at[n], list_sems.at[n])
        for n, source in enumerate((index, owners))
    ]
    for copy in list_copies:
        copy.start()
    wait, count = fetch((gate, value), (gate_stage, value_stage), sems, tile, 0, 4)
    for copy in list_copies:
        copy.wait()
    row = channel_of_row(lists[0], lists[1], owner_count, onehot_t.shape[1])
    channels[...] = jnp.broadcast_to(row, channels.shape)
    build_onehot(onehot_t, row)

    def step(i, _):
        at = pl.ds(wait(i), tile)
        gated = gate_stage[at, :] * value_stage[at, :]

        @pl.when(i < head_tiles)
        def _():
            gated_head[at, :] = gated

        for n, block in enumerate(pick_rows(gated, onehot_t[...], rows)):
            acc[i * (tile // LANES) + n] = block
            picked[i * (tile // LANES) + n] = block.astype(bf16)
        return 0

    lax.fori_loop(0, count, step, 0)
    for s in range(slots):
        part = jnp.swapaxes(acc[:, s * owner_count : (s + 1) * owner_count, :], 0, 1)
        payload[:, :, s * LANES : (s + 1) * LANES] = part.astype(bf16)


def first_kernel(channels, filters_far, outer_fwd_far, turn_far, inner_far, *refs):
    gated_head, skip, *dense = refs[:6]
    onehot, others, skip_wide, spectra, *outs = refs[6:14]
    filters, outer_fwd, turn, inner, spectra_stage, table_sems = refs[14:20]
    sources = (filters_far, outer_fwd_far, turn_far, inner_far)
    stages = (filters, outer_fwd, turn, inner)
    tables = [
        pltpu.make_async_copy(source, stage, table_sems.at[n])
        for n, (source, stage) in enumerate(zip(sources, stages))
    ]
    for copy in tables:
        copy.start()
    scratch = refs[20:]
    build_onehot(scratch[0], channels[0:1, :])
    hit = iota(onehot.shape, 1) == to_column(channels[0:1, :])[: onehot.shape[0]]
    onehot[...] = hit.astype(f32).astype(bf16)
    kept = jnp.max(hit.astype(f32), axis=0, keepdims=True)
    others[...] = jnp.broadcast_to(1.0 - kept, others.shape)
    skip_col = jnp.sum(jnp.where(hit, skip[...], 0.0), axis=1, keepdims=True)
    skip_wide[...] = jnp.broadcast_to(skip_col, skip_wide.shape)

    def send(s):
        return pltpu.make_async_copy(
            spectra_stage.at[s], spectra.at[s], table_sems.at[len(tables) + s]
        )

    def beside():
        for copy in tables:
            copy.wait()
        for s, part in enumerate(filter_spectra(filters, outer_fwd, turn, inner)):
            spectra_stage[s] = part
            send(s).start()

    base_pass(0, gated_head, others, skip, dense, outs, None, scratch, beside)
    for s in range(spectra.shape[0]):
        send(s).wait()


def second_kernel(first, channels, others, skip, *refs):
    base, tail, *outs = refs[5:10]
    build_onehot(refs[10], channels[0:1, :])
    base_pass(first, None, others, skip, refs[:4], [base] + outs, tail, refs[10:], None)


def base_pass(first, head, others, skip, dense, outs, tail, scratch, beside):
    base, sums, picked_gate, picked_res = outs
    onehot_t, gate_stage, value_stage, out_stage, res_stage, base_stage = scratch[:6]
    partial, base_sems, gate_sems, sems = scratch[6:]
    rows = picked_gate.shape[1]
    slab = out_stage.shape[1]
    tile = partial.shape[0]
    head_rows = 0 if head is None else head.shape[0]
    wait, count = fetch(dense[2:], (out_stage, res_stage), sems, tile, first)
    wait_gate, _ = fetch(
        dense[:2], (gate_stage, value_stage), gate_sems, tile, first + head_rows
    )
    if beside is not None:
        beside()
    head_tiles = head_rows // tile
    kept_tiles = base_stage.shape[0] // tile

    def copy(i):
        at = pl.multiple_of(i * tile, tile)
        return pltpu.make_async_copy(
            base_stage.at[pl.ds(at, tile), :], base.at[pl.ds(first + at, tile), :], base_sems.at[i]
        )

    def step(i, in_head, in_tail):
        start = wait(i)
        gate_start = start if in_head else wait_gate(i - head_tiles)
        target, target_start = (tail, start - kept_tiles * tile) if in_tail else (base_stage, start)
        chunks = range(0, tile, CHUNK)
        totals = [jnp.zeros((CHUNK, LANES), f32) for _ in chunks]
        for j in range(0, slab, LANES):
            lanes = slice(j, j + LANES)
            skips = skip[:, lanes]
            mask = others[0:1, lanes].astype(bf16)
            for n, c in enumerate(chunks):
                at = pl.ds(start + c, CHUNK)
                gate_at = pl.ds(gate_start + c, CHUNK)
                if in_head:
                    gated = head[gate_at, lanes]
                else:
                    gated = gate_stage[gate_at, lanes] * value_stage[gate_at, lanes]
                mixed = out_stage[at, lanes].astype(f32) * (skips * gated.astype(f32))
                hidden = (res_stage[at, lanes].astype(f32) + mixed).astype(bf16) * mask
                target[pl.ds(pl.multiple_of(target_start + c, CHUNK), CHUNK), lanes] = hidden
                hidden = hidden.astype(f32)
                totals[n] = totals[n] + hidden * hidden
        if not in_tail:
            copy(i).start()
        for n, c in enumerate(chunks):
            partial[c : c + CHUNK, :] = totals[n]
        total = jnp.sum(partial[...].T, axis=0, keepdims=True)
        at = pl.ds(start, tile)
        both = jnp.concatenate([out_stage[at, :], res_stage[at, :]], axis=0)
        both = pick_rows(both, onehot_t[...], rows)
        picks_gate, picks_res = both[: tile // LANES], both[tile // LANES :]
        for n in range(tile // LANES):
            block = i * (tile // LANES) + n
            sums[block] = total[:, n * LANES : (n + 1) * LANES]
            picked_gate[block] = picks_gate[n].astype(bf16)
            picked_res[block] = picks_res[n].astype(bf16)
        return 0

    if head_tiles:
        lax.fori_loop(0, head_tiles, lambda i, _: step(i, True, False), 0)
    lax.fori_loop(head_tiles, kept_tiles, lambda i, _: step(i, False, False), 0)
    if tail is not None:
        lax.fori_loop(kept_tiles, count, lambda i, _: step(i, False, True), 0)
    lax.fori_loop(0, kept_tiles, lambda i, _: (copy(i).wait(), 0)[1], 0)


def kept_kernel(conv, picked, skip_wide, *refs):
    hidden, totals = refs[-2:]
    owner_count, blocks = conv.shape[:2]
    first = 0
    for n in range(0, len(refs) - 2, 3):
        sums, picked_gate, picked_res = refs[n : n + 3]
        size = sums.shape[0]
        at_h = slice(first, first + size)
        total = jnp.zeros((size, LANES), f32)
        for s in range(conv.shape[2] // LANES):
            at = slice(s * owner_count, (s + 1) * owner_count)
            lanes = slice(s * LANES, (s + 1) * LANES)
            wide = jnp.swapaxes(conv[:, at_h, lanes].astype(f32), 0, 1)
            wide = wide + skip_wide[at, :] * picked[at_h, at, :].astype(f32)
            value = picked_res[:, at, :].astype(f32) + picked_gate[:, at, :].astype(f32) * wide
            value = value.astype(bf16)
            hidden[at_h, at, :] = value
            value = value.astype(f32)
            total = total + jnp.sum(value * value, axis=1)
        for i in range(size):
            totals[first + i] = total[i : i + 1, :] + sums[i]
        first = first + size


def hidden_kernel(base, tail, hidden_kept, onehot, hidden, held, base_stage, base_sems, sems):
    slab = held.shape[1]
    wide = min(slab, 2 * LANES)
    count = sems.shape[0]
    tile = held.shape[0] // count
    tail_tiles = tail.shape[0] // tile
    wait, staged = fetch((base,), (base_stage,), base_sems, tile, 0, 4)

    def copy(i):
        rows = pl.ds(pl.multiple_of(i * tile, tile), tile)
        return pltpu.make_async_copy(held.at[rows, :], hidden.at[rows, :], sems.at[i])

    def step(i, source, start):
        blocks = range(tile // LANES)
        kept = [hidden_kept[i * (tile // LANES) + n].astype(f32).T.astype(bf16) for n in blocks]
        kept = jnp.concatenate(kept, axis=0)
        rows = pl.ds(pl.multiple_of(i * tile, tile), tile)
        for j in range(0, slab, wide):
            lanes = slice(j, j + wide)
            placed = dot(kept, onehot[:, lanes]).astype(bf16)
            held[rows, lanes] = source[pl.ds(start, tile), lanes] + placed
        copy(i).start()
        return 0

    for n in range(tail_tiles):
        step(staged + n, tail, n * tile)
    lax.fori_loop(0, staged, lambda i, _: step(i, base_stage, wait(i)), 0)
    lax.fori_loop(0, count, lambda i, _: (copy(i).wait(), 0)[1], 0)


def norm_kernel(width, count, *refs):
    parts = refs[:count]
    held, gain, normed, stage, turned, sems = refs[count:]
    slab = held.shape[1]

    def copy(i):
        rows = pl.ds(pl.multiple_of(i * LANES, LANES), LANES)
        return pltpu.make_async_copy(stage.at[rows, :], normed.at[rows, :], sems.at[i])

    def step(i, _):
        total = parts[0][i]
        for part in parts[1:]:
            total = total + part[i]
        scale = lax.rsqrt(total / width + norm_eps)
        turned[...] = jnp.broadcast_to(scale, (LANES, LANES)).T
        first = pl.multiple_of(i * LANES, LANES)
        for c in range(0, LANES, CHUNK):
            at = pl.ds(first + c, CHUNK)
            scales = turned[c : c + CHUNK, :]
            for j in range(0, slab, LANES):
                lanes = slice(j, j + LANES)
                value = held[at, lanes].astype(f32) * scales * gain[:, lanes]
                stage[at, lanes] = value.astype(bf16)
        copy(i).start()
        return 0

    lax.fori_loop(0, sems.shape[0], step, 0)
    lax.fori_loop(0, sems.shape[0], lambda i, _: (copy(i).wait(), 0)[1], 0)


def in_hbm(x):
    return pltpu.with_memory_space_constraint(x, pltpu.HBM)


def in_vmem(x):
    return pltpu.with_memory_space_constraint(x, pltpu.VMEM)


def call(kernel, outs, ins, flops, moved, limit, scratch=(), far=(), far_outs=(), alias=None):
    near = pl.BlockSpec(memory_space=pltpu.VMEM)
    away = pl.BlockSpec(memory_space=pl.ANY)
    return pl.pallas_call(
        kernel,
        out_shape=outs,
        in_specs=[away if n in far else near for n in range(len(ins))],
        out_specs=[away if n in far_outs else near for n in range(len(outs))],
        scratch_shapes=list(scratch),
        input_output_aliases=alias or {},
        compiler_params=pltpu.CompilerParams(vmem_limit_bytes=limit),
        cost_estimate=pl.CostEstimate(flops=flops, bytes_accessed=moved, transcendentals=0),
    )(*ins)


def local(
    gate_in, value_in, out_gate, residual, filters, kept_index, kept_owner, skip_bias, norm_gain
):
    tok_rows, slab = gate_in.shape
    slots, length = filters.shape[2:]
    chan_devices = lax.axis_size("chan")
    owner_count = lax.axis_size("seqo") * lax.axis_size("seqi")
    rows = slots * owner_count
    lanes_rows = -(-rows // LANES) * LANES
    blocks = tok_rows // LANES
    outer = length // LANES
    tile = TILE if tok_rows % TILE == 0 else LANES
    dense = tok_rows * slab * 2
    sds = jax.ShapeDtypeStruct
    tables = [in_hbm(jnp.asarray(x)) for x in dft_tables(length)]
    outer_fwd, turn, inner, outer_back = tables
    skip_row = skip_bias[None, :]
    gain_row = norm_gain[None, :]
    gate_in, value_in, out_gate, residual = map(in_hbm, (gate_in, value_in, out_gate, residual))
    picks = sds((blocks, rows, LANES), bf16)
    row_sums = sds((blocks, 1, LANES), f32)
    buffer = (owner_count, blocks, slots * LANES)
    whole = (tok_rows, slab)
    head_rows = tok_rows // 4 // tile * tile
    tail_rows = tok_rows // 8 // tile * tile

    payload, picked, channels, gated_head = call(
        functools.partial(pick_kernel, owner_count, slots),
        [
            sds(buffer, bf16),
            picks,
            sds((8, lanes_rows), jnp.int32),
            pltpu.VMEM((head_rows, slab), bf16),
        ],
        [in_hbm(kept_index), in_hbm(kept_owner), gate_in, value_in],
        2 * tok_rows * slab * rows,
        2 * dense,
        24 * MIB,
        scratch=[
            pltpu.VMEM((blocks, rows, LANES), f32),
            pltpu.VMEM(whole, bf16),
            pltpu.VMEM(whole, bf16),
            pltpu.VMEM((slab, lanes_rows), bf16),
            pltpu.VMEM((2,) + kept_index.shape, jnp.int32),
            pltpu.SemaphoreType.DMA((2,)),
            pltpu.SemaphoreType.DMA((2, tok_rows // tile)),
        ],
        far=(0, 1, 2, 3),
    )

    incoming = lax.all_to_all(payload, ("seqo", "seqi"), split_axis=0, concat_axis=0, tiled=True)

    dense_ins = [gate_in, value_in, out_gate, residual]

    def base_parts(count, head, tail):
        part = count * LANES
        outs = [
            pltpu.HBM(whole, bf16),
            sds((count, 1, LANES), f32),
            sds((count, rows, LANES), bf16),
            sds((count, rows, LANES), bf16),
        ]
        scratch = [
            pltpu.VMEM((slab, lanes_rows), bf16),
            pltpu.VMEM((part - head, slab), bf16),
            pltpu.VMEM((part - head, slab), bf16),
            pltpu.VMEM((part, slab), bf16),
            pltpu.VMEM((part, slab), bf16),
            pltpu.VMEM((part - tail, slab), bf16),
            pltpu.VMEM((LANES, LANES), f32),
            pltpu.SemaphoreType.DMA(((part - tail) // LANES,)),
            pltpu.SemaphoreType.DMA((2, (part - head) // LANES)),
            pltpu.SemaphoreType.DMA((2, count)),
        ]
        return outs, scratch, 4 * part * slab * rows, 10 * part * slab

    early = max(head_rows // LANES + 1, blocks * EARLY // 16)
    outs, scratch, flops, moved = base_parts(early, head_rows, 0)
    spectrum = (slots, outer, 2 * LANES)
    table_ins = [in_hbm(filters[0, 0]), outer_fwd, turn, inner]
    onehot, others, skip_wide, spectra, base, *first_picks = call(
        first_kernel,
        [
            sds((rows, slab), bf16),
            sds((8, slab), f32),
            sds((rows, LANES), f32),
            pltpu.HBM(spectrum, f32),
        ]
        + outs,
        [channels] + table_ins + [in_vmem(gated_head), skip_row] + dense_ins,
        flops,
        moved,
        36 * MIB,
        scratch=[pltpu.VMEM(x.shape, x.dtype) for x in table_ins]
        + [pltpu.VMEM(spectrum, f32), pltpu.SemaphoreType.DMA((len(table_ins) + slots,))]
        + scratch,
        far=(1, 2, 3, 4, 7, 8, 9, 10),
        far_outs=(3, 4),
    )

    conv_ins = [incoming, outer_fwd, turn, inner, in_hbm(spectra), outer_back]
    (convolved,) = call(
        convolve_kernel,
        [pltpu.HBM(buffer, bf16)],
        conv_ins,
        2 * slots * length * 2 * (5 * outer + 12 * LANES),
        8 * MIB,
        20 * MIB,
        scratch=[pltpu.VMEM(x.shape, x.dtype) for x in conv_ins[1:]]
        + [pltpu.VMEM(buffer, bf16), pltpu.SemaphoreType.DMA((len(conv_ins) - 1 + slots,))],
        far=tuple(range(1, len(conv_ins))),
        far_outs=(0,),
    )
    convolved, channels = lax.optimization_barrier((convolved, channels))

    returned = lax.all_to_all(convolved, ("seqo", "seqi"), split_axis=0, concat_axis=0, tiled=True)

    outs, scratch, flops, moved = base_parts(blocks - early, 0, tail_rows)
    base, tail, *more_picks = call(
        functools.partial(second_kernel, early * LANES),
        [outs[0], pltpu.VMEM((tail_rows, slab), bf16)] + outs[1:],
        [channels, others, skip_row] + dense_ins + [base],
        flops,
        moved,
        36 * MIB,
        scratch=scratch,
        far=(3, 4, 5, 6, 7),
        far_outs=(0,),
        alias={7: 0},
    )

    hidden_kept, totals = call(
        kept_kernel,
        [picks, row_sums],
        [returned, picked, skip_wide, *first_picks, *more_picks],
        8 * rows * tok_rows,
        10 * rows * tok_rows,
        16 * MIB,
    )

    parts = [totals]
    for shift in range(1, chan_devices):
        ring = [(i, (i + shift) % chan_devices) for i in range(chan_devices)]
        parts.append(lax.ppermute(totals, "chan", ring))

    hidden, held = call(
        hidden_kernel,
        [pltpu.HBM(whole, bf16), pltpu.VMEM(whole, bf16)],
        [in_hbm(base), in_vmem(tail), hidden_kept, onehot],
        2 * tok_rows * slab * rows,
        2 * dense,
        16 * MIB,
        scratch=[
            pltpu.VMEM((tok_rows - tail_rows, slab), bf16),
            pltpu.SemaphoreType.DMA((1, (tok_rows - tail_rows) // tile)),
            pltpu.SemaphoreType.DMA((tok_rows // tile,)),
        ],
        far=(0,),
        far_outs=(0,),
    )
    (normed,) = call(
        functools.partial(norm_kernel, float(slab * chan_devices), len(parts)),
        [pltpu.HBM(whole, bf16)],
        parts + [in_vmem(held), gain_row],
        4 * tok_rows * slab,
        2 * dense,
        16 * MIB,
        scratch=[
            pltpu.VMEM(whole, bf16),
            pltpu.VMEM((LANES, LANES), f32),
            pltpu.SemaphoreType.DMA((blocks,)),
        ],
        far_outs=(0,),
    )
    return (hidden, normed)


def solution(mesh):
    positions = P(("seqo", "seqi"), "chan")
    in_specs = (
        positions,
        positions,
        positions,
        positions,
        P("chan", ("seqo", "seqi"), None, None),
        P("chan", None),
        P("chan", None),
        P("chan"),
        P("chan"),
    )
    return jax.shard_map(
        local, mesh=mesh, in_specs=in_specs, out_specs=(positions, positions), check_vma=False
    )
```

```python
import functools

import jax
import jax.numpy as jnp
import numpy as np
from jax import lax
from jax.experimental import pallas as pl
from jax.experimental.pallas import tpu as pltpu
from jax.sharding import PartitionSpec as P

LANES = 128
TILE = 256
CHUNK = 16
GROUP = 3
EARLY = 8
MIB = 1 << 20
norm_eps = 1e-06
f32 = jnp.float32
bf16 = jnp.bfloat16


def split_np(table):
    high = table.astype(jnp.bfloat16)
    low = (table - high.astype(np.float64)).astype(jnp.bfloat16)
    return high, low


def dft_tables(length):
    inner = LANES
    outer = length // inner
    a = np.arange(outer)
    b = np.arange(inner)
    quarter = np.arange(outer) + 0.25
    outer_angle = 2 * np.pi / outer * np.mod(quarter[:, None] * a[None, :], outer)
    turn_angle = 2 * np.pi / length * (quarter[:, None] * b[None, :])
    inner_angle = 2 * np.pi / inner * np.mod(b[:, None] * b[None, :], inner)
    outer_fwd = np.concatenate([np.cos(outer_angle), -np.sin(outer_angle)], axis=0)
    c, s = np.cos(inner_angle), np.sin(inner_angle)
    inner_fwd = np.concatenate(
        [np.concatenate([c, -s], axis=1), np.concatenate([s, c], axis=1)], axis=0
    )
    inner_back = np.concatenate(
        [np.concatenate([c, s], axis=1), np.concatenate([-s, c], axis=1)], axis=0
    )
    outer_back = np.concatenate([np.cos(outer_angle).T, -np.sin(outer_angle).T], axis=1) / length
    turn = np.concatenate([np.cos(turn_angle), np.sin(turn_angle)], axis=1).astype(np.float32)
    outer_fwd = np.concatenate(split_np(outer_fwd), axis=1)
    inner = np.concatenate(split_np(inner_fwd) + split_np(inner_back), axis=0)
    outer_back = np.concatenate(split_np(outer_back), axis=1)
    return outer_fwd, turn, inner, outer_back


def split(value):
    high = value.astype(bf16)
    low = (value - high.astype(f32)).astype(bf16)
    return high, low


def dot(x, y):
    return jnp.dot(x, y, preferred_element_type=f32)


def dot_rows(x, y):
    return lax.dot_general(x, y, (((0,), (0,)), ((), ())), preferred_element_type=f32)


def times_table(value, table):
    high, low = split(value)
    depth = value.shape[1]
    stacked = jnp.concatenate([table, table[:depth]], axis=0)
    return dot(jnp.concatenate([high, high, low], axis=1), stacked)


def table_times(table, value):
    high, low = split(value)
    depth = value.shape[0]
    stacked = jnp.concatenate([table, table[:, :depth]], axis=1)
    return dot(stacked, jnp.concatenate([high, high, low], axis=0))


def to_spectrum(blocks, slots, outer_fwd, turn, inner_fwd):
    outer = blocks.shape[0]
    first = dot(outer_fwd, jnp.concatenate([blocks, blocks], axis=0))
    turn, inner_fwd = turn(), inner_fwd()
    cos, sin = turn[:, :LANES], turn[:, LANES:]
    turned = []
    for s in range(slots):
        re = first[:outer, s * LANES : (s + 1) * LANES]
        im = first[outer:, s * LANES : (s + 1) * LANES]
        turned.append(jnp.concatenate([re * cos + im * sin, im * cos - re * sin], axis=1))
    return grouped(turned, inner_fwd)


def grouped(values, table):
    result = []
    for s in range(0, len(values), GROUP):
        part = values[s : s + GROUP]
        size = part[0].shape[0]
        product = times_table(jnp.concatenate(part, axis=0), table)
        result += [product[n * size : (n + 1) * size] for n in range(len(part))]
    return result


def filter_spectra(filters, outer_fwd, turn, inner):
    slots, length = filters.shape
    outer = length // LANES
    wide = filters[...].astype(f32)
    blocks = [wide[s].reshape(outer, LANES) for s in range(slots)]
    blocks = jnp.concatenate(blocks, axis=1).astype(bf16)
    return to_spectrum(
        blocks, slots, outer_fwd[...], lambda: turn[...], lambda: inner[: 4 * LANES, :]
    )


def convolve_kernel(
    signals, spectra, outer_fwd_far, turn_far, inner_far, outer_back_far, out, *scratch
):
    sources = (outer_fwd_far, turn_far, inner_far, outer_back_far)
    outer_fwd, turn_ref, inner, outer_back, result, sems = scratch
    copies = [
        pltpu.make_async_copy(source, scratch[n], sems.at[n]) for n, source in enumerate(sources)
    ]
    for copy in copies:
        copy.start()
    slots, outer = spectra.shape[:2]

    def turn_now():
        copies[1].wait()
        return turn_ref[...]

    def inner_now():
        copies[2].wait()
        return inner[: 4 * LANES, :]

    copies[0].wait()
    blocks = signals[...].reshape(outer, slots * LANES)
    parts = to_spectrum(blocks, slots, outer_fwd[...], turn_now, inner_now)
    turn = turn_ref[...]
    cos, sin = turn[:, :LANES], turn[:, LANES:]
    joint = []
    for s in range(slots):
        sig_re, sig_im = parts[s][:, :LANES], parts[s][:, LANES:]
        ker_re, ker_im = spectra[s, :, :LANES], spectra[s, :, LANES:]
        joint.append(
            jnp.concatenate(
                [sig_re * ker_re - sig_im * ker_im, sig_re * ker_im + sig_im * ker_re], axis=1
            )
        )
    turned = []
    for back in grouped(joint, inner[4 * LANES :, :]):
        re, im = back[:, :LANES], back[:, LANES:]
        turned.append(jnp.concatenate([re * cos - im * sin, im * cos + re * sin], axis=0))
    copies[3].wait()
    sends = []
    for s in range(0, slots, 2):
        pair = turned[s : s + 2]
        causal = table_times(outer_back[...], jnp.concatenate(pair, axis=1)).astype(bf16)
        lanes = pl.ds(s * LANES, len(pair) * LANES)
        result[:, :, lanes] = causal.reshape(out.shape[:2] + (len(pair) * LANES,))
        sends.append(
            pltpu.make_async_copy(
                result.at[:, :, lanes], out.at[:, :, lanes], sems.at[len(copies) + len(sends)]
            )
        )
        sends[-1].start()
    for send in sends:
        send.wait()


def iota(shape, axis):
    return lax.broadcasted_iota(jnp.int32, shape, axis)


def to_column(row):
    size = row.shape[1]
    same = iota((size, size), 0) == iota((size, size), 1)
    return jnp.sum(jnp.where(same, row, 0), axis=1, keepdims=True)


def channel_of_row(index_row, owners_row, owner_count, rows):
    slots = owners_row.shape[1]
    owners_col = to_column(owners_row)
    index_col = to_column(index_row)
    earlier = (owners_col == owners_row) & (iota((slots, slots), 1) < iota((slots, slots), 0))
    rank_col = jnp.sum(earlier.astype(jnp.int32), axis=1, keepdims=True)
    target_col = jnp.where(owners_col >= 0, rank_col * owner_count + owners_col, -1)
    hit = target_col == iota((slots, rows), 1)
    return jnp.sum(jnp.where(hit, index_col + 1, 0), axis=0, keepdims=True) - 1


def pick_rows(onehot, tile):
    picked = lax.dot_general(
        onehot, tile, (((1,), (1,)), ((), ())), preferred_element_type=f32
    )
    return [picked[:, i : i + LANES] for i in range(0, tile.shape[0], LANES)]


def fetch(sources, stages, sems, tile, first=0, ahead=3):
    count = stages[0].shape[0] // tile

    def copies(i):
        at = pl.multiple_of(i * tile, tile)
        return [
            pltpu.make_async_copy(
                source.at[pl.ds(first + at, tile), :], stage.at[pl.ds(at, tile), :], sems.at[n, i]
            )
            for n, (source, stage) in enumerate(zip(sources, stages))
        ]

    def start(i):
        for copy in copies(i):
            copy.start()

    for i in range(min(ahead, count)):
        start(i)

    def wait(i):
        for copy in copies(i):
            copy.wait()

        @pl.when(i + ahead < count)
        def _():
            start(i + ahead)

        return pl.multiple_of(i * tile, tile)

    return wait, count


def build_onehot(onehot, row):
    hit = iota(onehot.shape, 1) == to_column(row)[: onehot.shape[0]]
    onehot[...] = hit.astype(f32).astype(bf16)
    return hit


def pick_kernel(owner_count, slots, index, owners, gate, value, *refs):
    payload, picked, channels, gated_head = refs[:4]
    acc, gate_stage, value_stage, onehot, lists, list_sems, sems = refs[4:]
    tile = gate_stage.shape[0] // sems.shape[1]
    list_copies = [
        pltpu.make_async_copy(source, lists.at[n], list_sems.at[n])
        for n, source in enumerate((index, owners))
    ]
    for copy in list_copies:
        copy.start()
    wait, count = fetch((gate, value), (gate_stage, value_stage), sems, tile, 0, 4)
    for copy in list_copies:
        copy.wait()
    row = channel_of_row(lists[0], lists[1], owner_count, channels.shape[1])
    channels[...] = jnp.broadcast_to(row, channels.shape)
    build_onehot(onehot, row)

    def step(i, in_head):
        at = pl.ds(wait(i), tile)
        gated = gate_stage[at, :] * value_stage[at, :]
        if in_head:
            gated_head[at, :] = gated
        for n, block in enumerate(pick_rows(onehot[...], gated)):
            acc[i * (tile // LANES) + n] = block
            picked[i * (tile // LANES) + n] = block.astype(bf16)
        return 0

    head_tiles = gated_head.shape[0] // tile
    lax.fori_loop(0, head_tiles, lambda i, _: step(i, True), 0)
    lax.fori_loop(head_tiles, count, lambda i, _: step(i, False), 0)
    for s in range(slots):
        part = jnp.swapaxes(acc[:, s * owner_count : (s + 1) * owner_count, :], 0, 1)
        payload[:, :, s * LANES : (s + 1) * LANES] = part.astype(bf16)


def filter_kernel(filters, outer_fwd, turn, inner, spectra):
    for s, part in enumerate(filter_spectra(filters, outer_fwd, turn, inner)):
        spectra[s] = part


def first_kernel(channels, gated_head, skip, *refs):
    onehot, others, skip_wide, *outs = refs[4:11]

    def beside():
        hit = build_onehot(onehot, channels[0:1, :])
        kept = jnp.max(hit.astype(f32), axis=0, keepdims=True)
        others[...] = jnp.broadcast_to(1.0 - kept, others.shape)
        skip_col = jnp.sum(jnp.where(hit, skip[...], 0.0), axis=1, keepdims=True)
        skip_wide[...] = jnp.broadcast_to(skip_col, skip_wide.shape)

    base_pass(0, gated_head, onehot, others, skip, refs[:4], outs, refs[11:], beside)


def second_kernel(first, onehot, others, skip, *refs):
    base_pass(first, None, onehot, others, skip, refs[:4], refs[5:9], refs[9:], None)


def base_pass(first, head, onehot, others, skip, dense, outs, scratch, beside):
    base, sums, picked_gate, picked_res = outs
    gate_stage, value_stage, out_stage, res_stage, base_stage = scratch[:5]
    partial, base_sems, gate_sems, sems = scratch[5:]
    slab = out_stage.shape[1]
    tile = partial.shape[0]
    head_rows = 0 if head is None else head.shape[0]
    wait, count = fetch(dense[2:], (out_stage, res_stage), sems, tile, first)
    wait_gate, _ = fetch(
        dense[:2], (gate_stage, value_stage), gate_sems, tile, first + head_rows
    )
    if beside is not None:
        beside()
    head_tiles = head_rows // tile

    def copy(i):
        at = pl.multiple_of(i * tile, tile)
        return pltpu.make_async_copy(
            base_stage.at[pl.ds(at, tile), :], base.at[pl.ds(first + at, tile), :], base_sems.at[i]
        )

    def step(i, in_head):
        start = wait(i)
        gate_start = start if in_head else wait_gate(i - head_tiles)
        chunks = range(0, tile, CHUNK)
        totals = [jnp.zeros((CHUNK, LANES), f32) for _ in chunks]
        for j in range(0, slab, LANES):
            lanes = slice(j, j + LANES)
            skips = skip[:, lanes]
            mask = others[0:1, lanes].astype(bf16)
            for n, c in enumerate(chunks):
                at = pl.ds(start + c, CHUNK)
                gate_at = pl.ds(gate_start + c, CHUNK)
                if in_head:
                    gated = head[gate_at, lanes]
                else:
                    gated = gate_stage[gate_at, lanes] * value_stage[gate_at, lanes]
                mixed = out_stage[at, lanes].astype(f32) * (skips * gated.astype(f32))
                hidden = (res_stage[at, lanes].astype(f32) + mixed).astype(bf16) * mask
                base_stage[at, lanes] = hidden
                hidden = hidden.astype(f32)
                totals[n] = totals[n] + hidden * hidden
        copy(i).start()
        for n, c in enumerate(chunks):
            partial[c : c + CHUNK, :] = totals[n]
        total = jnp.sum(partial[...].T, axis=0, keepdims=True)
        at = pl.ds(start, tile)
        both = jnp.concatenate([out_stage[at, :], res_stage[at, :]], axis=0)
        both = pick_rows(onehot[...], both)
        picks_gate, picks_res = both[: tile // LANES], both[tile // LANES :]
        for n in range(tile // LANES):
            block = i * (tile // LANES) + n
            sums[block] = total[:, n * LANES : (n + 1) * LANES]
            picked_gate[block] = picks_gate[n].astype(bf16)
            picked_res[block] = picks_res[n].astype(bf16)
        return 0

    if head_tiles:
        lax.fori_loop(0, head_tiles, lambda i, _: step(i, True), 0)
    lax.fori_loop(head_tiles, count, lambda i, _: step(i, False), 0)
    lax.fori_loop(0, count, lambda i, _: (copy(i).wait(), 0)[1], 0)


def kept_kernel(conv, picked, skip_wide, *refs):
    hidden, totals = refs[-2:]
    owner_count, blocks = conv.shape[:2]
    first = 0
    for n in range(0, len(refs) - 2, 3):
        sums, picked_gate, picked_res = refs[n : n + 3]
        size = sums.shape[0]
        at_h = slice(first, first + size)
        total = jnp.zeros((size, LANES), f32)
        for s in range(conv.shape[2] // LANES):
            at = slice(s * owner_count, (s + 1) * owner_count)
            lanes = slice(s * LANES, (s + 1) * LANES)
            wide = jnp.swapaxes(conv[:, at_h, lanes].astype(f32), 0, 1)
            wide = wide + skip_wide[at, :] * picked[at_h, at, :].astype(f32)
            value = picked_res[:, at, :].astype(f32) + picked_gate[:, at, :].astype(f32) * wide
            value = value.astype(bf16)
            hidden[at_h, at, :] = value
            value = value.astype(f32)
            total = total + jnp.sum(value * value, axis=1)
        for i in range(size):
            totals[first + i] = total[i : i + 1, :] + sums[i]
        first = first + size


def hidden_kernel(base, hidden_kept, onehot, hidden, held, base_stage, base_sems, sems):
    slab = held.shape[1]
    wide = min(slab, 2 * LANES)
    count = sems.shape[0]
    tile = held.shape[0] // count
    wait, _ = fetch((base,), (base_stage,), base_sems, tile, 0, 4)

    def copy(i):
        rows = pl.ds(pl.multiple_of(i * tile, tile), tile)
        return pltpu.make_async_copy(held.at[rows, :], hidden.at[rows, :], sems.at[i])

    def step(i, _):
        blocks = range(tile // LANES)
        kept = [hidden_kept[i * (tile // LANES) + n].astype(f32).T.astype(bf16) for n in blocks]
        kept = jnp.concatenate(kept, axis=0)
        rows = pl.ds(wait(i), tile)
        for j in range(0, slab, wide):
            lanes = slice(j, j + wide)
            placed = dot(kept, onehot[:, lanes]).astype(bf16)
            held[rows, lanes] = base_stage[rows, lanes] + placed
        copy(i).start()
        return 0

    lax.fori_loop(0, count, step, 0)
    lax.fori_loop(0, count, lambda i, _: (copy(i).wait(), 0)[1], 0)


def norm_kernel(width, count, *refs):
    parts = refs[:count]
    held, gain, normed, stage, turned, sems = refs[count:]
    slab = held.shape[1]

    def copy(i):
        rows = pl.ds(pl.multiple_of(i * LANES, LANES), LANES)
        return pltpu.make_async_copy(stage.at[rows, :], normed.at[rows, :], sems.at[i])

    def step(i, _):
        total = parts[0][i]
        for part in parts[1:]:
            total = total + part[i]
        scale = lax.rsqrt(total / width + norm_eps)
        turned[...] = jnp.broadcast_to(scale, (LANES, LANES)).T
        first = pl.multiple_of(i * LANES, LANES)
        for c in range(0, LANES, CHUNK):
            at = pl.ds(first + c, CHUNK)
            scales = turned[c : c + CHUNK, :]
            for j in range(0, slab, LANES):
                lanes = slice(j, j + LANES)
                value = held[at, lanes].astype(f32) * scales * gain[:, lanes]
                stage[at, lanes] = value.astype(bf16)
        copy(i).start()
        return 0

    lax.fori_loop(0, sems.shape[0], step, 0)
    lax.fori_loop(0, sems.shape[0], lambda i, _: (copy(i).wait(), 0)[1], 0)


def in_hbm(x):
    return pltpu.with_memory_space_constraint(x, pltpu.HBM)


def in_vmem(x):
    return pltpu.with_memory_space_constraint(x, pltpu.VMEM)


def call(kernel, outs, ins, flops, moved, limit, scratch=(), far=(), far_outs=(), alias=None):
    near = pl.BlockSpec(memory_space=pltpu.VMEM)
    away = pl.BlockSpec(memory_space=pl.ANY)
    return pl.pallas_call(
        kernel,
        out_shape=outs,
        in_specs=[away if n in far else near for n in range(len(ins))],
        out_specs=[away if n in far_outs else near for n in range(len(outs))],
        scratch_shapes=list(scratch),
        input_output_aliases=alias or {},
        compiler_params=pltpu.CompilerParams(vmem_limit_bytes=limit),
        cost_estimate=pl.CostEstimate(flops=flops, bytes_accessed=moved, transcendentals=0),
    )(*ins)


def local(
    gate_in, value_in, out_gate, residual, filters, kept_index, kept_owner, skip_bias, norm_gain
):
    tok_rows, slab = gate_in.shape
    slots, length = filters.shape[2:]
    chan_devices = lax.axis_size("chan")
    owner_count = lax.axis_size("seqo") * lax.axis_size("seqi")
    rows = slots * owner_count
    lanes_rows = -(-rows // LANES) * LANES
    blocks = tok_rows // LANES
    outer = length // LANES
    tile = TILE if tok_rows % TILE == 0 else LANES
    dense = tok_rows * slab * 2
    sds = jax.ShapeDtypeStruct
    tables = [in_hbm(jnp.asarray(x)) for x in dft_tables(length)]
    outer_fwd, turn, inner, outer_back = tables
    skip_row = skip_bias[None, :]
    gain_row = norm_gain[None, :]
    gate_in, value_in, out_gate, residual = map(in_hbm, (gate_in, value_in, out_gate, residual))
    picks = sds((blocks, rows, LANES), bf16)
    row_sums = sds((blocks, 1, LANES), f32)
    buffer = (owner_count, blocks, slots * LANES)
    whole = (tok_rows, slab)
    head_rows = tok_rows // 4 // tile * tile

    payload, picked, channels, gated_head = call(
        functools.partial(pick_kernel, owner_count, slots),
        [
            sds(buffer, bf16),
            picks,
            sds((8, lanes_rows), jnp.int32),
            pltpu.VMEM((head_rows, slab), bf16),
        ],
        [in_hbm(kept_index), in_hbm(kept_owner), gate_in, value_in],
        2 * tok_rows * slab * rows,
        2 * dense,
        24 * MIB,
        scratch=[
            pltpu.VMEM((blocks, rows, LANES), f32),
            pltpu.VMEM(whole, bf16),
            pltpu.VMEM(whole, bf16),
            pltpu.VMEM((rows, slab), bf16),
            pltpu.VMEM((2,) + kept_index.shape, jnp.int32),
            pltpu.SemaphoreType.DMA((2,)),
            pltpu.SemaphoreType.DMA((2, tok_rows // tile)),
        ],
        far=(0, 1, 2, 3),
    )

    incoming = lax.all_to_all(payload, ("seqo", "seqi"), split_axis=0, concat_axis=0, tiled=True)

    dense_ins = [gate_in, value_in, out_gate, residual]

    def base_parts(count, head):
        part = count * LANES
        outs = [
            pltpu.HBM(whole, bf16),
            sds((count, 1, LANES), f32),
            sds((count, rows, LANES), bf16),
            sds((count, rows, LANES), bf16),
        ]
        scratch = [
            pltpu.VMEM((part - head, slab), bf16),
            pltpu.VMEM((part - head, slab), bf16),
            pltpu.VMEM((part, slab), bf16),
            pltpu.VMEM((part, slab), bf16),
            pltpu.VMEM((part, slab), bf16),
            pltpu.VMEM((LANES, LANES), f32),
            pltpu.SemaphoreType.DMA((count,)),
            pltpu.SemaphoreType.DMA((2, (part - head) // LANES)),
            pltpu.SemaphoreType.DMA((2, count)),
        ]
        return outs, scratch, 4 * part * slab * rows, 10 * part * slab

    early = max(head_rows // LANES + 1, blocks * EARLY // 16)
    outs, scratch, flops, moved = base_parts(early, head_rows)
    onehot, others, skip_wide, base, *first_picks = call(
        first_kernel,
        [sds((rows, slab), bf16), sds((8, slab), f32), sds((rows, LANES), f32)] + outs,
        [channels, in_vmem(gated_head), skip_row] + dense_ins,
        flops,
        moved,
        36 * MIB,
        scratch=scratch,
        far=(3, 4, 5, 6),
        far_outs=(3,),
    )
    (spectra,) = call(
        filter_kernel,
        [pltpu.VMEM((slots, outer, 2 * LANES), f32)],
        [filters[0, 0]] + [jnp.asarray(x) for x in dft_tables(length)[:3]],
        2 * slots * length * 2 * (2 * outer + 6 * LANES),
        4 * MIB,
        16 * MIB,
    )
    spectra, base = lax.optimization_barrier((spectra, base))

    conv_ins = [incoming, in_vmem(spectra), outer_fwd, turn, inner, outer_back]
    (convolved,) = call(
        convolve_kernel,
        [pltpu.HBM(buffer, bf16)],
        conv_ins,
        2 * slots * length * 2 * (5 * outer + 12 * LANES),
        8 * MIB,
        20 * MIB,
        scratch=[pltpu.VMEM(x.shape, x.dtype) for x in conv_ins[2:]]
        + [pltpu.VMEM(buffer, bf16), pltpu.SemaphoreType.DMA((len(conv_ins) + slots,))],
        far=tuple(range(2, len(conv_ins))),
        far_outs=(0,),
    )
    convolved, onehot = lax.optimization_barrier((convolved, onehot))

    returned = lax.all_to_all(convolved, ("seqo", "seqi"), split_axis=0, concat_axis=0, tiled=True)

    outs, scratch, flops, moved = base_parts(blocks - early, 0)
    base, *more_picks = call(
        functools.partial(second_kernel, early * LANES),
        outs,
        [onehot, others, skip_row] + dense_ins + [base],
        flops,
        moved,
        36 * MIB,
        scratch=scratch,
        far=(3, 4, 5, 6, 7),
        far_outs=(0,),
        alias={7: 0},
    )

    hidden_kept, totals = call(
        kept_kernel,
        [picks, row_sums],
        [returned, picked, skip_wide, *first_picks, *more_picks],
        8 * rows * tok_rows,
        10 * rows * tok_rows,
        16 * MIB,
    )

    parts = [totals]
    for shift in range(1, chan_devices):
        ring = [(i, (i + shift) % chan_devices) for i in range(chan_devices)]
        parts.append(lax.ppermute(totals, "chan", ring))

    hidden, held = call(
        hidden_kernel,
        [pltpu.HBM(whole, bf16), pltpu.VMEM(whole, bf16)],
        [in_hbm(base), hidden_kept, onehot],
        2 * tok_rows * slab * rows,
        2 * dense,
        16 * MIB,
        scratch=[
            pltpu.VMEM(whole, bf16),
            pltpu.SemaphoreType.DMA((1, tok_rows // tile)),
            pltpu.SemaphoreType.DMA((tok_rows // tile,)),
        ],
        far=(0,),
        far_outs=(0,),
    )
    (normed,) = call(
        functools.partial(norm_kernel, float(slab * chan_devices), len(parts)),
        [pltpu.HBM(whole, bf16)],
        parts + [in_vmem(held), gain_row],
        4 * tok_rows * slab,
        2 * dense,
        16 * MIB,
        scratch=[
            pltpu.VMEM(whole, bf16),
            pltpu.VMEM((LANES, LANES), f32),
            pltpu.SemaphoreType.DMA((blocks,)),
        ],
        far_outs=(0,),
    )
    return (hidden, normed)


def solution(mesh):
    positions = P(("seqo", "seqi"), "chan")
    in_specs = (
        positions,
        positions,
        positions,
        positions,
        P("chan", ("seqo", "seqi"), None, None),
        P("chan", None),
        P("chan", None),
        P("chan"),
        P("chan"),
    )
    return jax.shard_map(
        local, mesh=mesh, in_specs=in_specs, out_specs=(positions, positions), check_vma=False
    )
```

```python
import functools

import jax
import jax.numpy as jnp
import numpy as np
from jax import lax
from jax.experimental import pallas as pl
from jax.experimental.pallas import tpu as pltpu
from jax.sharding import PartitionSpec as P

LANES = 128
TILE = 256
CHUNK = 16
GROUP = 3
AHEAD = 3
EARLY = 8
MIB = 1 << 20
norm_eps = 1e-06
f32 = jnp.float32
bf16 = jnp.bfloat16


def split_np(table):
    high = table.astype(jnp.bfloat16)
    low = (table - high.astype(np.float64)).astype(jnp.bfloat16)
    return high, low


def dft_tables(length):
    inner = LANES
    outer = length // inner
    a = np.arange(outer)
    b = np.arange(inner)
    quarter = np.arange(outer) + 0.25
    outer_angle = 2 * np.pi / outer * np.mod(quarter[:, None] * a[None, :], outer)
    turn_angle = 2 * np.pi / length * (quarter[:, None] * b[None, :])
    inner_angle = 2 * np.pi / inner * np.mod(b[:, None] * b[None, :], inner)
    outer_fwd = np.concatenate([np.cos(outer_angle), -np.sin(outer_angle)], axis=0)
    c, s = np.cos(inner_angle), np.sin(inner_angle)
    inner_fwd = np.concatenate(
        [np.concatenate([c, -s], axis=1), np.concatenate([s, c], axis=1)], axis=0
    )
    inner_back = np.concatenate(
        [np.concatenate([c, s], axis=1), np.concatenate([-s, c], axis=1)], axis=0
    )
    outer_back = np.concatenate([np.cos(outer_angle).T, -np.sin(outer_angle).T], axis=1) / length
    turn = np.concatenate([np.cos(turn_angle), np.sin(turn_angle)], axis=1).astype(np.float32)
    outer_fwd = np.concatenate(split_np(outer_fwd), axis=0)
    inner = np.concatenate(split_np(inner_fwd) + split_np(inner_back), axis=0)
    outer_back = np.concatenate(split_np(outer_back), axis=1)
    return outer_fwd, turn, inner, outer_back


def split(value):
    high = value.astype(bf16)
    low = (value - high.astype(f32)).astype(bf16)
    return high, low


def dot(x, y):
    return jnp.dot(x, y, preferred_element_type=f32)


def dot_rows(x, y):
    return lax.dot_general(x, y, (((0,), (0,)), ((), ())), preferred_element_type=f32)


def times_table(value, table):
    high, low = split(value)
    depth = value.shape[1]
    stacked = jnp.concatenate([table, table[:depth]], axis=0)
    return dot(jnp.concatenate([high, high, low], axis=1), stacked)


def table_times(table, value):
    high, low = split(value)
    depth = value.shape[0]
    stacked = jnp.concatenate([table, table[:, :depth]], axis=1)
    return dot(stacked, jnp.concatenate([high, high, low], axis=0))


def to_spectrum(blocks, slots, outer_fwd, turn, inner_fwd):
    outer = blocks.shape[0]
    first = dot(outer_fwd(0), blocks)
    first = first + dot(outer_fwd(1), blocks)
    turn, inner_fwd = turn(), inner_fwd()
    cos, sin = turn[:, :LANES], turn[:, LANES:]
    turned = []
    for s in range(slots):
        re = first[:outer, s * LANES : (s + 1) * LANES]
        im = first[outer:, s * LANES : (s + 1) * LANES]
        turned.append(jnp.concatenate([re * cos + im * sin, im * cos - re * sin], axis=1))
    return grouped(turned, inner_fwd)


def grouped(values, table):
    result = []
    for s in range(0, len(values), GROUP):
        part = values[s : s + GROUP]
        size = part[0].shape[0]
        product = times_table(jnp.concatenate(part, axis=0), table)
        result += [product[n * size : (n + 1) * size] for n in range(len(part))]
    return result


def filter_spectra(filters, outer_fwd, turn, inner):
    slots, length = filters.shape
    outer = length // LANES
    wide = filters[...].astype(f32)
    blocks = [wide[s].reshape(outer, LANES) for s in range(slots)]
    blocks = jnp.concatenate(blocks, axis=1).astype(bf16)
    return to_spectrum(
        blocks,
        slots,
        lambda n: outer_fwd[2 * outer * n : 2 * outer * (n + 1), :],
        lambda: turn[...],
        lambda: inner[: 4 * LANES, :],
    )


def convolve_kernel(
    signals, spectra, outer_fwd_far, turn_far, inner_far, outer_back_far, out, *scratch
):
    sources = (outer_fwd_far, turn_far, inner_far, outer_back_far)
    outer_fwd, turn_ref, inner, outer_back, result, sems = scratch
    slots, outer = spectra.shape[:2]
    halves = [pl.ds(2 * outer * n, 2 * outer) for n in range(2)]
    copies = [
        pltpu.make_async_copy(outer_fwd_far.at[half, :], outer_fwd.at[half, :], sems.at[n])
        for n, half in enumerate(halves)
    ] + [
        pltpu.make_async_copy(source, scratch[n], sems.at[n + 1])
        for n, source in enumerate(sources)
        if n > 0
    ]
    for copy in copies:
        copy.start()

    def outer_now(n):
        copies[n].wait()
        return outer_fwd[halves[n], :]

    def turn_now():
        copies[2].wait()
        return turn_ref[...]

    def inner_now():
        copies[3].wait()
        return inner[: 4 * LANES, :]

    blocks = signals[...].reshape(outer, slots * LANES)
    parts = to_spectrum(blocks, slots, outer_now, turn_now, inner_now)
    turn = turn_ref[...]
    cos, sin = turn[:, :LANES], turn[:, LANES:]
    joint = []
    for s in range(slots):
        sig_re, sig_im = parts[s][:, :LANES], parts[s][:, LANES:]
        ker_re, ker_im = spectra[s, :, :LANES], spectra[s, :, LANES:]
        joint.append(
            jnp.concatenate(
                [sig_re * ker_re - sig_im * ker_im, sig_re * ker_im + sig_im * ker_re], axis=1
            )
        )
    turned = []
    for back in grouped(joint, inner[4 * LANES :, :]):
        re, im = back[:, :LANES], back[:, LANES:]
        turned.append(jnp.concatenate([re * cos - im * sin, im * cos + re * sin], axis=0))
    copies[4].wait()
    sends = []
    for s in range(0, slots, 2):
        pair = turned[s : s + 2]
        causal = table_times(outer_back[...], jnp.concatenate(pair, axis=1)).astype(bf16)
        lanes = pl.ds(s * LANES, len(pair) * LANES)
        result[:, :, lanes] = causal.reshape(out.shape[:2] + (len(pair) * LANES,))
        sends.append(
            pltpu.make_async_copy(
                result.at[:, :, lanes], out.at[:, :, lanes], sems.at[len(copies) + len(sends)]
            )
        )
        sends[-1].start()
    for send in sends:
        send.wait()


def iota(shape, axis):
    return lax.broadcasted_iota(jnp.int32, shape, axis)


def to_column(row):
    size = row.shape[1]
    same = iota((size, size), 0) == iota((size, size), 1)
    return jnp.sum(jnp.where(same, row, 0), axis=1, keepdims=True)


def channel_of_row(index_row, owners_row, owner_count, rows):
    slots = owners_row.shape[1]
    owners_col = to_column(owners_row)
    index_col = to_column(index_row)
    earlier = (owners_col == owners_row) & (iota((slots, slots), 1) < iota((slots, slots), 0))
    rank_col = jnp.sum(earlier.astype(jnp.int32), axis=1, keepdims=True)
    target_col = jnp.where(owners_col >= 0, rank_col * owner_count + owners_col, -1)
    hit = target_col == iota((slots, rows), 1)
    return jnp.sum(jnp.where(hit, index_col + 1, 0), axis=0, keepdims=True) - 1


def pick_rows(onehot, tile):
    picked = lax.dot_general(
        onehot, tile, (((1,), (1,)), ((), ())), preferred_element_type=f32
    )
    return [picked[:, i : i + LANES] for i in range(0, tile.shape[0], LANES)]


def fetch(sources, stages, sems, tile, first=0, ahead=3, begin=True):
    count = stages[0].shape[0] // tile

    def copies(i):
        at = pl.multiple_of(i * tile, tile)
        return [
            pltpu.make_async_copy(
                source.at[pl.ds(first + at, tile), :], stage.at[pl.ds(at, tile), :], sems.at[n, i]
            )
            for n, (source, stage) in enumerate(zip(sources, stages))
        ]

    def start(i):
        for copy in copies(i):
            copy.start()

    ahead = min(ahead, count)
    if begin:
        for i in range(ahead):
            start(i)

    def wait(i):
        for copy in copies(i):
            copy.wait()

        @pl.when(i + ahead < count)
        def _():
            start(i + ahead)

        return pl.multiple_of(i * tile, tile)

    return start, wait, ahead


def build_onehot(onehot, row):
    hit = iota(onehot.shape, 1) == to_column(row)[: onehot.shape[0]]
    onehot[...] = hit.astype(f32).astype(bf16)
    return hit


def pick_kernel(owner_count, slots, index, owners, gate, value, *refs):
    payload, picked, channels, gated_head = refs[:4]
    acc, gate_stage, value_stage, onehot, lists, list_sems, sems = refs[4:]
    tile = gate_stage.shape[0] // sems.shape[1]
    list_copies = [
        pltpu.make_async_copy(source, lists.at[n], list_sems.at[n])
        for n, source in enumerate((index, owners))
    ]
    for copy in list_copies:
        copy.start()
    count = sems.shape[1]
    _, wait, _ = fetch((gate, value), (gate_stage, value_stage), sems, tile, 0, 4)
    for copy in list_copies:
        copy.wait()
    row = channel_of_row(lists[0], lists[1], owner_count, channels.shape[1])
    channels[...] = jnp.broadcast_to(row, channels.shape)
    build_onehot(onehot, row)

    def step(i, in_head):
        at = pl.ds(wait(i), tile)
        gated = gate_stage[at, :] * value_stage[at, :]
        if in_head:
            gated_head[at, :] = gated
        for n, block in enumerate(pick_rows(onehot[...], gated)):
            acc[i * (tile // LANES) + n] = block
            picked[i * (tile // LANES) + n] = block.astype(bf16)
        return 0

    head_tiles = gated_head.shape[0] // tile
    lax.fori_loop(0, head_tiles, lambda i, _: step(i, True), 0)
    lax.fori_loop(head_tiles, count, lambda i, _: step(i, False), 0)
    for s in range(slots):
        part = jnp.swapaxes(acc[:, s * owner_count : (s + 1) * owner_count, :], 0, 1)
        payload[:, :, s * LANES : (s + 1) * LANES] = part.astype(bf16)


def filter_kernel(filters, outer_fwd, turn, inner, spectra):
    for s, part in enumerate(filter_spectra(filters, outer_fwd, turn, inner)):
        spectra[s] = part


def first_kernel(channels, gated_head, skip, *refs):
    onehot, others, skip_wide, *outs = refs[4:11]

    def beside():
        hit = build_onehot(onehot, channels[0:1, :])
        kept = jnp.max(hit.astype(f32), axis=0, keepdims=True)
        others[...] = jnp.broadcast_to(1.0 - kept, others.shape)
        skip_col = jnp.sum(jnp.where(hit, skip[...], 0.0), axis=1, keepdims=True)
        skip_wide[...] = jnp.broadcast_to(skip_col, skip_wide.shape)

    base_pass(0, gated_head, onehot, others, skip, refs[:4], outs, refs[11:], beside)


def second_kernel(first, onehot, others, skip, *refs):
    base_pass(first, None, onehot, others, skip, refs[:4], refs[5:9], refs[9:], None)


def base_pass(first, head, onehot, others, skip, dense, outs, scratch, beside):
    base, sums, picked_gate, picked_res = outs
    gate_stage, value_stage, out_stage, res_stage, base_stage = scratch[:5]
    partial, base_sems, gate_sems, sems = scratch[5:]
    slab = out_stage.shape[1]
    tile = partial.shape[0]
    head_rows = 0 if head is None else head.shape[0]
    head_tiles = head_rows // tile
    count = sems.shape[1]
    late = head_tiles > AHEAD
    _, wait, _ = fetch(dense[2:], (out_stage, res_stage), sems, tile, first, AHEAD)
    start_gate, wait_gate, early = fetch(
        dense[:2], (gate_stage, value_stage), gate_sems, tile, first + head_rows, AHEAD, not late
    )
    if beside is not None:
        beside()

    def copy(i):
        at = pl.multiple_of(i * tile, tile)
        return pltpu.make_async_copy(
            base_stage.at[pl.ds(at, tile), :], base.at[pl.ds(first + at, tile), :], base_sems.at[i]
        )

    def step(i, in_head):
        start = wait(i)
        if in_head and late:

            @pl.when((i > 0) & (i <= early))
            def _():
                start_gate(i - 1)

        gate_start = start if in_head else wait_gate(i - head_tiles)
        chunks = range(0, tile, CHUNK)
        totals = [jnp.zeros((CHUNK, LANES), f32) for _ in chunks]
        for j in range(0, slab, LANES):
            lanes = slice(j, j + LANES)
            skips = skip[:, lanes]
            mask = others[0:1, lanes].astype(bf16)
            for n, c in enumerate(chunks):
                at = pl.ds(start + c, CHUNK)
                gate_at = pl.ds(gate_start + c, CHUNK)
                if in_head:
                    gated = head[gate_at, lanes]
                else:
                    gated = gate_stage[gate_at, lanes] * value_stage[gate_at, lanes]
                mixed = out_stage[at, lanes].astype(f32) * (skips * gated.astype(f32))
                hidden = (res_stage[at, lanes].astype(f32) + mixed).astype(bf16) * mask
                base_stage[at, lanes] = hidden
                hidden = hidden.astype(f32)
                totals[n] = totals[n] + hidden * hidden
        copy(i).start()
        for n, c in enumerate(chunks):
            partial[c : c + CHUNK, :] = totals[n]
        total = jnp.sum(partial[...].T, axis=0, keepdims=True)
        at = pl.ds(start, tile)
        both = jnp.concatenate([out_stage[at, :], res_stage[at, :]], axis=0)
        both = pick_rows(onehot[...], both)
        picks_gate, picks_res = both[: tile // LANES], both[tile // LANES :]
        for n in range(tile // LANES):
            block = i * (tile // LANES) + n
            sums[block] = total[:, n * LANES : (n + 1) * LANES]
            picked_gate[block] = picks_gate[n].astype(bf16)
            picked_res[block] = picks_res[n].astype(bf16)
        return 0

    if head_tiles:
        lax.fori_loop(0, head_tiles, lambda i, _: step(i, True), 0)
    lax.fori_loop(head_tiles, count, lambda i, _: step(i, False), 0)
    lax.fori_loop(0, count, lambda i, _: (copy(i).wait(), 0)[1], 0)


def kept_kernel(conv, picked, skip_wide, *refs):
    hidden, totals = refs[-2:]
    owner_count, blocks = conv.shape[:2]
    first = 0
    for n in range(0, len(refs) - 2, 3):
        sums, picked_gate, picked_res = refs[n : n + 3]
        size = sums.shape[0]
        at_h = slice(first, first + size)
        total = jnp.zeros((size, LANES), f32)
        for s in range(conv.shape[2] // LANES):
            at = slice(s * owner_count, (s + 1) * owner_count)
            lanes = slice(s * LANES, (s + 1) * LANES)
            wide = jnp.swapaxes(conv[:, at_h, lanes].astype(f32), 0, 1)
            wide = wide + skip_wide[at, :] * picked[at_h, at, :].astype(f32)
            value = picked_res[:, at, :].astype(f32) + picked_gate[:, at, :].astype(f32) * wide
            value = value.astype(bf16)
            hidden[at_h, at, :] = value
            value = value.astype(f32)
            total = total + jnp.sum(value * value, axis=1)
        for i in range(size):
            totals[first + i] = total[i : i + 1, :] + sums[i]
        first = first + size


def hidden_kernel(base, hidden_kept, onehot, hidden, held, base_stage, base_sems, sems):
    slab = held.shape[1]
    wide = min(slab, 2 * LANES)
    count = sems.shape[0]
    tile = held.shape[0] // count
    _, wait, _ = fetch((base,), (base_stage,), base_sems, tile, 0, 4)

    def copy(i):
        rows = pl.ds(pl.multiple_of(i * tile, tile), tile)
        return pltpu.make_async_copy(held.at[rows, :], hidden.at[rows, :], sems.at[i])

    def step(i, _):
        blocks = range(tile // LANES)
        kept = [hidden_kept[i * (tile // LANES) + n].astype(f32).T.astype(bf16) for n in blocks]
        kept = jnp.concatenate(kept, axis=0)
        rows = pl.ds(wait(i), tile)
        for j in range(0, slab, wide):
            lanes = slice(j, j + wide)
            placed = dot(kept, onehot[:, lanes]).astype(bf16)
            held[rows, lanes] = base_stage[rows, lanes] + placed
        copy(i).start()
        return 0

    lax.fori_loop(0, count, step, 0)
    lax.fori_loop(0, count, lambda i, _: (copy(i).wait(), 0)[1], 0)


def norm_kernel(width, count, *refs):
    parts = refs[:count]
    held, gain, normed, stage, turned, sems = refs[count:]
    slab = held.shape[1]

    def copy(i):
        rows = pl.ds(pl.multiple_of(i * LANES, LANES), LANES)
        return pltpu.make_async_copy(stage.at[rows, :], normed.at[rows, :], sems.at[i])

    def step(i, _):
        total = parts[0][i]
        for part in parts[1:]:
            total = total + part[i]
        scale = lax.rsqrt(total / width + norm_eps)
        turned[...] = jnp.broadcast_to(scale, (LANES, LANES)).T
        first = pl.multiple_of(i * LANES, LANES)
        for c in range(0, LANES, CHUNK):
            at = pl.ds(first + c, CHUNK)
            scales = turned[c : c + CHUNK, :]
            for j in range(0, slab, LANES):
                lanes = slice(j, j + LANES)
                value = held[at, lanes].astype(f32) * scales * gain[:, lanes]
                stage[at, lanes] = value.astype(bf16)
        copy(i).start()
        return 0

    lax.fori_loop(0, sems.shape[0], step, 0)
    lax.fori_loop(0, sems.shape[0], lambda i, _: (copy(i).wait(), 0)[1], 0)


def in_hbm(x):
    return pltpu.with_memory_space_constraint(x, pltpu.HBM)


def in_vmem(x):
    return pltpu.with_memory_space_constraint(x, pltpu.VMEM)


def call(kernel, outs, ins, flops, moved, limit, scratch=(), far=(), far_outs=(), alias=None):
    near = pl.BlockSpec(memory_space=pltpu.VMEM)
    away = pl.BlockSpec(memory_space=pl.ANY)
    return pl.pallas_call(
        kernel,
        out_shape=outs,
        in_specs=[away if n in far else near for n in range(len(ins))],
        out_specs=[away if n in far_outs else near for n in range(len(outs))],
        scratch_shapes=list(scratch),
        input_output_aliases=alias or {},
        compiler_params=pltpu.CompilerParams(vmem_limit_bytes=limit),
        cost_estimate=pl.CostEstimate(flops=flops, bytes_accessed=moved, transcendentals=0),
    )(*ins)


def local(
    gate_in, value_in, out_gate, residual, filters, kept_index, kept_owner, skip_bias, norm_gain
):
    tok_rows, slab = gate_in.shape
    slots, length = filters.shape[2:]
    chan_devices = lax.axis_size("chan")
    owner_count = lax.axis_size("seqo") * lax.axis_size("seqi")
    rows = slots * owner_count
    lanes_rows = -(-rows // LANES) * LANES
    blocks = tok_rows // LANES
    outer = length // LANES
    tile = TILE if tok_rows % TILE == 0 else LANES
    dense = tok_rows * slab * 2
    sds = jax.ShapeDtypeStruct
    tables = [in_hbm(jnp.asarray(x)) for x in dft_tables(length)]
    outer_fwd, turn, inner, outer_back = tables
    skip_row = skip_bias[None, :]
    gain_row = norm_gain[None, :]
    gate_in, value_in, out_gate, residual = map(in_hbm, (gate_in, value_in, out_gate, residual))
    picks = sds((blocks, rows, LANES), bf16)
    row_sums = sds((blocks, 1, LANES), f32)
    buffer = (owner_count, blocks, slots * LANES)
    whole = (tok_rows, slab)
    head_rows = tok_rows // 4 // tile * tile

    payload, picked, channels, gated_head = call(
        functools.partial(pick_kernel, owner_count, slots),
        [
            sds(buffer, bf16),
            picks,
            sds((8, lanes_rows), jnp.int32),
            pltpu.VMEM((head_rows, slab), bf16),
        ],
        [in_hbm(kept_index), in_hbm(kept_owner), gate_in, value_in],
        2 * tok_rows * slab * rows,
        2 * dense,
        24 * MIB,
        scratch=[
            pltpu.VMEM((blocks, rows, LANES), f32),
            pltpu.VMEM(whole, bf16),
            pltpu.VMEM(whole, bf16),
            pltpu.VMEM((rows, slab), bf16),
            pltpu.VMEM((2,) + kept_index.shape, jnp.int32),
            pltpu.SemaphoreType.DMA((2,)),
            pltpu.SemaphoreType.DMA((2, tok_rows // tile)),
        ],
        far=(0, 1, 2, 3),
    )

    incoming = lax.all_to_all(payload, ("seqo", "seqi"), split_axis=0, concat_axis=0, tiled=True)

    dense_ins = [gate_in, value_in, out_gate, residual]

    def base_parts(count, head):
        part = count * LANES
        outs = [
            pltpu.HBM(whole, bf16),
            sds((count, 1, LANES), f32),
            sds((count, rows, LANES), bf16),
            sds((count, rows, LANES), bf16),
        ]
        scratch = [
            pltpu.VMEM((part - head, slab), bf16),
            pltpu.VMEM((part - head, slab), bf16),
            pltpu.VMEM((part, slab), bf16),
            pltpu.VMEM((part, slab), bf16),
            pltpu.VMEM((part, slab), bf16),
            pltpu.VMEM((LANES, LANES), f32),
            pltpu.SemaphoreType.DMA((count,)),
            pltpu.SemaphoreType.DMA((2, (part - head) // LANES)),
            pltpu.SemaphoreType.DMA((2, count)),
        ]
        return outs, scratch, 4 * part * slab * rows, 10 * part * slab

    early = max(head_rows // LANES + 1, blocks * EARLY // 16)
    outs, scratch, flops, moved = base_parts(early, head_rows)
    onehot, others, skip_wide, base, *first_picks = call(
        first_kernel,
        [sds((rows, slab), bf16), sds((8, slab), f32), sds((rows, LANES), f32)] + outs,
        [channels, in_vmem(gated_head), skip_row] + dense_ins,
        flops,
        moved,
        36 * MIB,
        scratch=scratch,
        far=(3, 4, 5, 6),
        far_outs=(3,),
    )
    (spectra,) = call(
        filter_kernel,
        [pltpu.VMEM((slots, outer, 2 * LANES), f32)],
        [filters[0, 0]] + [jnp.asarray(x) for x in dft_tables(length)[:3]],
        2 * slots * length * 2 * (2 * outer + 6 * LANES),
        4 * MIB,
        16 * MIB,
    )
    spectra, base = lax.optimization_barrier((spectra, base))

    conv_ins = [incoming, in_vmem(spectra), outer_fwd, turn, inner, outer_back]
    (convolved,) = call(
        convolve_kernel,
        [pltpu.HBM(buffer, bf16)],
        conv_ins,
        2 * slots * length * 2 * (5 * outer + 12 * LANES),
        8 * MIB,
        20 * MIB,
        scratch=[pltpu.VMEM(x.shape, x.dtype) for x in conv_ins[2:]]
        + [pltpu.VMEM(buffer, bf16), pltpu.SemaphoreType.DMA((len(conv_ins) + slots,))],
        far=tuple(range(2, len(conv_ins))),
        far_outs=(0,),
    )
    convolved, onehot = lax.optimization_barrier((convolved, onehot))

    returned = lax.all_to_all(convolved, ("seqo", "seqi"), split_axis=0, concat_axis=0, tiled=True)

    outs, scratch, flops, moved = base_parts(blocks - early, 0)
    base, *more_picks = call(
        functools.partial(second_kernel, early * LANES),
        outs,
        [onehot, others, skip_row] + dense_ins + [base],
        flops,
        moved,
        36 * MIB,
        scratch=scratch,
        far=(3, 4, 5, 6, 7),
        far_outs=(0,),
        alias={7: 0},
    )

    hidden_kept, totals = call(
        kept_kernel,
        [picks, row_sums],
        [returned, picked, skip_wide, *first_picks, *more_picks],
        8 * rows * tok_rows,
        10 * rows * tok_rows,
        16 * MIB,
    )

    parts = [totals]
    for shift in range(1, chan_devices):
        ring = [(i, (i + shift) % chan_devices) for i in range(chan_devices)]
        parts.append(lax.ppermute(totals, "chan", ring))

    hidden, held = call(
        hidden_kernel,
        [pltpu.HBM(whole, bf16), pltpu.VMEM(whole, bf16)],
        [in_hbm(base), hidden_kept, onehot],
        2 * tok_rows * slab * rows,
        2 * dense,
        16 * MIB,
        scratch=[
            pltpu.VMEM(whole, bf16),
            pltpu.SemaphoreType.DMA((1, tok_rows // tile)),
            pltpu.SemaphoreType.DMA((tok_rows // tile,)),
        ],
        far=(0,),
        far_outs=(0,),
    )
    (normed,) = call(
        functools.partial(norm_kernel, float(slab * chan_devices), len(parts)),
        [pltpu.HBM(whole, bf16)],
        parts + [in_vmem(held), gain_row],
        4 * tok_rows * slab,
        2 * dense,
        16 * MIB,
        scratch=[
            pltpu.VMEM(whole, bf16),
            pltpu.VMEM((LANES, LANES), f32),
            pltpu.SemaphoreType.DMA((blocks,)),
        ],
        far_outs=(0,),
    )
    return (hidden, normed)


def solution(mesh):
    positions = P(("seqo", "seqi"), "chan")
    in_specs = (
        positions,
        positions,
        positions,
        positions,
        P("chan", ("seqo", "seqi"), None, None),
        P("chan", None),
        P("chan", None),
        P("chan"),
        P("chan"),
    )
    return jax.shard_map(
        local, mesh=mesh, in_specs=in_specs, out_specs=(positions, positions), check_vma=False
    )
```

```python
import functools

import jax
import jax.numpy as jnp
import numpy as np
from jax import lax
from jax.experimental import pallas as pl
from jax.experimental.pallas import tpu as pltpu
from jax.sharding import PartitionSpec as P

LANES = 128
TILE = 256
CHUNK = 16
GROUP = 3
AHEAD = 3
EARLY = 8
MIB = 1 << 20
norm_eps = 1e-06
f32 = jnp.float32
bf16 = jnp.bfloat16


def split_np(table):
    high = table.astype(jnp.bfloat16)
    low = (table - high.astype(np.float64)).astype(jnp.bfloat16)
    return high, low


def dft_tables(length):
    inner = LANES
    outer = length // inner
    a = np.arange(outer)
    b = np.arange(inner)
    quarter = np.arange(outer) + 0.25
    outer_angle = 2 * np.pi / outer * np.mod(quarter[:, None] * a[None, :], outer)
    turn_angle = 2 * np.pi / length * (quarter[:, None] * b[None, :])
    inner_angle = 2 * np.pi / inner * np.mod(b[:, None] * b[None, :], inner)
    outer_fwd = np.concatenate([np.cos(outer_angle), -np.sin(outer_angle)], axis=0)
    c, s = np.cos(inner_angle), np.sin(inner_angle)
    inner_fwd = np.concatenate(
        [np.concatenate([c, -s], axis=1), np.concatenate([s, c], axis=1)], axis=0
    )
    inner_back = np.concatenate(
        [np.concatenate([c, s], axis=1), np.concatenate([-s, c], axis=1)], axis=0
    )
    outer_back = np.concatenate([np.cos(outer_angle).T, -np.sin(outer_angle).T], axis=1) / length
    turn = np.concatenate([np.cos(turn_angle), np.sin(turn_angle)], axis=1).astype(np.float32)
    outer_fwd = np.concatenate(split_np(outer_fwd), axis=0)
    inner = np.concatenate(split_np(inner_fwd) + split_np(inner_back), axis=0)
    outer_back = np.concatenate(split_np(outer_back), axis=1)
    return outer_fwd, turn, inner, outer_back


def split(value):
    high = value.astype(bf16)
    low = (value - high.astype(f32)).astype(bf16)
    return high, low


def dot(x, y):
    return jnp.dot(x, y, preferred_element_type=f32)


def dot_rows(x, y):
    return lax.dot_general(x, y, (((0,), (0,)), ((), ())), preferred_element_type=f32)


def times_table(value, table):
    high, low = split(value)
    depth = value.shape[1]
    stacked = jnp.concatenate([table, table[:depth]], axis=0)
    return dot(jnp.concatenate([high, high, low], axis=1), stacked)


def table_times(table, value):
    high, low = split(value)
    depth = value.shape[0]
    stacked = jnp.concatenate([table, table[:, :depth]], axis=1)
    return dot(stacked, jnp.concatenate([high, high, low], axis=0))


def to_spectrum(blocks, slots, outer_fwd, turn, inner_fwd):
    outer = blocks.shape[0]
    first = dot(outer_fwd(0), blocks)
    first = first + dot(outer_fwd(1), blocks)
    turn, inner_fwd = turn(), inner_fwd()
    cos, sin = turn[:, :LANES], turn[:, LANES:]
    turned = []
    for s in range(slots):
        re = first[:outer, s * LANES : (s + 1) * LANES]
        im = first[outer:, s * LANES : (s + 1) * LANES]
        turned.append(jnp.concatenate([re * cos + im * sin, im * cos - re * sin], axis=1))
    return grouped(turned, inner_fwd)


def grouped(values, table):
    result = []
    for s in range(0, len(values), GROUP):
        part = values[s : s + GROUP]
        size = part[0].shape[0]
        product = times_table(jnp.concatenate(part, axis=0), table)
        result += [product[n * size : (n + 1) * size] for n in range(len(part))]
    return result


def filter_spectra(filters, outer_fwd, turn, inner):
    slots, length = filters.shape
    outer = length // LANES
    wide = filters[...].astype(f32)
    blocks = [wide[s].reshape(outer, LANES) for s in range(slots)]
    blocks = jnp.concatenate(blocks, axis=1).astype(bf16)
    return to_spectrum(
        blocks,
        slots,
        lambda n: outer_fwd[2 * outer * n : 2 * outer * (n + 1), :],
        lambda: turn[...],
        lambda: inner[: 4 * LANES, :],
    )


def convolve_kernel(
    outer_devices, inner_devices, signals, spectra, outer_fwd_far, turn_far, inner_far, outer_back_far, out, *scratch
):
    sources = (outer_fwd_far, turn_far, inner_far, outer_back_far)
    outer_fwd, turn_ref, inner, outer_back, result, sems = scratch
    slots, outer = spectra.shape[:2]
    halves = [pl.ds(2 * outer * n, 2 * outer) for n in range(2)]
    copies = [
        pltpu.make_async_copy(outer_fwd_far.at[half, :], outer_fwd.at[half, :], sems.at[n])
        for n, half in enumerate(halves)
    ] + [
        pltpu.make_async_copy(source, scratch[n], sems.at[n + 1])
        for n, source in enumerate(sources)
        if n > 0
    ]
    for copy in copies:
        copy.start()

    def outer_now(n):
        copies[n].wait()
        return outer_fwd[halves[n], :]

    def turn_now():
        copies[2].wait()
        return turn_ref[...]

    def inner_now():
        copies[3].wait()
        return inner[: 4 * LANES, :]

    places = [
        place_of(n, outer_devices, inner_devices) for n in range(outer_devices * inner_devices)
    ]
    piece = signals.shape[1]
    blocks = jnp.concatenate([signals[place] for place in places], axis=0)
    parts = to_spectrum(blocks, slots, outer_now, turn_now, inner_now)
    turn = turn_ref[...]
    cos, sin = turn[:, :LANES], turn[:, LANES:]
    joint = []
    for s in range(slots):
        sig_re, sig_im = parts[s][:, :LANES], parts[s][:, LANES:]
        ker_re, ker_im = spectra[s, :, :LANES], spectra[s, :, LANES:]
        joint.append(
            jnp.concatenate(
                [sig_re * ker_re - sig_im * ker_im, sig_re * ker_im + sig_im * ker_re], axis=1
            )
        )
    turned = []
    for back in grouped(joint, inner[4 * LANES :, :]):
        re, im = back[:, :LANES], back[:, LANES:]
        turned.append(jnp.concatenate([re * cos - im * sin, im * cos + re * sin], axis=0))
    copies[4].wait()
    sends = []
    for s in range(0, slots, 2):
        pair = turned[s : s + 2]
        causal = table_times(outer_back[...], jnp.concatenate(pair, axis=1)).astype(bf16)
        lanes = pl.ds(s * LANES, len(pair) * LANES)
        for n, place in enumerate(places):
            result[place, :, lanes] = causal[n * piece : (n + 1) * piece]
        sends.append(
            pltpu.make_async_copy(
                result.at[:, :, lanes], out.at[:, :, lanes], sems.at[len(copies) + len(sends)]
            )
        )
        sends[-1].start()
    for send in sends:
        send.wait()


def place_of(owner, outer_devices, inner_devices):
    return owner % inner_devices * outer_devices + owner // inner_devices


def iota(shape, axis):
    return lax.broadcasted_iota(jnp.int32, shape, axis)


def to_column(row):
    size = row.shape[1]
    same = iota((size, size), 0) == iota((size, size), 1)
    return jnp.sum(jnp.where(same, row, 0), axis=1, keepdims=True)


def channel_of_row(index_row, owners_row, outer_devices, inner_devices, rows):
    slots = owners_row.shape[1]
    owners_col = to_column(owners_row)
    index_col = to_column(index_row)
    earlier = (owners_col == owners_row) & (iota((slots, slots), 1) < iota((slots, slots), 0))
    rank_col = jnp.sum(earlier.astype(jnp.int32), axis=1, keepdims=True)
    outer_col = jnp.zeros_like(owners_col)
    for n in range(1, outer_devices):
        outer_col = outer_col + (owners_col >= n * inner_devices).astype(jnp.int32)
    place_col = (owners_col - outer_col * inner_devices) * outer_devices + outer_col
    owner_count = outer_devices * inner_devices
    target_col = jnp.where(owners_col >= 0, rank_col * owner_count + place_col, -1)
    hit = target_col == iota((slots, rows), 1)
    return jnp.sum(jnp.where(hit, index_col + 1, 0), axis=0, keepdims=True) - 1


def pick_rows(onehot, tile):
    picked = lax.dot_general(
        onehot, tile, (((1,), (1,)), ((), ())), preferred_element_type=f32
    )
    return [picked[:, i : i + LANES] for i in range(0, tile.shape[0], LANES)]


def fetch(sources, stages, sems, tile, first=0, ahead=3, begin=True):
    count = stages[0].shape[0] // tile

    def copies(i):
        at = pl.multiple_of(i * tile, tile)
        return [
            pltpu.make_async_copy(
                source.at[pl.ds(first + at, tile), :], stage.at[pl.ds(at, tile), :], sems.at[n, i]
            )
            for n, (source, stage) in enumerate(zip(sources, stages))
        ]

    def start(i):
        for copy in copies(i):
            copy.start()

    ahead = min(ahead, count)
    if begin:
        for i in range(ahead):
            start(i)

    def wait(i):
        for copy in copies(i):
            copy.wait()

        @pl.when(i + ahead < count)
        def _():
            start(i + ahead)

        return pl.multiple_of(i * tile, tile)

    return start, wait, ahead


def build_onehot(onehot, row):
    hit = iota(onehot.shape, 1) == to_column(row)[: onehot.shape[0]]
    onehot[...] = hit.astype(f32).astype(bf16)
    return hit


def pick_kernel(outer_devices, inner_devices, slots, index, owners, gate, value, *refs):
    payload, picked, channels, gated_head = refs[:4]
    acc, gate_stage, value_stage, onehot, lists, list_sems, sems = refs[4:]
    tile = gate_stage.shape[0] // sems.shape[1]
    list_copies = [
        pltpu.make_async_copy(source, lists.at[n], list_sems.at[n])
        for n, source in enumerate((index, owners))
    ]
    for copy in list_copies:
        copy.start()
    count = sems.shape[1]
    _, wait, _ = fetch((gate, value), (gate_stage, value_stage), sems, tile, 0, 4)
    for copy in list_copies:
        copy.wait()
    owner_count = outer_devices * inner_devices
    row = channel_of_row(lists[0], lists[1], outer_devices, inner_devices, channels.shape[1])
    channels[...] = jnp.broadcast_to(row, channels.shape)
    build_onehot(onehot, row)

    def step(i, in_head):
        at = pl.ds(wait(i), tile)
        gated = gate_stage[at, :] * value_stage[at, :]
        if in_head:
            gated_head[at, :] = gated
        for n, block in enumerate(pick_rows(onehot[...], gated)):
            acc[i * (tile // LANES) + n] = block
            picked[i * (tile // LANES) + n] = block.astype(bf16)
        return 0

    head_tiles = gated_head.shape[0] // tile
    lax.fori_loop(0, head_tiles, lambda i, _: step(i, True), 0)
    lax.fori_loop(head_tiles, count, lambda i, _: step(i, False), 0)
    for s in range(slots):
        part = jnp.swapaxes(acc[:, s * owner_count : (s + 1) * owner_count, :], 0, 1)
        payload[:, :, s * LANES : (s + 1) * LANES] = part.astype(bf16)


def filter_kernel(filters, outer_fwd, turn, inner, spectra):
    for s, part in enumerate(filter_spectra(filters, outer_fwd, turn, inner)):
        spectra[s] = part


def first_kernel(channels, gated_head, skip, *refs):
    onehot, others, skip_wide, *outs = refs[4:11]

    def beside():
        hit = build_onehot(onehot, channels[0:1, :])
        kept = jnp.max(hit.astype(f32), axis=0, keepdims=True)
        others[...] = jnp.broadcast_to(1.0 - kept, others.shape)
        skip_col = jnp.sum(jnp.where(hit, skip[...], 0.0), axis=1, keepdims=True)
        skip_wide[...] = jnp.broadcast_to(skip_col, skip_wide.shape)

    base_pass(0, gated_head, onehot, others, skip, refs[:4], outs, refs[11:], beside)


def second_kernel(first, onehot, others, skip, *refs):
    base_pass(first, None, onehot, others, skip, refs[:4], refs[5:9], refs[9:], None)


def base_pass(first, head, onehot, others, skip, dense, outs, scratch, beside):
    base, sums, picked_gate, picked_res = outs
    gate_stage, value_stage, out_stage, res_stage, base_stage = scratch[:5]
    partial, base_sems, gate_sems, sems = scratch[5:]
    slab = out_stage.shape[1]
    tile = partial.shape[0]
    head_rows = 0 if head is None else head.shape[0]
    head_tiles = head_rows // tile
    count = sems.shape[1]
    late = head_tiles > AHEAD
    _, wait, _ = fetch(dense[2:], (out_stage, res_stage), sems, tile, first, AHEAD)
    start_gate, wait_gate, early = fetch(
        dense[:2], (gate_stage, value_stage), gate_sems, tile, first + head_rows, AHEAD, not late
    )
    if beside is not None:
        beside()

    def copy(i):
        at = pl.multiple_of(i * tile, tile)
        return pltpu.make_async_copy(
            base_stage.at[pl.ds(at, tile), :], base.at[pl.ds(first + at, tile), :], base_sems.at[i]
        )

    def step(i, in_head):
        start = wait(i)
        if in_head and late:

            @pl.when((i > 0) & (i <= early))
            def _():
                start_gate(i - 1)

        gate_start = start if in_head else wait_gate(i - head_tiles)
        chunks = range(0, tile, CHUNK)
        totals = [jnp.zeros((CHUNK, LANES), f32) for _ in chunks]
        for j in range(0, slab, LANES):
            lanes = slice(j, j + LANES)
            skips = skip[:, lanes]
            mask = others[0:1, lanes].astype(bf16)
            for n, c in enumerate(chunks):
                at = pl.ds(start + c, CHUNK)
                gate_at = pl.ds(gate_start + c, CHUNK)
                if in_head:
                    gated = head[gate_at, lanes]
                else:
                    gated = gate_stage[gate_at, lanes] * value_stage[gate_at, lanes]
                mixed = out_stage[at, lanes].astype(f32) * (skips * gated.astype(f32))
                hidden = (res_stage[at, lanes].astype(f32) + mixed).astype(bf16) * mask
                base_stage[at, lanes] = hidden
                hidden = hidden.astype(f32)
                totals[n] = totals[n] + hidden * hidden
        copy(i).start()
        for n, c in enumerate(chunks):
            partial[c : c + CHUNK, :] = totals[n]
        total = jnp.sum(partial[...].T, axis=0, keepdims=True)
        at = pl.ds(start, tile)
        both = jnp.concatenate([out_stage[at, :], res_stage[at, :]], axis=0)
        both = pick_rows(onehot[...], both)
        picks_gate, picks_res = both[: tile // LANES], both[tile // LANES :]
        for n in range(tile // LANES):
            block = i * (tile // LANES) + n
            sums[block] = total[:, n * LANES : (n + 1) * LANES]
            picked_gate[block] = picks_gate[n].astype(bf16)
            picked_res[block] = picks_res[n].astype(bf16)
        return 0

    if head_tiles:
        lax.fori_loop(0, head_tiles, lambda i, _: step(i, True), 0)
    lax.fori_loop(head_tiles, count, lambda i, _: step(i, False), 0)
    lax.fori_loop(0, count, lambda i, _: (copy(i).wait(), 0)[1], 0)


def kept_kernel(conv, picked, skip_wide, *refs):
    hidden, totals = refs[-2:]
    owner_count, blocks = conv.shape[:2]
    first = 0
    for n in range(0, len(refs) - 2, 3):
        sums, picked_gate, picked_res = refs[n : n + 3]
        size = sums.shape[0]
        at_h = slice(first, first + size)
        total = jnp.zeros((size, LANES), f32)
        for s in range(conv.shape[2] // LANES):
            at = slice(s * owner_count, (s + 1) * owner_count)
            lanes = slice(s * LANES, (s + 1) * LANES)
            wide = jnp.swapaxes(conv[:, at_h, lanes].astype(f32), 0, 1)
            wide = wide + skip_wide[at, :] * picked[at_h, at, :].astype(f32)
            value = picked_res[:, at, :].astype(f32) + picked_gate[:, at, :].astype(f32) * wide
            value = value.astype(bf16)
            hidden[at_h, at, :] = value
            value = value.astype(f32)
            total = total + jnp.sum(value * value, axis=1)
        for i in range(size):
            totals[first + i] = total[i : i + 1, :] + sums[i]
        first = first + size


def hidden_kernel(base, hidden_kept, onehot, hidden, held, base_stage, base_sems, sems):
    slab = held.shape[1]
    wide = min(slab, 2 * LANES)
    count = sems.shape[0]
    tile = held.shape[0] // count
    _, wait, _ = fetch((base,), (base_stage,), base_sems, tile, 0, 4)

    def copy(i):
        rows = pl.ds(pl.multiple_of(i * tile, tile), tile)
        return pltpu.make_async_copy(held.at[rows, :], hidden.at[rows, :], sems.at[i])

    def step(i, _):
        blocks = range(tile // LANES)
        kept = [hidden_kept[i * (tile // LANES) + n].astype(f32).T.astype(bf16) for n in blocks]
        kept = jnp.concatenate(kept, axis=0)
        rows = pl.ds(wait(i), tile)
        for j in range(0, slab, wide):
            lanes = slice(j, j + wide)
            placed = dot(kept, onehot[:, lanes]).astype(bf16)
            held[rows, lanes] = base_stage[rows, lanes] + placed
        copy(i).start()
        return 0

    lax.fori_loop(0, count, step, 0)
    lax.fori_loop(0, count, lambda i, _: (copy(i).wait(), 0)[1], 0)


def norm_kernel(width, count, *refs):
    parts = refs[:count]
    held, gain, normed, stage, turned, sems = refs[count:]
    slab = held.shape[1]

    def copy(i):
        rows = pl.ds(pl.multiple_of(i * LANES, LANES), LANES)
        return pltpu.make_async_copy(stage.at[rows, :], normed.at[rows, :], sems.at[i])

    def step(i, _):
        total = parts[0][i]
        for part in parts[1:]:
            total = total + part[i]
        scale = lax.rsqrt(total / width + norm_eps)
        turned[...] = jnp.broadcast_to(scale, (LANES, LANES)).T
        first = pl.multiple_of(i * LANES, LANES)
        for c in range(0, LANES, CHUNK):
            at = pl.ds(first + c, CHUNK)
            scales = turned[c : c + CHUNK, :]
            for j in range(0, slab, LANES):
                lanes = slice(j, j + LANES)
                value = held[at, lanes].astype(f32) * scales * gain[:, lanes]
                stage[at, lanes] = value.astype(bf16)
        copy(i).start()
        return 0

    lax.fori_loop(0, sems.shape[0], step, 0)
    lax.fori_loop(0, sems.shape[0], lambda i, _: (copy(i).wait(), 0)[1], 0)


def in_hbm(x):
    return pltpu.with_memory_space_constraint(x, pltpu.HBM)


def in_vmem(x):
    return pltpu.with_memory_space_constraint(x, pltpu.VMEM)


def call(kernel, outs, ins, flops, moved, limit, scratch=(), far=(), far_outs=(), alias=None):
    near = pl.BlockSpec(memory_space=pltpu.VMEM)
    away = pl.BlockSpec(memory_space=pl.ANY)
    return pl.pallas_call(
        kernel,
        out_shape=outs,
        in_specs=[away if n in far else near for n in range(len(ins))],
        out_specs=[away if n in far_outs else near for n in range(len(outs))],
        scratch_shapes=list(scratch),
        input_output_aliases=alias or {},
        compiler_params=pltpu.CompilerParams(vmem_limit_bytes=limit),
        cost_estimate=pl.CostEstimate(flops=flops, bytes_accessed=moved, transcendentals=0),
    )(*ins)


def local(
    gate_in, value_in, out_gate, residual, filters, kept_index, kept_owner, skip_bias, norm_gain
):
    tok_rows, slab = gate_in.shape
    slots, length = filters.shape[2:]
    chan_devices = lax.axis_size("chan")
    outer_devices, inner_devices = lax.axis_size("seqo"), lax.axis_size("seqi")
    owner_count = outer_devices * inner_devices
    rows = slots * owner_count
    lanes_rows = -(-rows // LANES) * LANES
    blocks = tok_rows // LANES
    outer = length // LANES
    tile = TILE if tok_rows % TILE == 0 else LANES
    dense = tok_rows * slab * 2
    sds = jax.ShapeDtypeStruct
    tables = [in_hbm(jnp.asarray(x)) for x in dft_tables(length)]
    outer_fwd, turn, inner, outer_back = tables
    skip_row = skip_bias[None, :]
    gain_row = norm_gain[None, :]
    gate_in, value_in, out_gate, residual = map(in_hbm, (gate_in, value_in, out_gate, residual))
    picks = sds((blocks, rows, LANES), bf16)
    row_sums = sds((blocks, 1, LANES), f32)
    buffer = (owner_count, blocks, slots * LANES)
    whole = (tok_rows, slab)
    head_rows = tok_rows // 4 // tile * tile

    payload, picked, channels, gated_head = call(
        functools.partial(pick_kernel, outer_devices, inner_devices, slots),
        [
            sds(buffer, bf16),
            picks,
            sds((8, lanes_rows), jnp.int32),
            pltpu.VMEM((head_rows, slab), bf16),
        ],
        [in_hbm(kept_index), in_hbm(kept_owner), gate_in, value_in],
        2 * tok_rows * slab * rows,
        2 * dense,
        24 * MIB,
        scratch=[
            pltpu.VMEM((blocks, rows, LANES), f32),
            pltpu.VMEM(whole, bf16),
            pltpu.VMEM(whole, bf16),
            pltpu.VMEM((rows, slab), bf16),
            pltpu.VMEM((2,) + kept_index.shape, jnp.int32),
            pltpu.SemaphoreType.DMA((2,)),
            pltpu.SemaphoreType.DMA((2, tok_rows // tile)),
        ],
        far=(0, 1, 2, 3),
    )

    incoming = lax.all_to_all(payload, ("seqi", "seqo"), split_axis=0, concat_axis=0, tiled=True)

    dense_ins = [gate_in, value_in, out_gate, residual]

    def base_parts(count, head):
        part = count * LANES
        outs = [
            pltpu.HBM(whole, bf16),
            sds((count, 1, LANES), f32),
            sds((count, rows, LANES), bf16),
            sds((count, rows, LANES), bf16),
        ]
        scratch = [
            pltpu.VMEM((part - head, slab), bf16),
            pltpu.VMEM((part - head, slab), bf16),
            pltpu.VMEM((part, slab), bf16),
            pltpu.VMEM((part, slab), bf16),
            pltpu.VMEM((part, slab), bf16),
            pltpu.VMEM((LANES, LANES), f32),
            pltpu.SemaphoreType.DMA((count,)),
            pltpu.SemaphoreType.DMA((2, (part - head) // LANES)),
            pltpu.SemaphoreType.DMA((2, count)),
        ]
        return outs, scratch, 4 * part * slab * rows, 10 * part * slab

    early = max(head_rows // LANES + 1, blocks * EARLY // 16)
    outs, scratch, flops, moved = base_parts(early, head_rows)
    onehot, others, skip_wide, base, *first_picks = call(
        first_kernel,
        [sds((rows, slab), bf16), sds((8, slab), f32), sds((rows, LANES), f32)] + outs,
        [channels, in_vmem(gated_head), skip_row] + dense_ins,
        flops,
        moved,
        36 * MIB,
        scratch=scratch,
        far=(3, 4, 5, 6),
        far_outs=(3,),
    )
    (spectra,) = call(
        filter_kernel,
        [pltpu.VMEM((slots, outer, 2 * LANES), f32)],
        [filters[0, 0]] + [jnp.asarray(x) for x in dft_tables(length)[:3]],
        2 * slots * length * 2 * (2 * outer + 6 * LANES),
        4 * MIB,
        16 * MIB,
    )
    spectra, base = lax.optimization_barrier((spectra, base))

    conv_ins = [incoming, in_vmem(spectra), outer_fwd, turn, inner, outer_back]
    (convolved,) = call(
        functools.partial(convolve_kernel, outer_devices, inner_devices),
        [pltpu.HBM(buffer, bf16)],
        conv_ins,
        2 * slots * length * 2 * (5 * outer + 12 * LANES),
        8 * MIB,
        20 * MIB,
        scratch=[pltpu.VMEM(x.shape, x.dtype) for x in conv_ins[2:]]
        + [pltpu.VMEM(buffer, bf16), pltpu.SemaphoreType.DMA((len(conv_ins) + slots,))],
        far=tuple(range(2, len(conv_ins))),
        far_outs=(0,),
    )
    convolved, onehot = lax.optimization_barrier((convolved, onehot))

    returned = lax.all_to_all(convolved, ("seqi", "seqo"), split_axis=0, concat_axis=0, tiled=True)

    outs, scratch, flops, moved = base_parts(blocks - early, 0)
    base, *more_picks = call(
        functools.partial(second_kernel, early * LANES),
        outs,
        [onehot, others, skip_row] + dense_ins + [base],
        flops,
        moved,
        36 * MIB,
        scratch=scratch,
        far=(3, 4, 5, 6, 7),
        far_outs=(0,),
        alias={7: 0},
    )

    hidden_kept, totals = call(
        kept_kernel,
        [picks, row_sums],
        [returned, picked, skip_wide, *first_picks, *more_picks],
        8 * rows * tok_rows,
        10 * rows * tok_rows,
        16 * MIB,
    )

    parts = [totals]
    for shift in range(1, chan_devices):
        ring = [(i, (i + shift) % chan_devices) for i in range(chan_devices)]
        parts.append(lax.ppermute(totals, "chan", ring))

    hidden, held = call(
        hidden_kernel,
        [pltpu.HBM(whole, bf16), pltpu.VMEM(whole, bf16)],
        [in_hbm(base), hidden_kept, onehot],
        2 * tok_rows * slab * rows,
        2 * dense,
        16 * MIB,
        scratch=[
            pltpu.VMEM(whole, bf16),
            pltpu.SemaphoreType.DMA((1, tok_rows // tile)),
            pltpu.SemaphoreType.DMA((tok_rows // tile,)),
        ],
        far=(0,),
        far_outs=(0,),
    )
    (normed,) = call(
        functools.partial(norm_kernel, float(slab * chan_devices), len(parts)),
        [pltpu.HBM(whole, bf16)],
        parts + [in_vmem(held), gain_row],
        4 * tok_rows * slab,
        2 * dense,
        16 * MIB,
        scratch=[
            pltpu.VMEM(whole, bf16),
            pltpu.VMEM((LANES, LANES), f32),
            pltpu.SemaphoreType.DMA((blocks,)),
        ],
        far_outs=(0,),
    )
    return (hidden, normed)


def solution(mesh):
    positions = P(("seqo", "seqi"), "chan")
    in_specs = (
        positions,
        positions,
        positions,
        positions,
        P("chan", ("seqo", "seqi"), None, None),
        P("chan", None),
        P("chan", None),
        P("chan"),
        P("chan"),
    )
    return jax.shard_map(
        local, mesh=mesh, in_specs=in_specs, out_specs=(positions, positions), check_vma=False
    )
```

```python
import functools

import jax
import jax.numpy as jnp
import numpy as np
from jax import lax
from jax.experimental import pallas as pl
from jax.experimental.pallas import tpu as pltpu
from jax.sharding import PartitionSpec as P

LANES = 128
TILE = 256
CHUNK = 16
GROUP = 3
AHEAD = 3
EARLY = 8
MIB = 1 << 20
norm_eps = 1e-06
f32 = jnp.float32
bf16 = jnp.bfloat16


def split_np(table):
    high = table.astype(jnp.bfloat16)
    low = (table - high.astype(np.float64)).astype(jnp.bfloat16)
    return high, low


def dft_tables(length):
    inner = LANES
    outer = length // inner
    a = np.arange(outer)
    b = np.arange(inner)
    quarter = np.arange(outer) + 0.25
    outer_angle = 2 * np.pi / outer * np.mod(quarter[:, None] * a[None, :], outer)
    turn_angle = 2 * np.pi / length * (quarter[:, None] * b[None, :])
    inner_angle = 2 * np.pi / inner * np.mod(b[:, None] * b[None, :], inner)
    outer_fwd = np.concatenate([np.cos(outer_angle), -np.sin(outer_angle)], axis=0)
    c, s = np.cos(inner_angle), np.sin(inner_angle)
    inner_fwd = np.concatenate(
        [np.concatenate([c, -s], axis=1), np.concatenate([s, c], axis=1)], axis=0
    )
    inner_back = np.concatenate(
        [np.concatenate([c, s], axis=1), np.concatenate([-s, c], axis=1)], axis=0
    )
    outer_back = np.concatenate([np.cos(outer_angle).T, -np.sin(outer_angle).T], axis=1) / length
    turn = np.concatenate([np.cos(turn_angle), np.sin(turn_angle)], axis=1).astype(np.float32)
    outer_fwd = np.concatenate(split_np(outer_fwd), axis=0)
    inner = np.concatenate(split_np(inner_fwd) + split_np(inner_back), axis=0)
    outer_back = np.concatenate(split_np(outer_back), axis=1)
    return outer_fwd, turn, inner, outer_back


def split(value):
    high = value.astype(bf16)
    low = (value - high.astype(f32)).astype(bf16)
    return high, low


def dot(x, y):
    return jnp.dot(x, y, preferred_element_type=f32)


def dot_rows(x, y):
    return lax.dot_general(x, y, (((0,), (0,)), ((), ())), preferred_element_type=f32)


def times_table(value, table):
    high, low = split(value)
    depth = value.shape[1]
    stacked = jnp.concatenate([table, table[:depth]], axis=0)
    return dot(jnp.concatenate([high, high, low], axis=1), stacked)


def table_times(table, value):
    high, low = split(value)
    depth = value.shape[0]
    stacked = jnp.concatenate([table, table[:, :depth]], axis=1)
    return dot(stacked, jnp.concatenate([high, high, low], axis=0))


def to_spectrum(blocks, slots, outer_fwd, turn, inner_fwd):
    outer = blocks.shape[0]
    first = dot(outer_fwd(0), blocks)
    first = first + dot(outer_fwd(1), blocks)
    turn, inner_fwd = turn(), inner_fwd()
    cos, sin = turn[:, :LANES], turn[:, LANES:]
    turned = []
    for s in range(slots):
        re = first[:outer, s * LANES : (s + 1) * LANES]
        im = first[outer:, s * LANES : (s + 1) * LANES]
        turned.append(jnp.concatenate([re * cos + im * sin, im * cos - re * sin], axis=1))
    return grouped(turned, inner_fwd)


def grouped(values, table):
    result = []
    for s in range(0, len(values), GROUP):
        part = values[s : s + GROUP]
        size = part[0].shape[0]
        product = times_table(jnp.concatenate(part, axis=0), table)
        result += [product[n * size : (n + 1) * size] for n in range(len(part))]
    return result


def filter_spectra(filters, outer_fwd, turn, inner):
    slots, length = filters.shape
    outer = length // LANES
    wide = filters[...].astype(f32)
    blocks = [wide[s].reshape(outer, LANES) for s in range(slots)]
    blocks = jnp.concatenate(blocks, axis=1).astype(bf16)
    return to_spectrum(
        blocks,
        slots,
        lambda n: outer_fwd[2 * outer * n : 2 * outer * (n + 1), :],
        lambda: turn[...],
        lambda: inner[: 4 * LANES, :],
    )


def convolve_kernel(
    signals, spectra, outer_fwd_far, turn_far, inner_far, outer_back_far, out, *scratch
):
    sources = (outer_fwd_far, turn_far, inner_far, outer_back_far)
    outer_fwd, turn_ref, inner, outer_back, result, sems = scratch
    slots, outer = spectra.shape[:2]
    halves = [pl.ds(2 * outer * n, 2 * outer) for n in range(2)]
    copies = [
        pltpu.make_async_copy(outer_fwd_far.at[half, :], outer_fwd.at[half, :], sems.at[n])
        for n, half in enumerate(halves)
    ] + [
        pltpu.make_async_copy(source, scratch[n], sems.at[n + 1])
        for n, source in enumerate(sources)
        if n > 0
    ]
    for copy in copies:
        copy.start()

    def outer_now(n):
        copies[n].wait()
        return outer_fwd[halves[n], :]

    def turn_now():
        copies[2].wait()
        return turn_ref[...]

    def inner_now():
        copies[3].wait()
        return inner[: 4 * LANES, :]

    blocks = signals[...].reshape(outer, slots * LANES)
    parts = to_spectrum(blocks, slots, outer_now, turn_now, inner_now)
    turn = turn_ref[...]
    cos, sin = turn[:, :LANES], turn[:, LANES:]
    joint = []
    for s in range(slots):
        sig_re, sig_im = parts[s][:, :LANES], parts[s][:, LANES:]
        ker_re, ker_im = spectra[s, :, :LANES], spectra[s, :, LANES:]
        joint.append(
            jnp.concatenate(
                [sig_re * ker_re - sig_im * ker_im, sig_re * ker_im + sig_im * ker_re], axis=1
            )
        )
    turned = []
    for back in grouped(joint, inner[4 * LANES :, :]):
        re, im = back[:, :LANES], back[:, LANES:]
        turned.append(jnp.concatenate([re * cos - im * sin, im * cos + re * sin], axis=0))
    copies[4].wait()
    sends = []
    for s in range(0, slots, 2):
        pair = turned[s : s + 2]
        causal = table_times(outer_back[...], jnp.concatenate(pair, axis=1)).astype(bf16)
        lanes = pl.ds(s * LANES, len(pair) * LANES)
        result[:, :, lanes] = causal.reshape(out.shape[:2] + (len(pair) * LANES,))
        sends.append(
            pltpu.make_async_copy(
                result.at[:, :, lanes], out.at[:, :, lanes], sems.at[len(copies) + len(sends)]
            )
        )
        sends[-1].start()
    for send in sends:
        send.wait()


def iota(shape, axis):
    return lax.broadcasted_iota(jnp.int32, shape, axis)


def to_column(row):
    size = row.shape[1]
    same = iota((size, size), 0) == iota((size, size), 1)
    return jnp.sum(jnp.where(same, row, 0), axis=1, keepdims=True)


def channel_of_row(index_row, owners_row, owner_count, rows):
    slots = owners_row.shape[1]
    owners_col = to_column(owners_row)
    index_col = to_column(index_row)
    earlier = (owners_col == owners_row) & (iota((slots, slots), 1) < iota((slots, slots), 0))
    rank_col = jnp.sum(earlier.astype(jnp.int32), axis=1, keepdims=True)
    target_col = jnp.where(owners_col >= 0, rank_col * owner_count + owners_col, -1)
    hit = target_col == iota((slots, rows), 1)
    return jnp.sum(jnp.where(hit, index_col + 1, 0), axis=0, keepdims=True) - 1


def pick_rows(onehot, tile):
    picked = lax.dot_general(
        onehot, tile, (((1,), (1,)), ((), ())), preferred_element_type=f32
    )
    return [picked[:, i : i + LANES] for i in range(0, tile.shape[0], LANES)]


def fetch(sources, stages, sems, tile, first=0, ahead=3, begin=True):
    count = stages[0].shape[0] // tile

    def copies(i):
        at = pl.multiple_of(i * tile, tile)
        return [
            pltpu.make_async_copy(
                source.at[pl.ds(first + at, tile), :], stage.at[pl.ds(at, tile), :], sems.at[n, i]
            )
            for n, (source, stage) in enumerate(zip(sources, stages))
        ]

    def start(i):
        for copy in copies(i):
            copy.start()

    ahead = min(ahead, count)
    if begin:
        for i in range(ahead):
            start(i)

    def wait(i):
        for copy in copies(i):
            copy.wait()

        @pl.when(i + ahead < count)
        def _():
            start(i + ahead)

        return pl.multiple_of(i * tile, tile)

    return start, wait, ahead


def build_onehot(onehot, row):
    hit = iota(onehot.shape, 1) == to_column(row)[: onehot.shape[0]]
    onehot[...] = hit.astype(f32).astype(bf16)
    return hit


def pick_kernel(owner_count, slots, index, owners, gate, value, *refs):
    payload, picked, channels, gated_head = refs[:4]
    acc, gate_stage, value_stage, onehot, payload_stage, lists, list_sems, sems = refs[4:]
    tile = gate_stage.shape[0] // sems.shape[1]
    list_copies = [
        pltpu.make_async_copy(source, lists.at[n], list_sems.at[n])
        for n, source in enumerate((index, owners))
    ]
    for copy in list_copies:
        copy.start()
    count = sems.shape[1]
    _, wait, _ = fetch((gate, value), (gate_stage, value_stage), sems, tile, 0, 4)
    for copy in list_copies:
        copy.wait()
    row = channel_of_row(lists[0], lists[1], owner_count, channels.shape[1])
    channels[...] = jnp.broadcast_to(row, channels.shape)
    build_onehot(onehot, row)

    def step(i, in_head):
        at = pl.ds(wait(i), tile)
        gated = gate_stage[at, :] * value_stage[at, :]
        if in_head:
            gated_head[at, :] = gated
        for n, block in enumerate(pick_rows(onehot[...], gated)):
            acc[i * (tile // LANES) + n] = block
            picked[i * (tile // LANES) + n] = block.astype(bf16)
        return 0

    head_tiles = gated_head.shape[0] // tile
    lax.fori_loop(0, head_tiles, lambda i, _: step(i, True), 0)
    lax.fori_loop(head_tiles, count, lambda i, _: step(i, False), 0)
    sends = []
    for s in range(slots):
        part = jnp.swapaxes(acc[:, s * owner_count : (s + 1) * owner_count, :], 0, 1)
        lanes = pl.ds(s * LANES, LANES)
        payload_stage[:, :, lanes] = part.astype(bf16)
        sends.append(
            pltpu.make_async_copy(
                payload_stage.at[:, :, lanes], payload.at[:, :, lanes], list_sems.at[2 + s]
            )
        )
        sends[-1].start()
    for send in sends:
        send.wait()


def filter_kernel(filters, outer_fwd, turn, inner, spectra):
    for s, part in enumerate(filter_spectra(filters, outer_fwd, turn, inner)):
        spectra[s] = part


def first_kernel(channels, gated_head, skip, *refs):
    onehot, others, skip_wide, *outs = refs[4:11]

    def beside():
        hit = build_onehot(onehot, channels[0:1, :])
        kept = jnp.max(hit.astype(f32), axis=0, keepdims=True)
        others[...] = jnp.broadcast_to(1.0 - kept, others.shape)
        skip_col = jnp.sum(jnp.where(hit, skip[...], 0.0), axis=1, keepdims=True)
        skip_wide[...] = jnp.broadcast_to(skip_col, skip_wide.shape)

    base_pass(0, gated_head, onehot, others, skip, refs[:4], outs, refs[11:], beside)


def second_kernel(first, onehot, others, skip, *refs):
    base_pass(first, None, onehot, others, skip, refs[:4], refs[5:9], refs[9:], None)


def base_pass(first, head, onehot, others, skip, dense, outs, scratch, beside):
    base, sums, picked_gate, picked_res = outs
    gate_stage, value_stage, out_stage, res_stage, base_stage = scratch[:5]
    partial, base_sems, gate_sems, sems = scratch[5:]
    slab = out_stage.shape[1]
    tile = partial.shape[0]
    head_rows = 0 if head is None else head.shape[0]
    head_tiles = head_rows // tile
    count = sems.shape[1]
    late = head_tiles > AHEAD
    _, wait, _ = fetch(dense[2:], (out_stage, res_stage), sems, tile, first, AHEAD)
    start_gate, wait_gate, early = fetch(
        dense[:2], (gate_stage, value_stage), gate_sems, tile, first + head_rows, AHEAD, not late
    )
    if beside is not None:
        beside()

    def copy(i):
        at = pl.multiple_of(i * tile, tile)
        return pltpu.make_async_copy(
            base_stage.at[pl.ds(at, tile), :], base.at[pl.ds(first + at, tile), :], base_sems.at[i]
        )

    def step(i, in_head):
        start = wait(i)
        if in_head and late:

            @pl.when((i > 0) & (i <= early))
            def _():
                start_gate(i - 1)

        gate_start = start if in_head else wait_gate(i - head_tiles)
        chunks = range(0, tile, CHUNK)
        totals = [jnp.zeros((CHUNK, LANES), f32) for _ in chunks]
        for j in range(0, slab, LANES):
            lanes = slice(j, j + LANES)
            skips = skip[:, lanes]
            mask = others[0:1, lanes].astype(bf16)
            for n, c in enumerate(chunks):
                at = pl.ds(start + c, CHUNK)
                gate_at = pl.ds(gate_start + c, CHUNK)
                if in_head:
                    gated = head[gate_at, lanes]
                else:
                    gated = gate_stage[gate_at, lanes] * value_stage[gate_at, lanes]
                mixed = out_stage[at, lanes].astype(f32) * (skips * gated.astype(f32))
                hidden = (res_stage[at, lanes].astype(f32) + mixed).astype(bf16) * mask
                base_stage[at, lanes] = hidden
                hidden = hidden.astype(f32)
                totals[n] = totals[n] + hidden * hidden
        copy(i).start()
        for n, c in enumerate(chunks):
            partial[c : c + CHUNK, :] = totals[n]
        total = jnp.sum(partial[...].T, axis=0, keepdims=True)
        at = pl.ds(start, tile)
        both = jnp.concatenate([out_stage[at, :], res_stage[at, :]], axis=0)
        both = pick_rows(onehot[...], both)
        picks_gate, picks_res = both[: tile // LANES], both[tile // LANES :]
        for n in range(tile // LANES):
            block = i * (tile // LANES) + n
            sums[block] = total[:, n * LANES : (n + 1) * LANES]
            picked_gate[block] = picks_gate[n].astype(bf16)
            picked_res[block] = picks_res[n].astype(bf16)
        return 0

    if head_tiles:
        lax.fori_loop(0, head_tiles, lambda i, _: step(i, True), 0)
    lax.fori_loop(head_tiles, count, lambda i, _: step(i, False), 0)
    lax.fori_loop(0, count, lambda i, _: (copy(i).wait(), 0)[1], 0)


def kept_kernel(conv, picked, skip_wide, *refs):
    hidden, totals = refs[-2:]
    owner_count, blocks = conv.shape[:2]
    first = 0
    for n in range(0, len(refs) - 2, 3):
        sums, picked_gate, picked_res = refs[n : n + 3]
        size = sums.shape[0]
        at_h = slice(first, first + size)
        total = jnp.zeros((size, LANES), f32)
        for s in range(conv.shape[2] // LANES):
            at = slice(s * owner_count, (s + 1) * owner_count)
            lanes = slice(s * LANES, (s + 1) * LANES)
            wide = jnp.swapaxes(conv[:, at_h, lanes].astype(f32), 0, 1)
            wide = wide + skip_wide[at, :] * picked[at_h, at, :].astype(f32)
            value = picked_res[:, at, :].astype(f32) + picked_gate[:, at, :].astype(f32) * wide
            value = value.astype(bf16)
            hidden[at_h, at, :] = value
            value = value.astype(f32)
            total = total + jnp.sum(value * value, axis=1)
        for i in range(size):
            totals[first + i] = total[i : i + 1, :] + sums[i]
        first = first + size


def hidden_kernel(base, hidden_kept, onehot, hidden, held, base_stage, base_sems, sems):
    slab = held.shape[1]
    wide = min(slab, 2 * LANES)
    count = sems.shape[0]
    tile = held.shape[0] // count
    _, wait, _ = fetch((base,), (base_stage,), base_sems, tile, 0, 4)

    def copy(i):
        rows = pl.ds(pl.multiple_of(i * tile, tile), tile)
        return pltpu.make_async_copy(held.at[rows, :], hidden.at[rows, :], sems.at[i])

    def step(i, _):
        blocks = range(tile // LANES)
        kept = [hidden_kept[i * (tile // LANES) + n].astype(f32).T.astype(bf16) for n in blocks]
        kept = jnp.concatenate(kept, axis=0)
        rows = pl.ds(wait(i), tile)
        for j in range(0, slab, wide):
            lanes = slice(j, j + wide)
            placed = dot(kept, onehot[:, lanes]).astype(bf16)
            held[rows, lanes] = base_stage[rows, lanes] + placed
        copy(i).start()
        return 0

    lax.fori_loop(0, count, step, 0)
    lax.fori_loop(0, count, lambda i, _: (copy(i).wait(), 0)[1], 0)


def norm_kernel(width, gathered, held, gain, normed, stage, turned, sems):
    slab = held.shape[1]

    def copy(i):
        rows = pl.ds(pl.multiple_of(i * LANES, LANES), LANES)
        return pltpu.make_async_copy(stage.at[rows, :], normed.at[rows, :], sems.at[i])

    def step(i, _):
        total = gathered[0, i]
        for n in range(1, gathered.shape[0]):
            total = total + gathered[n, i]
        scale = lax.rsqrt(total / width + norm_eps)
        turned[...] = jnp.broadcast_to(scale, (LANES, LANES)).T
        first = pl.multiple_of(i * LANES, LANES)
        for c in range(0, LANES, CHUNK):
            at = pl.ds(first + c, CHUNK)
            scales = turned[c : c + CHUNK, :]
            for j in range(0, slab, LANES):
                lanes = slice(j, j + LANES)
                value = held[at, lanes].astype(f32) * scales * gain[:, lanes]
                stage[at, lanes] = value.astype(bf16)
        copy(i).start()
        return 0

    lax.fori_loop(0, sems.shape[0], step, 0)
    lax.fori_loop(0, sems.shape[0], lambda i, _: (copy(i).wait(), 0)[1], 0)


def in_hbm(x):
    return pltpu.with_memory_space_constraint(x, pltpu.HBM)


def in_vmem(x):
    return pltpu.with_memory_space_constraint(x, pltpu.VMEM)


def call(kernel, outs, ins, flops, moved, limit, scratch=(), far=(), far_outs=(), alias=None):
    near = pl.BlockSpec(memory_space=pltpu.VMEM)
    away = pl.BlockSpec(memory_space=pl.ANY)
    return pl.pallas_call(
        kernel,
        out_shape=outs,
        in_specs=[away if n in far else near for n in range(len(ins))],
        out_specs=[away if n in far_outs else near for n in range(len(outs))],
        scratch_shapes=list(scratch),
        input_output_aliases=alias or {},
        compiler_params=pltpu.CompilerParams(vmem_limit_bytes=limit),
        cost_estimate=pl.CostEstimate(flops=flops, bytes_accessed=moved, transcendentals=0),
    )(*ins)


def local(
    gate_in, value_in, out_gate, residual, filters, kept_index, kept_owner, skip_bias, norm_gain
):
    tok_rows, slab = gate_in.shape
    slots, length = filters.shape[2:]
    chan_devices = lax.axis_size("chan")
    owner_count = lax.axis_size("seqo") * lax.axis_size("seqi")
    rows = slots * owner_count
    lanes_rows = -(-rows // LANES) * LANES
    blocks = tok_rows // LANES
    outer = length // LANES
    tile = TILE if tok_rows % TILE == 0 else LANES
    dense = tok_rows * slab * 2
    sds = jax.ShapeDtypeStruct
    tables = [in_hbm(jnp.asarray(x)) for x in dft_tables(length)]
    outer_fwd, turn, inner, outer_back = tables
    skip_row = skip_bias[None, :]
    gain_row = norm_gain[None, :]
    gate_in, value_in, out_gate, residual = map(in_hbm, (gate_in, value_in, out_gate, residual))
    picks = sds((blocks, rows, LANES), bf16)
    row_sums = sds((blocks, 1, LANES), f32)
    buffer = (owner_count, blocks, slots * LANES)
    whole = (tok_rows, slab)
    head_rows = tok_rows // 4 // tile * tile

    payload, picked, channels, gated_head = call(
        functools.partial(pick_kernel, owner_count, slots),
        [
            pltpu.HBM(buffer, bf16),
            picks,
            sds((8, lanes_rows), jnp.int32),
            pltpu.VMEM((head_rows, slab), bf16),
        ],
        [in_hbm(kept_index), in_hbm(kept_owner), gate_in, value_in],
        2 * tok_rows * slab * rows,
        2 * dense,
        24 * MIB,
        scratch=[
            pltpu.VMEM((blocks, rows, LANES), f32),
            pltpu.VMEM(whole, bf16),
            pltpu.VMEM(whole, bf16),
            pltpu.VMEM((rows, slab), bf16),
            pltpu.VMEM(buffer, bf16),
            pltpu.VMEM((2,) + kept_index.shape, jnp.int32),
            pltpu.SemaphoreType.DMA((2 + slots,)),
            pltpu.SemaphoreType.DMA((2, tok_rows // tile)),
        ],
        far=(0, 1, 2, 3),
        far_outs=(0,),
    )

    incoming = lax.all_to_all(payload, ("seqo", "seqi"), split_axis=0, concat_axis=0, tiled=True)

    dense_ins = [gate_in, value_in, out_gate, residual]

    def base_parts(count, head):
        part = count * LANES
        outs = [
            pltpu.HBM(whole, bf16),
            sds((count, 1, LANES), f32),
            sds((count, rows, LANES), bf16),
            sds((count, rows, LANES), bf16),
        ]
        scratch = [
            pltpu.VMEM((part - head, slab), bf16),
            pltpu.VMEM((part - head, slab), bf16),
            pltpu.VMEM((part, slab), bf16),
            pltpu.VMEM((part, slab), bf16),
            pltpu.VMEM((part, slab), bf16),
            pltpu.VMEM((LANES, LANES), f32),
            pltpu.SemaphoreType.DMA((count,)),
            pltpu.SemaphoreType.DMA((2, (part - head) // LANES)),
            pltpu.SemaphoreType.DMA((2, count)),
        ]
        return outs, scratch, 4 * part * slab * rows, 10 * part * slab

    early = max(head_rows // LANES + 1, blocks * EARLY // 16)
    outs, scratch, flops, moved = base_parts(early, head_rows)
    onehot, others, skip_wide, base, *first_picks = call(
        first_kernel,
        [sds((rows, slab), bf16), sds((8, slab), f32), sds((rows, LANES), f32)] + outs,
        [channels, in_vmem(gated_head), skip_row] + dense_ins,
        flops,
        moved,
        36 * MIB,
        scratch=scratch,
        far=(3, 4, 5, 6),
        far_outs=(3,),
    )
    (spectra,) = call(
        filter_kernel,
        [pltpu.VMEM((slots, outer, 2 * LANES), f32)],
        [filters[0, 0]] + [jnp.asarray(x) for x in dft_tables(length)[:3]],
        2 * slots * length * 2 * (2 * outer + 6 * LANES),
        4 * MIB,
        16 * MIB,
    )
    spectra, base = lax.optimization_barrier((spectra, base))

    conv_ins = [incoming, in_vmem(spectra), outer_fwd, turn, inner, outer_back]
    (convolved,) = call(
        convolve_kernel,
        [pltpu.HBM(buffer, bf16)],
        conv_ins,
        2 * slots * length * 2 * (5 * outer + 12 * LANES),
        8 * MIB,
        20 * MIB,
        scratch=[pltpu.VMEM(x.shape, x.dtype) for x in conv_ins[2:]]
        + [pltpu.VMEM(buffer, bf16), pltpu.SemaphoreType.DMA((len(conv_ins) + slots,))],
        far=tuple(range(2, len(conv_ins))),
        far_outs=(0,),
    )
    convolved, onehot = lax.optimization_barrier((convolved, onehot))

    returned = lax.all_to_all(convolved, ("seqo", "seqi"), split_axis=0, concat_axis=0, tiled=True)

    outs, scratch, flops, moved = base_parts(blocks - early, 0)
    base, *more_picks = call(
        functools.partial(second_kernel, early * LANES),
        outs,
        [onehot, others, skip_row] + dense_ins + [base],
        flops,
        moved,
        36 * MIB,
        scratch=scratch,
        far=(3, 4, 5, 6, 7),
        far_outs=(0,),
        alias={7: 0},
    )

    hidden_kept, totals = call(
        kept_kernel,
        [picks, row_sums],
        [returned, picked, skip_wide, *first_picks, *more_picks],
        8 * rows * tok_rows,
        10 * rows * tok_rows,
        16 * MIB,
    )

    gathered = lax.all_gather(totals, "chan")

    hidden, held = call(
        hidden_kernel,
        [pltpu.HBM(whole, bf16), pltpu.VMEM(whole, bf16)],
        [in_hbm(base), hidden_kept, onehot],
        2 * tok_rows * slab * rows,
        2 * dense,
        16 * MIB,
        scratch=[
            pltpu.VMEM(whole, bf16),
            pltpu.SemaphoreType.DMA((1, tok_rows // tile)),
            pltpu.SemaphoreType.DMA((tok_rows // tile,)),
        ],
        far=(0,),
        far_outs=(0,),
    )
    (normed,) = call(
        functools.partial(norm_kernel, float(slab * chan_devices)),
        [pltpu.HBM(whole, bf16)],
        [gathered, in_vmem(held), gain_row],
        4 * tok_rows * slab,
        2 * dense,
        16 * MIB,
        scratch=[
            pltpu.VMEM(whole, bf16),
            pltpu.VMEM((LANES, LANES), f32),
            pltpu.SemaphoreType.DMA((blocks,)),
        ],
        far_outs=(0,),
    )
    return (hidden, normed)


def solution(mesh):
    positions = P(("seqo", "seqi"), "chan")
    in_specs = (
        positions,
        positions,
        positions,
        positions,
        P("chan", ("seqo", "seqi"), None, None),
        P("chan", None),
        P("chan", None),
        P("chan"),
        P("chan"),
    )
    return jax.shard_map(
        local, mesh=mesh, in_specs=in_specs, out_specs=(positions, positions), check_vma=False
    )
```

```python
import functools

import jax
import jax.numpy as jnp
import numpy as np
from jax import lax
from jax.experimental import pallas as pl
from jax.experimental.pallas import tpu as pltpu
from jax.sharding import PartitionSpec as P

LANES = 128
TILE = 256
CHUNK = 16
GROUP = 3
AHEAD = 3
EARLY = 8
MIB = 1 << 20
norm_eps = 1e-06
f32 = jnp.float32
bf16 = jnp.bfloat16


def split_np(table):
    high = table.astype(jnp.bfloat16)
    low = (table - high.astype(np.float64)).astype(jnp.bfloat16)
    return high, low


def dft_tables(length):
    inner = LANES
    outer = length // inner
    a = np.arange(outer)
    b = np.arange(inner)
    quarter = np.arange(outer) + 0.25
    outer_angle = 2 * np.pi / outer * np.mod(quarter[:, None] * a[None, :], outer)
    turn_angle = 2 * np.pi / length * (quarter[:, None] * b[None, :])
    inner_angle = 2 * np.pi / inner * np.mod(b[:, None] * b[None, :], inner)
    outer_fwd = np.concatenate([np.cos(outer_angle), -np.sin(outer_angle)], axis=0)
    c, s = np.cos(inner_angle), np.sin(inner_angle)
    inner_fwd = np.concatenate(
        [np.concatenate([c, -s], axis=1), np.concatenate([s, c], axis=1)], axis=0
    )
    inner_back = np.concatenate(
        [np.concatenate([c, s], axis=1), np.concatenate([-s, c], axis=1)], axis=0
    )
    outer_back = np.concatenate([np.cos(outer_angle).T, -np.sin(outer_angle).T], axis=1) / length
    turn = np.concatenate([np.cos(turn_angle), np.sin(turn_angle)], axis=1).astype(np.float32)
    outer_fwd = np.concatenate(split_np(outer_fwd), axis=0)
    inner = np.concatenate(split_np(inner_fwd) + split_np(inner_back), axis=0)
    outer_back = np.concatenate(split_np(outer_back), axis=1)
    return outer_fwd, turn, inner, outer_back


def split(value):
    high = value.astype(bf16)
    low = (value - high.astype(f32)).astype(bf16)
    return high, low


def dot(x, y):
    return jnp.dot(x, y, preferred_element_type=f32)


def dot_rows(x, y):
    return lax.dot_general(x, y, (((0,), (0,)), ((), ())), preferred_element_type=f32)


def times_table(value, table):
    high, low = split(value)
    depth = value.shape[1]
    stacked = jnp.concatenate([table, table[:depth]], axis=0)
    return dot(jnp.concatenate([high, high, low], axis=1), stacked)


def table_times(table, value):
    high, low = split(value)
    depth = value.shape[0]
    stacked = jnp.concatenate([table, table[:, :depth]], axis=1)
    return dot(stacked, jnp.concatenate([high, high, low], axis=0))


def to_spectrum(blocks, slots, outer_fwd, turn, inner_fwd):
    outer = blocks.shape[0]
    first = dot(outer_fwd(0), blocks)
    first = first + dot(outer_fwd(1), blocks)
    turn, inner_fwd = turn(), inner_fwd()
    cos, sin = turn[:, :LANES], turn[:, LANES:]
    turned = []
    for s in range(slots):
        re = first[:outer, s * LANES : (s + 1) * LANES]
        im = first[outer:, s * LANES : (s + 1) * LANES]
        turned.append(jnp.concatenate([re * cos + im * sin, im * cos - re * sin], axis=1))
    return grouped(turned, inner_fwd)


def grouped(values, table):
    result = []
    for s in range(0, len(values), GROUP):
        part = values[s : s + GROUP]
        size = part[0].shape[0]
        product = times_table(jnp.concatenate(part, axis=0), table)
        result += [product[n * size : (n + 1) * size] for n in range(len(part))]
    return result


def filter_spectra(filters, outer_fwd, turn, inner):
    slots, length = filters.shape
    outer = length // LANES
    wide = filters[...].astype(f32)
    blocks = [wide[s].reshape(outer, LANES) for s in range(slots)]
    blocks = jnp.concatenate(blocks, axis=1).astype(bf16)
    return to_spectrum(
        blocks,
        slots,
        lambda n: outer_fwd[2 * outer * n : 2 * outer * (n + 1), :],
        lambda: turn[...],
        lambda: inner[: 4 * LANES, :],
    )


def convolve_kernel(
    signals, spectra, outer_fwd_far, turn_far, inner_far, outer_back_far, out, *scratch
):
    sources = (outer_fwd_far, turn_far, inner_far, outer_back_far)
    outer_fwd, turn_ref, inner, outer_back, result, sems = scratch
    slots, outer = spectra.shape[:2]
    halves = [pl.ds(2 * outer * n, 2 * outer) for n in range(2)]
    copies = [
        pltpu.make_async_copy(outer_fwd_far.at[half, :], outer_fwd.at[half, :], sems.at[n])
        for n, half in enumerate(halves)
    ] + [
        pltpu.make_async_copy(source, scratch[n], sems.at[n + 1])
        for n, source in enumerate(sources)
        if n > 0
    ]
    for copy in copies:
        copy.start()

    def outer_now(n):
        copies[n].wait()
        return outer_fwd[halves[n], :]

    def turn_now():
        copies[2].wait()
        return turn_ref[...]

    def inner_now():
        copies[3].wait()
        return inner[: 4 * LANES, :]

    blocks = signals[...].reshape(outer, slots * LANES)
    parts = to_spectrum(blocks, slots, outer_now, turn_now, inner_now)
    turn = turn_ref[...]
    cos, sin = turn[:, :LANES], turn[:, LANES:]
    joint = []
    for s in range(slots):
        sig_re, sig_im = parts[s][:, :LANES], parts[s][:, LANES:]
        ker_re, ker_im = spectra[s, :, :LANES], spectra[s, :, LANES:]
        joint.append(
            jnp.concatenate(
                [sig_re * ker_re - sig_im * ker_im, sig_re * ker_im + sig_im * ker_re], axis=1
            )
        )
    turned = []
    for back in grouped(joint, inner[4 * LANES :, :]):
        re, im = back[:, :LANES], back[:, LANES:]
        turned.append(jnp.concatenate([re * cos - im * sin, im * cos + re * sin], axis=0))
    copies[4].wait()
    sends = []
    for s in range(0, slots, 2):
        pair = turned[s : s + 2]
        causal = table_times(outer_back[...], jnp.concatenate(pair, axis=1)).astype(bf16)
        lanes = pl.ds(s * LANES, len(pair) * LANES)
        result[:, :, lanes] = causal.reshape(out.shape[:2] + (len(pair) * LANES,))
        sends.append(
            pltpu.make_async_copy(
                result.at[:, :, lanes], out.at[:, :, lanes], sems.at[len(copies) + len(sends)]
            )
        )
        sends[-1].start()
    for send in sends:
        send.wait()


def iota(shape, axis):
    return lax.broadcasted_iota(jnp.int32, shape, axis)


def to_column(row):
    size = row.shape[1]
    same = iota((size, size), 0) == iota((size, size), 1)
    return jnp.sum(jnp.where(same, row, 0), axis=1, keepdims=True)


def channel_of_row(index_row, owners_row, owner_count, rows):
    slots = owners_row.shape[1]
    owners_col = to_column(owners_row)
    index_col = to_column(index_row)
    earlier = (owners_col == owners_row) & (iota((slots, slots), 1) < iota((slots, slots), 0))
    rank_col = jnp.sum(earlier.astype(jnp.int32), axis=1, keepdims=True)
    target_col = jnp.where(owners_col >= 0, rank_col * owner_count + owners_col, -1)
    hit = target_col == iota((slots, rows), 1)
    return jnp.sum(jnp.where(hit, index_col + 1, 0), axis=0, keepdims=True) - 1


def pick_rows(onehot, tile):
    picked = lax.dot_general(
        onehot, tile, (((1,), (1,)), ((), ())), preferred_element_type=f32
    )
    return [picked[:, i : i + LANES] for i in range(0, tile.shape[0], LANES)]


def fetch(sources, stages, sems, tile, first=0, ahead=3, begin=True):
    count = stages[0].shape[0] // tile

    def copies(i):
        at = pl.multiple_of(i * tile, tile)
        return [
            pltpu.make_async_copy(
                source.at[pl.ds(first + at, tile), :], stage.at[pl.ds(at, tile), :], sems.at[n, i]
            )
            for n, (source, stage) in enumerate(zip(sources, stages))
        ]

    def start(i):
        for copy in copies(i):
            copy.start()

    ahead = min(ahead, count)
    if begin:
        for i in range(ahead):
            start(i)

    def wait(i):
        for copy in copies(i):
            copy.wait()

        @pl.when(i + ahead < count)
        def _():
            start(i + ahead)

        return pl.multiple_of(i * tile, tile)

    return start, wait, ahead


def build_onehot(onehot, row):
    hit = iota(onehot.shape, 1) == to_column(row)[: onehot.shape[0]]
    onehot[...] = hit.astype(f32).astype(bf16)
    return hit


def pick_kernel(owner_count, slots, index, owners, gate, value, *refs):
    payload, picked, channels, gated_head = refs[:4]
    acc, gate_stage, value_stage, onehot, payload_stage, lists, list_sems, sems = refs[4:]
    tile = gate_stage.shape[0] // sems.shape[1]
    list_copies = [
        pltpu.make_async_copy(source, lists.at[n], list_sems.at[n])
        for n, source in enumerate((index, owners))
    ]
    for copy in list_copies:
        copy.start()
    count = sems.shape[1]
    _, wait, _ = fetch((gate, value), (gate_stage, value_stage), sems, tile, 0, 5)
    for copy in list_copies:
        copy.wait()
    row = channel_of_row(lists[0], lists[1], owner_count, channels.shape[1])
    channels[...] = jnp.broadcast_to(row, channels.shape)
    build_onehot(onehot, row)

    def step(i, in_head):
        at = pl.ds(wait(i), tile)
        gated = gate_stage[at, :] * value_stage[at, :]
        if in_head:
            gated_head[at, :] = gated
        for n, block in enumerate(pick_rows(onehot[...], gated)):
            acc[i * (tile // LANES) + n] = block
            picked[i * (tile // LANES) + n] = block.astype(bf16)
        return 0

    head_tiles = gated_head.shape[0] // tile
    lax.fori_loop(0, head_tiles, lambda i, _: step(i, True), 0)
    lax.fori_loop(head_tiles, count, lambda i, _: step(i, False), 0)
    sends = []
    for s in range(slots):
        part = jnp.swapaxes(acc[:, s * owner_count : (s + 1) * owner_count, :], 0, 1)
        lanes = pl.ds(s * LANES, LANES)
        payload_stage[:, :, lanes] = part.astype(bf16)
        sends.append(
            pltpu.make_async_copy(
                payload_stage.at[:, :, lanes], payload.at[:, :, lanes], list_sems.at[2 + s]
            )
        )
        sends[-1].start()
    for send in sends:
        send.wait()


def filter_kernel(filters, outer_fwd, turn, inner, spectra):
    for s, part in enumerate(filter_spectra(filters, outer_fwd, turn, inner)):
        spectra[s] = part


def first_kernel(channels, gated_head, skip, *refs):
    onehot, others, skip_wide, *outs = refs[4:11]

    def beside():
        hit = build_onehot(onehot, channels[0:1, :])
        kept = jnp.max(hit.astype(f32), axis=0, keepdims=True)
        others[...] = jnp.broadcast_to(1.0 - kept, others.shape)
        skip_col = jnp.sum(jnp.where(hit, skip[...], 0.0), axis=1, keepdims=True)
        skip_wide[...] = jnp.broadcast_to(skip_col, skip_wide.shape)

    base_pass(0, gated_head, onehot, others, skip, refs[:4], outs, refs[11:], beside)


def second_kernel(first, onehot, others, skip, *refs):
    base_pass(first, None, onehot, others, skip, refs[:4], refs[5:9], refs[9:], None)


def base_pass(first, head, onehot, others, skip, dense, outs, scratch, beside):
    base, sums, picked_gate, picked_res = outs
    gate_stage, value_stage, out_stage, res_stage, base_stage = scratch[:5]
    partial, base_sems, gate_sems, sems = scratch[5:]
    slab = out_stage.shape[1]
    tile = partial.shape[0]
    head_rows = 0 if head is None else head.shape[0]
    head_tiles = head_rows // tile
    count = sems.shape[1]
    late = head_tiles > AHEAD
    _, wait, _ = fetch(dense[2:], (out_stage, res_stage), sems, tile, first, AHEAD)
    start_gate, wait_gate, early = fetch(
        dense[:2], (gate_stage, value_stage), gate_sems, tile, first + head_rows, AHEAD, not late
    )
    if beside is not None:
        beside()

    def copy(i):
        at = pl.multiple_of(i * tile, tile)
        return pltpu.make_async_copy(
            base_stage.at[pl.ds(at, tile), :], base.at[pl.ds(first + at, tile), :], base_sems.at[i]
        )

    def step(i, in_head):
        start = wait(i)
        if in_head and late:

            @pl.when((i > 0) & (i <= early))
            def _():
                start_gate(i - 1)

        gate_start = start if in_head else wait_gate(i - head_tiles)
        chunks = range(0, tile, CHUNK)
        totals = [jnp.zeros((CHUNK, LANES), f32) for _ in chunks]
        for j in range(0, slab, LANES):
            lanes = slice(j, j + LANES)
            skips = skip[:, lanes]
            mask = others[0:1, lanes].astype(bf16)
            for n, c in enumerate(chunks):
                at = pl.ds(start + c, CHUNK)
                gate_at = pl.ds(gate_start + c, CHUNK)
                if in_head:
                    gated = head[gate_at, lanes]
                else:
                    gated = gate_stage[gate_at, lanes] * value_stage[gate_at, lanes]
                mixed = out_stage[at, lanes].astype(f32) * (skips * gated.astype(f32))
                hidden = (res_stage[at, lanes].astype(f32) + mixed).astype(bf16) * mask
                base_stage[at, lanes] = hidden
                hidden = hidden.astype(f32)
                totals[n] = totals[n] + hidden * hidden
        copy(i).start()
        for n, c in enumerate(chunks):
            partial[c : c + CHUNK, :] = totals[n]
        total = jnp.sum(partial[...].T, axis=0, keepdims=True)
        at = pl.ds(start, tile)
        both = jnp.concatenate([out_stage[at, :], res_stage[at, :]], axis=0)
        both = pick_rows(onehot[...], both)
        picks_gate, picks_res = both[: tile // LANES], both[tile // LANES :]
        for n in range(tile // LANES):
            block = i * (tile // LANES) + n
            sums[block] = total[:, n * LANES : (n + 1) * LANES]
            picked_gate[block] = picks_gate[n].astype(bf16)
            picked_res[block] = picks_res[n].astype(bf16)
        return 0

    if head_tiles:
        lax.fori_loop(0, head_tiles, lambda i, _: step(i, True), 0)
    lax.fori_loop(head_tiles, count, lambda i, _: step(i, False), 0)
    lax.fori_loop(0, count, lambda i, _: (copy(i).wait(), 0)[1], 0)


def kept_kernel(conv, picked, skip_wide, *refs):
    hidden, totals = refs[-2:]
    owner_count, blocks = conv.shape[:2]
    first = 0
    for n in range(0, len(refs) - 2, 3):
        sums, picked_gate, picked_res = refs[n : n + 3]
        size = sums.shape[0]
        at_h = slice(first, first + size)
        total = jnp.zeros((size, LANES), f32)
        for s in range(conv.shape[2] // LANES):
            at = slice(s * owner_count, (s + 1) * owner_count)
            lanes = slice(s * LANES, (s + 1) * LANES)
            wide = jnp.swapaxes(conv[:, at_h, lanes].astype(f32), 0, 1)
            wide = wide + skip_wide[at, :] * picked[at_h, at, :].astype(f32)
            value = picked_res[:, at, :].astype(f32) + picked_gate[:, at, :].astype(f32) * wide
            value = value.astype(bf16)
            hidden[at_h, at, :] = value
            value = value.astype(f32)
            total = total + jnp.sum(value * value, axis=1)
        for i in range(size):
            totals[first + i] = total[i : i + 1, :] + sums[i]
        first = first + size


def hidden_kernel(base, hidden_kept, onehot, hidden, held, base_stage, base_sems, sems):
    slab = held.shape[1]
    wide = min(slab, 2 * LANES)
    count = sems.shape[0]
    tile = held.shape[0] // count
    _, wait, _ = fetch((base,), (base_stage,), base_sems, tile, 0, 4)

    def copy(i):
        rows = pl.ds(pl.multiple_of(i * tile, tile), tile)
        return pltpu.make_async_copy(held.at[rows, :], hidden.at[rows, :], sems.at[i])

    def step(i, _):
        blocks = range(tile // LANES)
        kept = [hidden_kept[i * (tile // LANES) + n].astype(f32).T.astype(bf16) for n in blocks]
        kept = jnp.concatenate(kept, axis=0)
        rows = pl.ds(wait(i), tile)
        for j in range(0, slab, wide):
            lanes = slice(j, j + wide)
            placed = dot(kept, onehot[:, lanes]).astype(bf16)
            held[rows, lanes] = base_stage[rows, lanes] + placed
        copy(i).start()
        return 0

    lax.fori_loop(0, count, step, 0)
    lax.fori_loop(0, count, lambda i, _: (copy(i).wait(), 0)[1], 0)


def norm_kernel(width, count, *refs):
    parts = refs[:count]
    held, gain, normed, stage, turned, sems = refs[count:]
    slab = held.shape[1]

    def copy(i):
        rows = pl.ds(pl.multiple_of(i * LANES, LANES), LANES)
        return pltpu.make_async_copy(stage.at[rows, :], normed.at[rows, :], sems.at[i])

    def step(i, _):
        total = parts[0][i]
        for part in parts[1:]:
            total = total + part[i]
        scale = lax.rsqrt(total / width + norm_eps)
        turned[...] = jnp.broadcast_to(scale, (LANES, LANES)).T
        first = pl.multiple_of(i * LANES, LANES)
        for c in range(0, LANES, CHUNK):
            at = pl.ds(first + c, CHUNK)
            scales = turned[c : c + CHUNK, :]
            for j in range(0, slab, LANES):
                lanes = slice(j, j + LANES)
                value = held[at, lanes].astype(f32) * scales * gain[:, lanes]
                stage[at, lanes] = value.astype(bf16)
        copy(i).start()
        return 0

    lax.fori_loop(0, sems.shape[0], step, 0)
    lax.fori_loop(0, sems.shape[0], lambda i, _: (copy(i).wait(), 0)[1], 0)


def in_hbm(x):
    return pltpu.with_memory_space_constraint(x, pltpu.HBM)


def in_vmem(x):
    return pltpu.with_memory_space_constraint(x, pltpu.VMEM)


def call(kernel, outs, ins, flops, moved, limit, scratch=(), far=(), far_outs=(), alias=None):
    near = pl.BlockSpec(memory_space=pltpu.VMEM)
    away = pl.BlockSpec(memory_space=pl.ANY)
    return pl.pallas_call(
        kernel,
        out_shape=outs,
        in_specs=[away if n in far else near for n in range(len(ins))],
        out_specs=[away if n in far_outs else near for n in range(len(outs))],
        scratch_shapes=list(scratch),
        input_output_aliases=alias or {},
        compiler_params=pltpu.CompilerParams(vmem_limit_bytes=limit),
        cost_estimate=pl.CostEstimate(flops=flops, bytes_accessed=moved, transcendentals=0),
    )(*ins)


def local(
    gate_in, value_in, out_gate, residual, filters, kept_index, kept_owner, skip_bias, norm_gain
):
    tok_rows, slab = gate_in.shape
    slots, length = filters.shape[2:]
    chan_devices = lax.axis_size("chan")
    owner_count = lax.axis_size("seqo") * lax.axis_size("seqi")
    rows = slots * owner_count
    lanes_rows = -(-rows // LANES) * LANES
    blocks = tok_rows // LANES
    outer = length // LANES
    tile = TILE if tok_rows % TILE == 0 else LANES
    dense = tok_rows * slab * 2
    sds = jax.ShapeDtypeStruct
    tables = [in_hbm(jnp.asarray(x)) for x in dft_tables(length)]
    outer_fwd, turn, inner, outer_back = tables
    skip_row = skip_bias[None, :]
    gain_row = norm_gain[None, :]
    gate_in, value_in, out_gate, residual = map(in_hbm, (gate_in, value_in, out_gate, residual))
    picks = sds((blocks, rows, LANES), bf16)
    row_sums = sds((blocks, 1, LANES), f32)
    buffer = (owner_count, blocks, slots * LANES)
    whole = (tok_rows, slab)
    head_rows = tok_rows // 4 // tile * tile

    payload, picked, channels, gated_head = call(
        functools.partial(pick_kernel, owner_count, slots),
        [
            pltpu.HBM(buffer, bf16),
            picks,
            sds((8, lanes_rows), jnp.int32),
            pltpu.VMEM((head_rows, slab), bf16),
        ],
        [in_hbm(kept_index), in_hbm(kept_owner), gate_in, value_in],
        2 * tok_rows * slab * rows,
        2 * dense,
        24 * MIB,
        scratch=[
            pltpu.VMEM((blocks, rows, LANES), f32),
            pltpu.VMEM(whole, bf16),
            pltpu.VMEM(whole, bf16),
            pltpu.VMEM((rows, slab), bf16),
            pltpu.VMEM(buffer, bf16),
            pltpu.VMEM((2,) + kept_index.shape, jnp.int32),
            pltpu.SemaphoreType.DMA((2 + slots,)),
            pltpu.SemaphoreType.DMA((2, tok_rows // tile)),
        ],
        far=(0, 1, 2, 3),
        far_outs=(0,),
    )

    incoming = lax.all_to_all(payload, ("seqo", "seqi"), split_axis=0, concat_axis=0, tiled=True)

    dense_ins = [gate_in, value_in, out_gate, residual]

    def base_parts(count, head):
        part = count * LANES
        outs = [
            pltpu.HBM(whole, bf16),
            sds((count, 1, LANES), f32),
            sds((count, rows, LANES), bf16),
            sds((count, rows, LANES), bf16),
        ]
        scratch = [
            pltpu.VMEM((part - head, slab), bf16),
            pltpu.VMEM((part - head, slab), bf16),
            pltpu.VMEM((part, slab), bf16),
            pltpu.VMEM((part, slab), bf16),
            pltpu.VMEM((part, slab), bf16),
            pltpu.VMEM((LANES, LANES), f32),
            pltpu.SemaphoreType.DMA((count,)),
            pltpu.SemaphoreType.DMA((2, (part - head) // LANES)),
            pltpu.SemaphoreType.DMA((2, count)),
        ]
        return outs, scratch, 4 * part * slab * rows, 10 * part * slab

    early = max(head_rows // LANES + 1, blocks * EARLY // 16)
    outs, scratch, flops, moved = base_parts(early, head_rows)
    onehot, others, skip_wide, base, *first_picks = call(
        first_kernel,
        [sds((rows, slab), bf16), sds((8, slab), f32), sds((rows, LANES), f32)] + outs,
        [channels, in_vmem(gated_head), skip_row] + dense_ins,
        flops,
        moved,
        36 * MIB,
        scratch=scratch,
        far=(3, 4, 5, 6),
        far_outs=(3,),
    )
    (spectra,) = call(
        filter_kernel,
        [pltpu.VMEM((slots, outer, 2 * LANES), f32)],
        [filters[0, 0]] + [jnp.asarray(x) for x in dft_tables(length)[:3]],
        2 * slots * length * 2 * (2 * outer + 6 * LANES),
        4 * MIB,
        16 * MIB,
    )
    spectra, base = lax.optimization_barrier((spectra, base))

    conv_ins = [incoming, in_vmem(spectra), outer_fwd, turn, inner, outer_back]
    (convolved,) = call(
        convolve_kernel,
        [pltpu.HBM(buffer, bf16)],
        conv_ins,
        2 * slots * length * 2 * (5 * outer + 12 * LANES),
        8 * MIB,
        20 * MIB,
        scratch=[pltpu.VMEM(x.shape, x.dtype) for x in conv_ins[2:]]
        + [pltpu.VMEM(buffer, bf16), pltpu.SemaphoreType.DMA((len(conv_ins) + slots,))],
        far=tuple(range(2, len(conv_ins))),
        far_outs=(0,),
    )
    convolved, onehot = lax.optimization_barrier((convolved, onehot))

    returned = lax.all_to_all(convolved, ("seqo", "seqi"), split_axis=0, concat_axis=0, tiled=True)

    outs, scratch, flops, moved = base_parts(blocks - early, 0)
    base, *more_picks = call(
        functools.partial(second_kernel, early * LANES),
        outs,
        [onehot, others, skip_row] + dense_ins + [base],
        flops,
        moved,
        36 * MIB,
        scratch=scratch,
        far=(3, 4, 5, 6, 7),
        far_outs=(0,),
        alias={7: 0},
    )

    hidden_kept, totals = call(
        kept_kernel,
        [picks, row_sums],
        [returned, picked, skip_wide, *first_picks, *more_picks],
        8 * rows * tok_rows,
        10 * rows * tok_rows,
        16 * MIB,
    )

    parts = [totals]
    for shift in range(1, chan_devices):
        ring = [(i, (i + shift) % chan_devices) for i in range(chan_devices)]
        parts.append(lax.ppermute(totals, "chan", ring))

    hidden, held = call(
        hidden_kernel,
        [pltpu.HBM(whole, bf16), pltpu.VMEM(whole, bf16)],
        [in_hbm(base), hidden_kept, onehot],
        2 * tok_rows * slab * rows,
        2 * dense,
        16 * MIB,
        scratch=[
            pltpu.VMEM(whole, bf16),
            pltpu.SemaphoreType.DMA((1, tok_rows // tile)),
            pltpu.SemaphoreType.DMA((tok_rows // tile,)),
        ],
        far=(0,),
        far_outs=(0,),
    )
    (normed,) = call(
        functools.partial(norm_kernel, float(slab * chan_devices), len(parts)),
        [pltpu.HBM(whole, bf16)],
        parts + [in_vmem(held), gain_row],
        4 * tok_rows * slab,
        2 * dense,
        16 * MIB,
        scratch=[
            pltpu.VMEM(whole, bf16),
            pltpu.VMEM((LANES, LANES), f32),
            pltpu.SemaphoreType.DMA((blocks,)),
        ],
        far_outs=(0,),
    )
    return (hidden, normed)


def solution(mesh):
    positions = P(("seqo", "seqi"), "chan")
    in_specs = (
        positions,
        positions,
        positions,
        positions,
        P("chan", ("seqo", "seqi"), None, None),
        P("chan", None),
        P("chan", None),
        P("chan"),
        P("chan"),
    )
    return jax.shard_map(
        local, mesh=mesh, in_specs=in_specs, out_specs=(positions, positions), check_vma=False
    )
```

```python
import functools

import jax
import jax.numpy as jnp
import numpy as np
from jax import lax
from jax.experimental import pallas as pl
from jax.experimental.pallas import tpu as pltpu
from jax.sharding import PartitionSpec as P

LANES = 128
TILE = 256
CHUNK = 16
GROUP = 3
AHEAD = 3
EARLY = 8
MIB = 1 << 20
norm_eps = 1e-06
f32 = jnp.float32
bf16 = jnp.bfloat16


def split_np(table):
    high = table.astype(jnp.bfloat16)
    low = (table - high.astype(np.float64)).astype(jnp.bfloat16)
    return high, low


def dft_tables(length):
    inner = LANES
    outer = length // inner
    a = np.arange(outer)
    b = np.arange(inner)
    quarter = np.arange(outer) + 0.25
    outer_angle = 2 * np.pi / outer * np.mod(quarter[:, None] * a[None, :], outer)
    turn_angle = 2 * np.pi / length * (quarter[:, None] * b[None, :])
    inner_angle = 2 * np.pi / inner * np.mod(b[:, None] * b[None, :], inner)
    outer_fwd = np.concatenate([np.cos(outer_angle), -np.sin(outer_angle)], axis=0)
    c, s = np.cos(inner_angle), np.sin(inner_angle)
    inner_fwd = np.concatenate(
        [np.concatenate([c, -s], axis=1), np.concatenate([s, c], axis=1)], axis=0
    )
    inner_back = np.concatenate(
        [np.concatenate([c, s], axis=1), np.concatenate([-s, c], axis=1)], axis=0
    )
    outer_back = np.concatenate([np.cos(outer_angle).T, -np.sin(outer_angle).T], axis=1) / length
    turn = np.concatenate([np.cos(turn_angle), np.sin(turn_angle)], axis=1).astype(np.float32)
    outer_fwd = np.concatenate(split_np(outer_fwd), axis=0)
    inner = np.concatenate(split_np(inner_fwd) + split_np(inner_back), axis=0)
    outer_back = np.concatenate(split_np(outer_back), axis=1)
    return outer_fwd, turn, inner, outer_back


def split(value):
    high = value.astype(bf16)
    low = (value - high.astype(f32)).astype(bf16)
    return high, low


def dot(x, y):
    return jnp.dot(x, y, preferred_element_type=f32)


def dot_rows(x, y):
    return lax.dot_general(x, y, (((0,), (0,)), ((), ())), preferred_element_type=f32)


def times_table(value, table):
    high, low = split(value)
    depth = value.shape[1]
    stacked = jnp.concatenate([table, table[:depth]], axis=0)
    return dot(jnp.concatenate([high, high, low], axis=1), stacked)


def table_times(table, value):
    high, low = split(value)
    depth = value.shape[0]
    stacked = jnp.concatenate([table, table[:, :depth]], axis=1)
    return dot(stacked, jnp.concatenate([high, high, low], axis=0))


def to_spectrum(blocks, slots, outer_fwd, turn, inner_fwd):
    outer = blocks.shape[0]
    first = dot(outer_fwd(0), blocks)
    first = first + dot(outer_fwd(1), blocks)
    turn, inner_fwd = turn(), inner_fwd()
    cos, sin = turn[:, :LANES], turn[:, LANES:]
    turned = []
    for s in range(slots):
        re = first[:outer, s * LANES : (s + 1) * LANES]
        im = first[outer:, s * LANES : (s + 1) * LANES]
        turned.append(jnp.concatenate([re * cos + im * sin, im * cos - re * sin], axis=1))
    return grouped(turned, inner_fwd)


def grouped(values, table):
    result = []
    for s in range(0, len(values), GROUP):
        part = values[s : s + GROUP]
        size = part[0].shape[0]
        product = times_table(jnp.concatenate(part, axis=0), table)
        result += [product[n * size : (n + 1) * size] for n in range(len(part))]
    return result


def filter_spectra(filters, outer_fwd, turn, inner):
    slots, length = filters.shape
    outer = length // LANES
    wide = filters[...].astype(f32)
    blocks = [wide[s].reshape(outer, LANES) for s in range(slots)]
    blocks = jnp.concatenate(blocks, axis=1).astype(bf16)
    return to_spectrum(
        blocks,
        slots,
        lambda n: outer_fwd[2 * outer * n : 2 * outer * (n + 1), :],
        lambda: turn[...],
        lambda: inner[: 4 * LANES, :],
    )


def convolve_kernel(
    signals, spectra, outer_fwd_far, turn_far, inner_far, outer_back_far, out, *scratch
):
    sources = (outer_fwd_far, turn_far, inner_far, outer_back_far)
    outer_fwd, turn_ref, inner, outer_back, result, sems = scratch
    slots, outer = spectra.shape[:2]
    halves = [pl.ds(2 * outer * n, 2 * outer) for n in range(2)]
    copies = [
        pltpu.make_async_copy(outer_fwd_far.at[half, :], outer_fwd.at[half, :], sems.at[n])
        for n, half in enumerate(halves)
    ] + [
        pltpu.make_async_copy(source, scratch[n], sems.at[n + 1])
        for n, source in enumerate(sources)
        if n > 0
    ]
    for copy in copies:
        copy.start()

    def outer_now(n):
        copies[n].wait()
        return outer_fwd[halves[n], :]

    def turn_now():
        copies[2].wait()
        return turn_ref[...]

    def inner_now():
        copies[3].wait()
        return inner[: 4 * LANES, :]

    blocks = signals[...].reshape(outer, slots * LANES)
    parts = to_spectrum(blocks, slots, outer_now, turn_now, inner_now)
    turn = turn_ref[...]
    cos, sin = turn[:, :LANES], turn[:, LANES:]
    joint = []
    for s in range(slots):
        sig_re, sig_im = parts[s][:, :LANES], parts[s][:, LANES:]
        ker_re, ker_im = spectra[s, :, :LANES], spectra[s, :, LANES:]
        joint.append(
            jnp.concatenate(
                [sig_re * ker_re - sig_im * ker_im, sig_re * ker_im + sig_im * ker_re], axis=1
            )
        )
    turned = []
    for back in grouped(joint, inner[4 * LANES :, :]):
        re, im = back[:, :LANES], back[:, LANES:]
        turned.append(jnp.concatenate([re * cos - im * sin, im * cos + re * sin], axis=0))
    copies[4].wait()
    sends = []
    for s in range(0, slots, 2):
        pair = turned[s : s + 2]
        causal = table_times(outer_back[...], jnp.concatenate(pair, axis=1)).astype(bf16)
        lanes = pl.ds(s * LANES, len(pair) * LANES)
        result[:, :, lanes] = causal.reshape(out.shape[:2] + (len(pair) * LANES,))
        sends.append(
            pltpu.make_async_copy(
                result.at[:, :, lanes], out.at[:, :, lanes], sems.at[len(copies) + len(sends)]
            )
        )
        sends[-1].start()
    for send in sends:
        send.wait()


def iota(shape, axis):
    return lax.broadcasted_iota(jnp.int32, shape, axis)


def to_column(row):
    size = row.shape[1]
    same = iota((size, size), 0) == iota((size, size), 1)
    return jnp.sum(jnp.where(same, row, 0), axis=1, keepdims=True)


def channel_of_row(index_row, owners_row, owner_count, rows):
    slots = owners_row.shape[1]
    owners_col = to_column(owners_row)
    index_col = to_column(index_row)
    earlier = (owners_col == owners_row) & (iota((slots, slots), 1) < iota((slots, slots), 0))
    rank_col = jnp.sum(earlier.astype(jnp.int32), axis=1, keepdims=True)
    target_col = jnp.where(owners_col >= 0, rank_col * owner_count + owners_col, -1)
    hit = target_col == iota((slots, rows), 1)
    return jnp.sum(jnp.where(hit, index_col + 1, 0), axis=0, keepdims=True) - 1


def pick_rows(onehot, tile):
    picked = lax.dot_general(
        onehot, tile, (((1,), (1,)), ((), ())), preferred_element_type=f32
    )
    return [picked[:, i : i + LANES] for i in range(0, tile.shape[0], LANES)]


def fetch(sources, stages, sems, tile, first=0, ahead=3, begin=True):
    count = stages[0].shape[0] // tile

    def copies(i):
        at = pl.multiple_of(i * tile, tile)
        return [
            pltpu.make_async_copy(
                source.at[pl.ds(first + at, tile), :], stage.at[pl.ds(at, tile), :], sems.at[n, i]
            )
            for n, (source, stage) in enumerate(zip(sources, stages))
        ]

    def start(i):
        for copy in copies(i):
            copy.start()

    ahead = min(ahead, count)
    if begin:
        for i in range(ahead):
            start(i)

    def wait(i):
        for copy in copies(i):
            copy.wait()

        @pl.when(i + ahead < count)
        def _():
            start(i + ahead)

        return pl.multiple_of(i * tile, tile)

    return start, wait, ahead


def build_onehot(onehot, row):
    hit = iota(onehot.shape, 1) == to_column(row)[: onehot.shape[0]]
    onehot[...] = hit.astype(f32).astype(bf16)
    return hit


def pick_kernel(owner_count, slots, index, owners, gate, value, *refs):
    payload, picked, channels, gated_head = refs[:4]
    acc, gate_stage, value_stage, onehot, payload_stage, lists, list_sems, sems = refs[4:]
    tile = gate_stage.shape[0] // sems.shape[1]
    list_copies = [
        pltpu.make_async_copy(source, lists.at[n], list_sems.at[n])
        for n, source in enumerate((index, owners))
    ]
    for copy in list_copies:
        copy.start()
    count = sems.shape[1]
    _, wait, _ = fetch((gate, value), (gate_stage, value_stage), sems, tile, 0, 4)
    for copy in list_copies:
        copy.wait()
    row = channel_of_row(lists[0], lists[1], owner_count, channels.shape[1])
    channels[...] = jnp.broadcast_to(row, channels.shape)
    build_onehot(onehot, row)

    def step(i, in_head):
        at = pl.ds(wait(i), tile)
        gated = gate_stage[at, :] * value_stage[at, :]
        if in_head:
            gated_head[at, :] = gated
        for n, block in enumerate(pick_rows(onehot[...], gated)):
            acc[i * (tile // LANES) + n] = block
            picked[i * (tile // LANES) + n] = block.astype(bf16)
        return 0

    head_tiles = gated_head.shape[0] // tile
    lax.fori_loop(0, head_tiles, lambda i, _: step(i, True), 0)
    lax.fori_loop(head_tiles, count, lambda i, _: step(i, False), 0)
    sends = []
    for s in range(slots):
        part = jnp.swapaxes(acc[:, s * owner_count : (s + 1) * owner_count, :], 0, 1)
        lanes = pl.ds(s * LANES, LANES)
        payload_stage[:, :, lanes] = part.astype(bf16)
        sends.append(
            pltpu.make_async_copy(
                payload_stage.at[:, :, lanes], payload.at[:, :, lanes], list_sems.at[2 + s]
            )
        )
        sends[-1].start()
    for send in sends:
        send.wait()


def filter_kernel(filters, outer_fwd, turn, inner, spectra):
    for s, part in enumerate(filter_spectra(filters, outer_fwd, turn, inner)):
        spectra[s] = part


def first_kernel(channels, gated_head, skip, *refs):
    onehot, others, skip_wide, *outs = refs[4:11]

    def beside():
        hit = build_onehot(onehot, channels[0:1, :])
        kept = jnp.max(hit.astype(f32), axis=0, keepdims=True)
        others[...] = jnp.broadcast_to(1.0 - kept, others.shape)
        skip_col = jnp.sum(jnp.where(hit, skip[...], 0.0), axis=1, keepdims=True)
        skip_wide[...] = jnp.broadcast_to(skip_col, skip_wide.shape)

    base_pass(0, gated_head, onehot, others, skip, refs[:4], outs, refs[11:], beside)


def second_kernel(first, onehot, others, skip, *refs):
    base_pass(first, None, onehot, others, skip, refs[:4], refs[5:9], refs[9:], None)


def base_pass(first, head, onehot, others, skip, dense, outs, scratch, beside):
    base, sums, picked_gate, picked_res = outs
    gate_stage, value_stage, out_stage, res_stage, base_stage = scratch[:5]
    partial, base_sems, gate_sems, sems = scratch[5:]
    slab = out_stage.shape[1]
    tile = partial.shape[0]
    head_rows = 0 if head is None else head.shape[0]
    head_tiles = head_rows // tile
    count = sems.shape[1]
    late = head_tiles > AHEAD
    _, wait, _ = fetch(dense[2:], (out_stage, res_stage), sems, tile, first, AHEAD)
    start_gate, wait_gate, early = fetch(
        dense[:2], (gate_stage, value_stage), gate_sems, tile, first + head_rows, AHEAD, not late
    )
    if beside is not None:
        beside()

    def copy(i):
        at = pl.multiple_of(i * tile, tile)
        return pltpu.make_async_copy(
            base_stage.at[pl.ds(at, tile), :], base.at[pl.ds(first + at, tile), :], base_sems.at[i]
        )

    def step(i, in_head):
        start = wait(i)
        if in_head and late:

            @pl.when((i > 0) & (i <= early))
            def _():
                start_gate(i - 1)

        gate_start = start if in_head else wait_gate(i - head_tiles)
        chunks = range(0, tile, CHUNK)
        totals = [jnp.zeros((CHUNK, LANES), f32) for _ in chunks]
        for j in range(0, slab, LANES):
            lanes = slice(j, j + LANES)
            skips = skip[:, lanes]
            mask = others[0:1, lanes].astype(bf16)
            for n, c in enumerate(chunks):
                at = pl.ds(start + c, CHUNK)
                gate_at = pl.ds(gate_start + c, CHUNK)
                if in_head:
                    gated = head[gate_at, lanes]
                else:
                    gated = gate_stage[gate_at, lanes] * value_stage[gate_at, lanes]
                mixed = out_stage[at, lanes].astype(f32) * (skips * gated.astype(f32))
                hidden = (res_stage[at, lanes].astype(f32) + mixed).astype(bf16) * mask
                base_stage[at, lanes] = hidden
                hidden = hidden.astype(f32)
                totals[n] = totals[n] + hidden * hidden
        copy(i).start()
        for n, c in enumerate(chunks):
            partial[c : c + CHUNK, :] = totals[n]
        total = jnp.sum(partial[...].T, axis=0, keepdims=True)
        at = pl.ds(start, tile)
        both = jnp.concatenate([out_stage[at, :], res_stage[at, :]], axis=0)
        both = pick_rows(onehot[...], both)
        picks_gate, picks_res = both[: tile // LANES], both[tile // LANES :]
        for n in range(tile // LANES):
            block = i * (tile // LANES) + n
            sums[block] = total[:, n * LANES : (n + 1) * LANES]
            picked_gate[block] = picks_gate[n].astype(bf16)
            picked_res[block] = picks_res[n].astype(bf16)
        return 0

    if head_tiles:
        lax.fori_loop(0, head_tiles, lambda i, _: step(i, True), 0)
    lax.fori_loop(head_tiles, count, lambda i, _: step(i, False), 0)
    lax.fori_loop(0, count, lambda i, _: (copy(i).wait(), 0)[1], 0)


def kept_kernel(conv, picked, skip_wide, *refs):
    hidden, totals = refs[-2:]
    owner_count, blocks = conv.shape[:2]
    first = 0
    for n in range(0, len(refs) - 2, 3):
        sums, picked_gate, picked_res = refs[n : n + 3]
        size = sums.shape[0]
        at_h = slice(first, first + size)
        total = jnp.zeros((size, LANES), f32)
        for s in range(conv.shape[2] // LANES):
            at = slice(s * owner_count, (s + 1) * owner_count)
            lanes = slice(s * LANES, (s + 1) * LANES)
            wide = jnp.swapaxes(conv[:, at_h, lanes].astype(f32), 0, 1)
            wide = wide + skip_wide[at, :] * picked[at_h, at, :].astype(f32)
            value = picked_res[:, at, :].astype(f32) + picked_gate[:, at, :].astype(f32) * wide
            value = value.astype(bf16)
            hidden[at_h, at, :] = value
            value = value.astype(f32)
            total = total + jnp.sum(value * value, axis=1)
        for i in range(size):
            totals[first + i] = total[i : i + 1, :] + sums[i]
        first = first + size


def hidden_kernel(base, hidden_kept, onehot, hidden, held, base_stage, base_sems, sems):
    slab = held.shape[1]
    wide = min(slab, 2 * LANES)
    count = sems.shape[0]
    tile = held.shape[0] // count
    _, wait, _ = fetch((base,), (base_stage,), base_sems, tile, 0, 4)

    def copy(i):
        rows = pl.ds(pl.multiple_of(i * tile, tile), tile)
        return pltpu.make_async_copy(held.at[rows, :], hidden.at[rows, :], sems.at[i])

    def step(i, _):
        blocks = range(tile // LANES)
        kept = [hidden_kept[i * (tile // LANES) + n].astype(f32).T.astype(bf16) for n in blocks]
        kept = jnp.concatenate(kept, axis=0)
        rows = pl.ds(wait(i), tile)
        for j in range(0, slab, wide):
            lanes = slice(j, j + wide)
            placed = dot(kept, onehot[:, lanes]).astype(bf16)
            held[rows, lanes] = base_stage[rows, lanes] + placed
        copy(i).start()
        return 0

    lax.fori_loop(0, count, step, 0)
    lax.fori_loop(0, count, lambda i, _: (copy(i).wait(), 0)[1], 0)


def norm_kernel(width, count, *refs):
    parts = refs[:count]
    held, gain, normed, stage, turned, sems = refs[count:]
    slab = held.shape[1]

    def copy(i):
        rows = pl.ds(pl.multiple_of(i * LANES, LANES), LANES)
        return pltpu.make_async_copy(stage.at[rows, :], normed.at[rows, :], sems.at[i])

    def step(i, _):
        total = parts[0][i]
        for part in parts[1:]:
            total = total + part[i]
        scale = lax.rsqrt(total / width + norm_eps)
        turned[...] = jnp.broadcast_to(scale, (LANES, LANES)).T
        first = pl.multiple_of(i * LANES, LANES)
        for c in range(0, LANES, CHUNK):
            at = pl.ds(first + c, CHUNK)
            scales = turned[c : c + CHUNK, :]
            for j in range(0, slab, LANES):
                lanes = slice(j, j + LANES)
                value = held[at, lanes].astype(f32) * scales * gain[:, lanes]
                stage[at, lanes] = value.astype(bf16)
        copy(i).start()
        return 0

    lax.fori_loop(0, sems.shape[0], step, 0)
    lax.fori_loop(0, sems.shape[0], lambda i, _: (copy(i).wait(), 0)[1], 0)


def in_hbm(x):
    return pltpu.with_memory_space_constraint(x, pltpu.HBM)


def in_vmem(x):
    return pltpu.with_memory_space_constraint(x, pltpu.VMEM)


def call(kernel, outs, ins, flops, moved, limit, scratch=(), far=(), far_outs=(), alias=None):
    near = pl.BlockSpec(memory_space=pltpu.VMEM)
    away = pl.BlockSpec(memory_space=pl.ANY)
    return pl.pallas_call(
        kernel,
        out_shape=outs,
        in_specs=[away if n in far else near for n in range(len(ins))],
        out_specs=[away if n in far_outs else near for n in range(len(outs))],
        scratch_shapes=list(scratch),
        input_output_aliases=alias or {},
        compiler_params=pltpu.CompilerParams(vmem_limit_bytes=limit),
        cost_estimate=pl.CostEstimate(flops=flops, bytes_accessed=moved, transcendentals=0),
    )(*ins)


def local(
    gate_in, value_in, out_gate, residual, filters, kept_index, kept_owner, skip_bias, norm_gain
):
    tok_rows, slab = gate_in.shape
    slots, length = filters.shape[2:]
    chan_devices = lax.axis_size("chan")
    owner_count = lax.axis_size("seqo") * lax.axis_size("seqi")
    rows = slots * owner_count
    lanes_rows = -(-rows // LANES) * LANES
    blocks = tok_rows // LANES
    outer = length // LANES
    tile = TILE if tok_rows % TILE == 0 else LANES
    dense = tok_rows * slab * 2
    sds = jax.ShapeDtypeStruct
    tables = [in_hbm(jnp.asarray(x)) for x in dft_tables(length)]
    outer_fwd, turn, inner, outer_back = tables
    skip_row = skip_bias[None, :]
    gain_row = norm_gain[None, :]
    gate_in, value_in, out_gate, residual = map(in_hbm, (gate_in, value_in, out_gate, residual))
    picks = sds((blocks, rows, LANES), bf16)
    row_sums = sds((blocks, 1, LANES), f32)
    buffer = (owner_count, blocks, slots * LANES)
    whole = (tok_rows, slab)
    head_rows = tok_rows // 4 // tile * tile

    payload, picked, channels, gated_head = call(
        functools.partial(pick_kernel, owner_count, slots),
        [
            pltpu.HBM(buffer, bf16),
            picks,
            sds((8, lanes_rows), jnp.int32),
            pltpu.VMEM((head_rows, slab), bf16),
        ],
        [in_hbm(kept_index), in_hbm(kept_owner), gate_in, value_in],
        2 * tok_rows * slab * rows,
        2 * dense,
        24 * MIB,
        scratch=[
            pltpu.VMEM((blocks, rows, LANES), f32),
            pltpu.VMEM(whole, bf16),
            pltpu.VMEM(whole, bf16),
            pltpu.VMEM((rows, slab), bf16),
            pltpu.VMEM(buffer, bf16),
            pltpu.VMEM((2,) + kept_index.shape, jnp.int32),
            pltpu.SemaphoreType.DMA((2 + slots,)),
            pltpu.SemaphoreType.DMA((2, tok_rows // tile)),
        ],
        far=(0, 1, 2, 3),
        far_outs=(0,),
    )

    incoming = lax.all_to_all(payload, ("seqo", "seqi"), split_axis=0, concat_axis=0, tiled=True)

    dense_ins = [gate_in, value_in, out_gate, residual]

    def base_parts(count, head):
        part = count * LANES
        outs = [
            pltpu.HBM(whole, bf16),
            sds((count, 1, LANES), f32),
            sds((count, rows, LANES), bf16),
            sds((count, rows, LANES), bf16),
        ]
        scratch = [
            pltpu.VMEM((part - head, slab), bf16),
            pltpu.VMEM((part - head, slab), bf16),
            pltpu.VMEM((part, slab), bf16),
            pltpu.VMEM((part, slab), bf16),
            pltpu.VMEM((part, slab), bf16),
            pltpu.VMEM((LANES, LANES), f32),
            pltpu.SemaphoreType.DMA((count,)),
            pltpu.SemaphoreType.DMA((2, (part - head) // LANES)),
            pltpu.SemaphoreType.DMA((2, count)),
        ]
        return outs, scratch, 4 * part * slab * rows, 10 * part * slab

    early = max(head_rows // LANES + 1, blocks * EARLY // 16)
    outs, scratch, flops, moved = base_parts(early, head_rows)
    onehot, others, skip_wide, base, *first_picks = call(
        first_kernel,
        [sds((rows, slab), bf16), sds((8, slab), f32), sds((rows, LANES), f32)] + outs,
        [channels, in_vmem(gated_head), skip_row] + dense_ins,
        flops,
        moved,
        36 * MIB,
        scratch=scratch,
        far=(3, 4, 5, 6),
        far_outs=(3,),
    )
    (spectra,) = call(
        filter_kernel,
        [pltpu.VMEM((slots, outer, 2 * LANES), f32)],
        [filters[0, 0]] + [jnp.asarray(x) for x in dft_tables(length)[:3]],
        2 * slots * length * 2 * (2 * outer + 6 * LANES),
        4 * MIB,
        16 * MIB,
    )
    spectra, base = lax.optimization_barrier((spectra, base))

    conv_ins = [incoming, in_vmem(spectra), outer_fwd, turn, inner, outer_back]
    (convolved,) = call(
        convolve_kernel,
        [pltpu.HBM(buffer, bf16)],
        conv_ins,
        2 * slots * length * 2 * (5 * outer + 12 * LANES),
        8 * MIB,
        20 * MIB,
        scratch=[pltpu.VMEM(x.shape, x.dtype) for x in conv_ins[2:]]
        + [pltpu.VMEM(buffer, bf16), pltpu.SemaphoreType.DMA((len(conv_ins) + slots,))],
        far=tuple(range(2, len(conv_ins))),
        far_outs=(0,),
    )
    convolved, onehot = lax.optimization_barrier((convolved, onehot))

    returned = lax.all_to_all(convolved, ("seqo", "seqi"), split_axis=0, concat_axis=0, tiled=True)

    outs, scratch, flops, moved = base_parts(blocks - early, 0)
    base, *more_picks = call(
        functools.partial(second_kernel, early * LANES),
        outs,
        [onehot, others, skip_row] + dense_ins + [base],
        flops,
        moved,
        36 * MIB,
        scratch=scratch,
        far=(3, 4, 5, 6, 7),
        far_outs=(0,),
        alias={7: 0},
    )

    hidden_kept, totals = call(
        kept_kernel,
        [picks, row_sums],
        [returned, picked, skip_wide, *first_picks, *more_picks],
        8 * rows * tok_rows,
        10 * rows * tok_rows,
        16 * MIB,
    )

    parts = [totals]
    for shift in range(1, chan_devices):
        ring = [(i, (i + shift) % chan_devices) for i in range(chan_devices)]
        parts.append(lax.ppermute(totals, "chan", ring))

    hidden, held = call(
        hidden_kernel,
        [pltpu.HBM(whole, bf16), pltpu.VMEM(whole, bf16)],
        [in_hbm(base), hidden_kept, onehot],
        2 * tok_rows * slab * rows,
        2 * dense,
        16 * MIB,
        scratch=[
            pltpu.VMEM(whole, bf16),
            pltpu.SemaphoreType.DMA((1, tok_rows // tile)),
            pltpu.SemaphoreType.DMA((tok_rows // tile,)),
        ],
        far=(0,),
        far_outs=(0,),
    )
    (normed,) = call(
        functools.partial(norm_kernel, float(slab * chan_devices), len(parts)),
        [pltpu.HBM(whole, bf16)],
        parts + [in_vmem(held), gain_row],
        4 * tok_rows * slab,
        2 * dense,
        16 * MIB,
        scratch=[
            pltpu.VMEM(whole, bf16),
            pltpu.VMEM((LANES, LANES), f32),
            pltpu.SemaphoreType.DMA((blocks,)),
        ],
        far_outs=(0,),
    )
    return (hidden, normed)


def solution(mesh):
    positions = P(("seqo", "seqi"), "chan")
    in_specs = (
        positions,
        positions,
        positions,
        positions,
        P("chan", ("seqo", "seqi"), None, None),
        P("chan", None),
        P("chan", None),
        P("chan"),
        P("chan"),
    )
    return jax.shard_map(
        local, mesh=mesh, in_specs=in_specs, out_specs=(positions, positions), check_vma=False
    )
```
